32 devices in a mesh: dp: 8 (over z, x), seq: 4 (over y, core).
Axes of the slice: x: 2, y: 2, z: 4, core: 2. Of those that a mesh axis runs over, the one named last changes fastest.
Arguments:
- tokens: bfloat16 [16, 512, 768], P('dp', 'seq'), may hold values from -6 to 6
- lengths: int32 [16], P('dp'), may hold values from 20 to 512, as said below
- query_key_value: bfloat16 [768, 2304], replicated, may hold values from -0.21875 to 0.21875
- query_bias: bfloat16 [768], replicated, may hold values from -3 to 3
- value_bias: bfloat16 [768], replicated, may hold values from -0.59765625 to 0.59765625
- attn_weight: bfloat16 [768, 768], replicated, may hold values from -1.75 to 1.75
- attn_bias: bfloat16 [768], replicated, may hold values from -2 to 2
- attn_gain: bfloat16 [768], replicated, may hold values from 0.5 to 1.5
- attn_shift: bfloat16 [768], replicated, may hold values from -2 to 2
- inner_weight: bfloat16 [768, 3072], replicated, may hold values from -0.21875 to 0.21875
- inner_bias: bfloat16 [3072], replicated, may hold values from -3 to 3
- outer_weight: bfloat16 [3072, 768], replicated, may hold values from -0.109375 to 0.109375
- outer_bias: bfloat16 [768], replicated, may hold values from -2 to 2
- ffn_gain: bfloat16 [768], replicated, may hold values from 0.5 to 1.5
- ffn_shift: bfloat16 [768], replicated, may hold values from -2 to 2
- cotangent: bfloat16 [16, 512, 768], P('dp', 'seq'), may hold values from -6 to 6
Outputs:
- layer_out: bfloat16 [16, 512, 768], P('dp', 'seq')
- input_grad: bfloat16 [16, 512, 768], P('dp', 'seq')
- grad_query_key_value: float32 [768, 2304], P('seq')
- grad_query_bias: float32 [768], P('seq')
- grad_value_bias: float32 [768], P('seq')
- grad_attn_weight: float32 [768, 768], P('seq')
- grad_attn_bias: float32 [768], P('seq')
- grad_attn_gain: float32 [768], P('seq')
- grad_attn_shift: float32 [768], P('seq')
- grad_inner_weight: float32 [768, 3072], P('seq')
- grad_inner_bias: float32 [3072], P('seq')
- grad_outer_weight: float32 [3072, 768], P('seq')
- grad_outer_bias: float32 [768], P('seq')
- grad_ffn_gain: float32 [768], P('seq')
- grad_ffn_shift: float32 [768], P('seq')
The draws below stay inside these ranges and needn't reach their ends.
Inputs may be any that keep to these rules, and one draw needn't show every extreme that they name: `lengths`: slots at or beyond a passage's length are padding. In every aligned group of 2 passages one has length 512, and some passage has length 20.
All inputs are finite; a program needn't handle non-finite values.
Results may differ from the reference program's by a relative error of at most 0.018.
Values may be sent and summed in bfloat16 or wider, within the bound.
No kernel may reach another device: no remote copies, remote signals or barrier semaphores. Data moves between devices by JAX's collectives and lax.ppermute only.
A program may use at most 192 MiB of HBM per device.

```python
import jax
import jax.numpy as jnp
from jax import lax

D = 768
H = 12
HD = 64
FF = 3072
LEN = 512
P_DEV = 2
PASSAGES = 16


def draw_lengths(key, part):
    key = jax.random.fold_in(key, 7)
    streams = jax.random.split(key, 5)
    nearly = jax.random.randint(streams[0], (PASSAGES,), LEN - LEN // 4, LEN + 1)
    shorter = jax.random.randint(streams[1], (PASSAGES,), 20, LEN - LEN // 4)
    picker = jax.random.randint(streams[2], (PASSAGES,), 0, 4)
    drawn = jnp.where(picker == 0, shorter, nearly)
    groups = PASSAGES // P_DEV
    chosen = jax.random.randint(streams[3], (groups,), 0, P_DEV)
    longest = jnp.arange(groups) * P_DEV + chosen
    drawn = drawn.at[longest].set(LEN)
    which_group = jax.random.randint(streams[4], (), 0, groups)
    shortest = which_group * P_DEV + (chosen[which_group] + 1) % P_DEV
    drawn = drawn.at[shortest].set(20)
    return drawn.astype(jnp.int32)


def levels(stream_key, extent, shards, least, top_value):
    level, own = 1.0, jax.random.fold_in(stream_key, 6)
    for dim, shards_of in shards:
        draws = jnp.exp(jax.random.uniform(jax.random.fold_in(own, dim), (shards_of,), jnp.float32, least / len(shards), top_value / len(shards)))
        level = level * jnp.repeat(draws, extent[dim] // shards_of).reshape([-1 if axis == dim else 1 for axis in range(len(extent))])
    return level


def gaussian(own_key, dims, deviation, bound, cuts=(), kind=jnp.bfloat16):
    level = levels(own_key, dims, cuts, -0.22, 0.18) if cuts else 1.0
    values = jax.random.normal(own_key, dims, jnp.float32) * deviation * level
    return jnp.minimum(jnp.maximum(values, -bound), bound).astype(kind)


def setup_inputs(seed: int = 0) -> dict:
    arg_keys = jax.random.split(jax.random.key(seed), 17)
    tokens = gaussian(arg_keys[0], (PASSAGES, LEN, D), 1.0, 6.0, ((0, 8), (1, 4)))
    lengths = draw_lengths(jax.random.fold_in(arg_keys[16], 71), 0)
    query_key_value = gaussian(arg_keys[2], (D, 3 * D), D ** -0.5, 0.21875)
    query_bias = gaussian(arg_keys[3], (D,), 0.5, 3.0)
    value_bias = gaussian(arg_keys[4], (D,), 0.1, 0.59765625)
    attn_weight = gaussian(arg_keys[5], (D, D), (max(D * 8 // LEN, 1)) ** -0.5, 1.75)
    attn_bias = gaussian(arg_keys[6], (D,), 0.3, 2.0)
    attn_gain = jnp.clip(1.0 + 0.1 * jax.random.normal(arg_keys[7], (D,), jnp.float32), 0.5, 1.5).astype(jnp.bfloat16)
    attn_shift = gaussian(arg_keys[8], (D,), 0.3, 2.0)
    inner_weight = gaussian(arg_keys[9], (D, FF), D ** -0.5, 0.21875)
    inner_bias = gaussian(arg_keys[10], (FF,), 0.5, 3.0)
    outer_weight = gaussian(arg_keys[11], (FF, D), FF ** -0.5, 0.109375)
    outer_bias = gaussian(arg_keys[12], (D,), 0.3, 2.0)
    ffn_gain = jnp.clip(1.0 + 0.1 * jax.random.normal(arg_keys[13], (D,), jnp.float32), 0.5, 1.5).astype(jnp.bfloat16)
    ffn_shift = gaussian(arg_keys[14], (D,), 0.3, 2.0)
    cotangent = gaussian(arg_keys[15], (PASSAGES, LEN, D), 1.0, 6.0, ((0, 8), (1, 4)))
    return dict(tokens=tokens, lengths=lengths, query_key_value=query_key_value, query_bias=query_bias, value_bias=value_bias, attn_weight=attn_weight, attn_bias=attn_bias, attn_gain=attn_gain, attn_shift=attn_shift, inner_weight=inner_weight, inner_bias=inner_bias, outer_weight=outer_weight, outer_bias=outer_bias, ffn_gain=ffn_gain, ffn_shift=ffn_shift, cotangent=cotangent)


EPS = 1e-12
HIGH = lax.Precision.HIGHEST

@jax.custom_vjp
def low(v):
    return lax.optimization_barrier(v.astype(jnp.bfloat16)).astype(jnp.float32)

@jax.custom_vjp
def low_back(v):
    return v

def low_keep(v):
    return (low(v), None)

def low_pass(kept, grad):
    return (grad,)

def back_keep(v):
    return (v, None)

def back_low(kept, grad):
    return (low(grad),)
low.defvjp(low_keep, low_pass)
low_back.defvjp(back_keep, back_low)

def layer_norm(field):
    centre = field - lax.optimization_barrier(jnp.mean(field, -1, keepdims=True))
    spread = lax.optimization_barrier(jnp.mean(centre * centre, -1, keepdims=True))
    return centre * lax.rsqrt(spread + EPS)

def forward(tokens, lengths, query_key_value, query_bias, value_bias, attn_weight, attn_bias, attn_gain, attn_shift, inner_weight, inner_bias, outer_weight, outer_bias, ffn_gain, ffn_shift):
    batch_size = tokens.shape[0]
    project = jnp.einsum('bld,de->ble', tokens, query_key_value, precision=HIGH)
    queries = low_back(low(project[..., :D] + query_bias)).reshape(batch_size, LEN, H, HD)
    key_rows = low_back(low(project[..., D:2 * D])).reshape(batch_size, LEN, H, HD)
    values = low_back(low(project[..., 2 * D:] + value_bias)).reshape(batch_size, LEN, H, HD)
    logits = jnp.einsum('bqhe,bkhe->bhqk', queries, key_rows, precision=HIGH) * HD ** (-0.5)
    logits = low_back(logits)
    usable = jnp.arange(LEN)[None, :] < lengths[:, None]
    masked = jnp.where(usable[:, None, None, :], logits, -1000000000.0)
    chance = low(jax.nn.softmax(masked, axis=-1))
    context = jnp.einsum('bhqk,bkhe->bqhe', chance, values, precision=HIGH).reshape(batch_size, LEN, D)
    context = low_back(low(context))
    attended = low_back(jnp.einsum('bld,de->ble', context, attn_weight, precision=HIGH) + attn_bias)
    hidden = layer_norm(tokens + attended) * attn_gain + attn_shift
    inner_pre = low_back(jnp.einsum('bld,df->blf', low(hidden), inner_weight, precision=HIGH) + inner_bias)
    active = low(jax.nn.gelu(inner_pre, approximate=False))
    outer_out = low_back(jnp.einsum('blf,fd->bld', active, outer_weight, precision=HIGH) + outer_bias)
    return layer_norm(hidden + outer_out) * ffn_gain + ffn_shift

def reference(tokens, lengths, query_key_value, query_bias, value_bias, attn_weight, attn_bias, attn_gain, attn_shift, inner_weight, inner_bias, outer_weight, outer_bias, ffn_gain, ffn_shift, cotangent):
    parameters = tuple((weight_matrix.astype(jnp.float32) for weight_matrix in (query_key_value, query_bias, value_bias, attn_weight, attn_bias, attn_gain, attn_shift, inner_weight, inner_bias, outer_weight, outer_bias, ffn_gain, ffn_shift)))
    block_size = max((count for count in (1, 2, 4, 8) if PASSAGES % count == 0))
    block_count = PASSAGES // block_size
    token_blocks = tokens.astype(jnp.float32).reshape(block_count, block_size, LEN, D)
    length_blocks = lengths.reshape(block_count, block_size)
    cotangent_blocks = cotangent.astype(jnp.float32).reshape(block_count, block_size, LEN, D)

    def single_block(total_sums, element):
        tok_block, len_block, cot_block = element

        def apply(tok_rows, *weights):
            return forward(tok_rows, len_block, *weights)
        result, pullback = jax.vjp(apply, tok_block, *parameters)
        gradients = pullback(cot_block)
        total_sums = tuple((left + right for left, right in zip(total_sums, gradients[1:])))
        return (total_sums, (result.astype(jnp.bfloat16), gradients[0].astype(jnp.bfloat16)))
    empty_slots = tuple((jnp.zeros(weight_matrix.shape, jnp.float32) for weight_matrix in parameters))
    total_sums, (output_rows, backward_pass) = lax.scan(single_block, empty_slots, (token_blocks, length_blocks, cotangent_blocks))
    layer_out = output_rows.reshape(PASSAGES, LEN, D)
    input_grad = backward_pass.reshape(PASSAGES, LEN, D)
    return (layer_out, input_grad, total_sums[0], total_sums[1], total_sums[2], total_sums[3], total_sums[4], total_sums[5], total_sums[6], total_sums[7], total_sums[8], total_sums[9], total_sums[10], total_sums[11], total_sums[12])
```

```python
import jax
import jax.numpy as jnp
from jax import lax
from jax.experimental import pallas as pl
from jax.experimental.pallas import tpu as pltpu
from jax.sharding import PartitionSpec as P

H = 12
HD = 64
EPS = 1e-12
F32 = jnp.float32
LOW = jnp.bfloat16
MIB = 1 << 20
PIECES = 8


def dot(a, b):
    return lax.dot_general(a, b, (((1,), (0,)), ((), ())), preferred_element_type=F32)


def dot_nt(a, b):
    return lax.dot_general(a, b, (((1,), (1,)), ((), ())), preferred_element_type=F32)


def dot_tn(a, b):
    return lax.dot_general(a, b, (((0,), (0,)), ((), ())), preferred_element_type=F32)


def vmem(shape=None, index=None):
    if shape is None:
        return pl.BlockSpec(memory_space=pltpu.VMEM)
    return pl.BlockSpec(shape, index)


SMEM = pl.BlockSpec(memory_space=pltpu.SMEM)


def key_mask(me, length, rows, quarter):
    slot = lax.broadcasted_iota(jnp.int32, (rows, 1), 0)
    block = slot // quarter
    return ((block ^ me) * quarter + (slot - block * quarter)) < length


def attend_kernel(where, lengths, x0, x1, x2, x3, w, qb, vb, qkv_out, lse_out, *context_out):
    p = pl.program_id(0)
    quarter = x0.shape[1]
    rows = 4 * quarter
    hw = w.shape[1] // 3
    heads = hw // HD
    x = jnp.concatenate([x0[0], x1[0], x2[0], x3[0]], 0)
    proj = dot(x, w[...])
    q = ((proj[:, :hw] + qb[...]).astype(LOW).astype(F32) * HD ** (-0.5)).astype(LOW)
    k = proj[:, hw : 2 * hw].astype(LOW)
    v = (proj[:, 2 * hw :] + vb[...]).astype(LOW)
    qkv_out[0] = jnp.concatenate([q, k, v], 1)
    usable = key_mask(where[0], lengths[p], rows, quarter)
    parts = []
    for h in range(heads):
        cols = slice(h * HD, (h + 1) * HD)
        logits = jnp.where(usable, dot_nt(k[:, cols], q[:, cols]), -1e9)
        highest = jnp.max(logits, 0, keepdims=True)
        weight = jnp.exp(logits - highest)
        total = jnp.sum(weight, 0, keepdims=True)
        lse_out[0, h : h + 1, :] = highest + jnp.log(total)
        parts.append(dot_tn(v[:, cols], weight.astype(LOW)) * (1.0 / total))
    context = jnp.concatenate(parts, 0).T.astype(LOW)
    for j in range(4):
        context_out[j][0] = context[j * quarter : (j + 1) * quarter]


def attend(where, lengths, shards, w, qb, vb):
    passages, quarter, width = shards[0].shape
    rows = 4 * quarter
    hw = w.shape[1] // 3
    heads = hw // HD
    block = vmem((1, quarter, width), lambda p: (p, 0, 0))
    whole = lambda *shape: vmem(shape, lambda p: (0,) * len(shape))
    return pl.pallas_call(
        attend_kernel,
        grid=(passages,),
        in_specs=[SMEM, SMEM] + [block] * 4 + [whole(width, 3 * hw), whole(1, hw), whole(1, hw)],
        out_specs=[
            vmem((1, rows, 3 * hw), lambda p: (p, 0, 0)),
            vmem((1, heads, rows), lambda p: (p, 0, 0)),
        ]
        + [vmem((1, quarter, hw), lambda p: (p, 0, 0))] * 4,
        out_shape=[
            jax.ShapeDtypeStruct((passages, rows, 3 * hw), LOW),
            jax.ShapeDtypeStruct((passages, heads, rows), F32),
        ]
        + [jax.ShapeDtypeStruct((passages, quarter, hw), LOW)] * 4,
        compiler_params=pltpu.CompilerParams(vmem_limit_bytes=40 * MIB),
        cost_estimate=pl.CostEstimate(flops=3 * 10**9, bytes_accessed=6 * 10**6, transcendentals=10**6),
        name="attend",
    )(where, lengths, *shards, w, qb, vb)


def attend_back_kernel(
    where, lengths, x0, x1, x2, x3, w, qkv, lse, g0, g1, g2, g3,
    keep_out, send_out, weight_out, bias_out, acc,
):
    p = pl.program_id(0)
    me = where[0]
    quarter = x0.shape[1]
    rows = 4 * quarter
    hw = w.shape[1] // 3
    heads = hw // HD
    scale = HD ** (-0.5)
    x = jnp.concatenate([x0[0], x1[0], x2[0], x3[0]], 0)
    g = jnp.concatenate([g0[0], g1[0], g2[0], g3[0]], 0)
    usable = key_mask(me, lengths[p], rows, quarter)
    q = qkv[0, :, :hw]
    k = qkv[0, :, hw : 2 * hw]
    v = qkv[0, :, 2 * hw :]
    grad_q, grad_k, grad_v = [], [], []
    for h in range(heads):
        cols = slice(h * HD, (h + 1) * HD)
        qh, kh, vh, gh = q[:, cols], k[:, cols], v[:, cols], g[:, cols]
        logits = jnp.where(usable, dot_nt(kh, qh), -1e9)
        chance = jnp.exp(logits - lse[0, h : h + 1, :])
        grad_chance = dot_nt(vh, gh)
        inner = jnp.sum(grad_chance * chance, 0, keepdims=True)
        grad_logits = (chance * (grad_chance - inner)).astype(LOW)
        grad_q.append(dot_tn(kh, grad_logits) * scale)
        grad_k.append(dot(grad_logits, qh))
        grad_v.append(dot(chance.astype(LOW), gh))
    gq = jnp.concatenate(grad_q, 0).T.astype(LOW)
    gk = jnp.concatenate(grad_k, 1).astype(LOW)
    gv = jnp.concatenate(grad_v, 1).astype(LOW)
    joined = jnp.concatenate([gq, gk, gv], 1)
    part = dot_tn(x, joined)
    sums = jnp.concatenate(
        [
            jnp.sum(gq.astype(F32), 0, keepdims=True),
            jnp.sum(gv.astype(F32), 0, keepdims=True),
        ],
        0,
    )

    @pl.when(p == 0)
    def _():
        acc[...] = part
        bias_out[...] = sums

    @pl.when(p > 0)
    def _():
        acc[...] += part
        bias_out[...] += sums

    back = dot_nt(joined, w[...]).astype(LOW)
    for j in range(4):
        out = send_out if j % 2 else keep_out
        out[j // 2, 0] = back[j * quarter : (j + 1) * quarter]

    @pl.when(p == pl.num_programs(0) - 1)
    def _():
        n = weight_out.shape[2]
        for j in range(4):
            for e in range(PIECES):
                start = pl.multiple_of((me ^ j) * (n * PIECES) + e * n, 8)
                weight_out[e, j] = acc[pl.ds(start, n), :].astype(LOW)


def attend_back(where, lengths, shards, w, qkv, lse, grads):
    passages, quarter, width = shards[0].shape
    rows = 4 * quarter
    hw = w.shape[1] // 3
    heads = hw // HD
    n = width // (4 * PIECES)
    block = vmem((1, quarter, width), lambda p: (p, 0, 0))
    gblock = vmem((1, quarter, hw), lambda p: (p, 0, 0))
    whole = lambda *shape: vmem(shape, lambda p: (0,) * len(shape))
    return pl.pallas_call(
        attend_back_kernel,
        grid=(passages,),
        in_specs=[SMEM, SMEM]
        + [block] * 4
        + [
            whole(width, 3 * hw),
            vmem((1, rows, 3 * hw), lambda p: (p, 0, 0)),
            vmem((1, heads, rows), lambda p: (p, 0, 0)),
        ]
        + [gblock] * 4,
        out_specs=[
            vmem((2, 1, quarter, width), lambda p: (0, p, 0, 0)),
            vmem((2, 1, quarter, width), lambda p: (0, p, 0, 0)),
            whole(PIECES, 4, n, 3 * hw),
            whole(2, hw),
        ],
        out_shape=[
            jax.ShapeDtypeStruct((2, passages, quarter, width), LOW),
            jax.ShapeDtypeStruct((2, passages, quarter, width), LOW),
            jax.ShapeDtypeStruct((PIECES, 4, n, 3 * hw), LOW),
            jax.ShapeDtypeStruct((2, hw), F32),
        ],
        scratch_shapes=[pltpu.VMEM((width, 3 * hw), F32)],
        compiler_params=pltpu.CompilerParams(vmem_limit_bytes=48 * MIB),
        cost_estimate=pl.CostEstimate(flops=5 * 10**9, bytes_accessed=10**7, transcendentals=10**6),
        name="attend_back",
    )(where, lengths, *shards, w, qkv, lse, *grads)


def normalise(field):
    centre = field - jnp.mean(field, -1, keepdims=True)
    scale = lax.rsqrt(jnp.mean(centre * centre, -1, keepdims=True) + EPS)
    return centre * scale, scale


def normalise_back(grad, normal, scale):
    return (
        grad
        - jnp.mean(grad, -1, keepdims=True)
        - normal * jnp.mean(grad * normal, -1, keepdims=True)
    ) * scale


def rows_kernel(
    where, x, c0, c1, c2, c3, cot, wa, vec, ib, wi_hbm, wo_hbm,
    layer_out, grad_one_out, hidden_out, active_out, inner_out, outer_out, attn_out,
    h0, h1, h2, h3, sums_out, inner_bias_out,
    wi, wo, slope, sem,
):
    me = where[0]
    width = x.shape[1]
    ff = ib.shape[1]
    chunk = width
    chunks = ff // chunk
    hw = c0.shape[1]

    def copies(c):
        cols = pl.ds(c * chunk, chunk)
        return (
            pltpu.make_async_copy(wi_hbm.at[:, cols], wi.at[:, cols], sem.at[2 * c]),
            pltpu.make_async_copy(wo_hbm.at[cols, :], wo.at[cols, :], sem.at[2 * c + 1]),
        )

    for c in range(chunks):
        for copy in copies(c):
            copy.start()
    row = lambda r: vec[r : r + 1, :]
    attn_bias, attn_gain, attn_shift, outer_bias, ffn_gain, ffn_shift = (row(r) for r in range(6))
    attended = attn_bias + x[...].astype(F32)
    for j, part in enumerate((c0, c1, c2, c3)):
        attended += dot(part[...], wa[me ^ j])
    normal_one, scale_one = normalise(attended)
    hidden = normal_one * attn_gain + attn_shift
    hidden_low = hidden.astype(LOW)
    hidden_out[...] = hidden_low
    pre_two = hidden + outer_bias
    for c in range(chunks):
        cols = slice(c * chunk, (c + 1) * chunk)
        first, second = copies(c)
        first.wait()
        u = dot(hidden_low, wi[:, cols]) + ib[:, cols]
        below = 0.5 * (1.0 + lax.erf(u * (0.5**0.5)))
        density = jnp.exp(-0.5 * u * u) * 0.3989422804014327
        active = (u * below).astype(LOW)
        slope[:, cols] = below + u * density
        active_out[:, cols] = active
        second.wait()
        pre_two += dot(active, wo[cols, :])
    normal_two, scale_two = normalise(pre_two)
    layer_out[...] = (normal_two * ffn_gain + ffn_shift).astype(LOW)
    dy = cot[...].astype(F32)
    sums_out[4:5, :] = jnp.sum(dy * normal_two, 0, keepdims=True)
    sums_out[5:6, :] = jnp.sum(dy, 0, keepdims=True)
    grad_two = normalise_back(dy * ffn_gain, normal_two, scale_two)
    grad_outer = grad_two.astype(LOW)
    outer_out[...] = grad_outer
    sums_out[3:4, :] = jnp.sum(grad_outer.astype(F32), 0, keepdims=True)
    grad_hidden = grad_two
    for c in range(chunks):
        cols = slice(c * chunk, (c + 1) * chunk)
        grad_inner = (dot_nt(grad_outer, wo[cols, :]) * slope[:, cols]).astype(LOW)
        inner_out[:, cols] = grad_inner
        inner_bias_out[:, cols] = jnp.sum(grad_inner.astype(F32), 0, keepdims=True)
        grad_hidden += dot_nt(grad_inner, wi[:, cols])
    sums_out[1:2, :] = jnp.sum(grad_hidden * normal_one, 0, keepdims=True)
    sums_out[2:3, :] = jnp.sum(grad_hidden, 0, keepdims=True)
    grad_one = normalise_back(grad_hidden * attn_gain, normal_one, scale_one)
    grad_one_out[...] = grad_one
    grad_attn = grad_one.astype(LOW)
    attn_out[...] = grad_attn
    sums_out[0:1, :] = jnp.sum(grad_attn.astype(F32), 0, keepdims=True)
    sums_out[6:8, :] = jnp.zeros((2, width), F32)
    for j, out in enumerate((h0, h1, h2, h3)):
        out[...] = dot_nt(grad_attn, wa[me ^ j]).astype(LOW)


def rows_pass(where, x, context, cot, wa, vec, ib, wi, wo):
    rows, width = x.shape
    ff = ib.shape[1]
    hw = context[0].shape[1]
    hbm = pl.BlockSpec(memory_space=pl.ANY)
    low = lambda *s: jax.ShapeDtypeStruct(s, LOW)
    full = lambda *s: jax.ShapeDtypeStruct(s, F32)
    return pl.pallas_call(
        rows_kernel,
        in_specs=[SMEM] + [vmem()] * 9 + [hbm, hbm],
        out_specs=[vmem()] * 13,
        out_shape=[
            low(rows, width), full(rows, width), low(rows, width), low(rows, ff), low(rows, ff),
            low(rows, width), low(rows, width),
            low(rows, hw), low(rows, hw), low(rows, hw), low(rows, hw),
            full(8, width), full(1, ff),
        ],
        scratch_shapes=[
            pltpu.VMEM(wi.shape, LOW),
            pltpu.VMEM(wo.shape, LOW),
            pltpu.VMEM((rows, ff), F32),
            pltpu.SemaphoreType.DMA((2 * (ff // width),)),
        ],
        compiler_params=pltpu.CompilerParams(vmem_limit_bytes=48 * MIB),
        cost_estimate=pl.CostEstimate(flops=6 * 10**9, bytes_accessed=2 * 10**7, transcendentals=10**6),
        name="rows_pass",
    )(where, x, *context, cot, wa, vec, ib, wi, wo)


def outer_grad_kernel(where, active, grad, send_out, keep_out):
    j = pl.program_id(0)
    width = grad.shape[1]
    n = width // PIECES
    relative = jnp.where(j < 2, 2 * j + 1, 2 * j - 4)
    cols = pl.ds(pl.multiple_of((where[0] ^ relative) * width, 128), width)
    product = dot_tn(active[:, cols], grad[...]).astype(LOW)

    def store(out):
        for e in range(PIECES):
            out[0, e] = product[e * n : (e + 1) * n]

    pl.when(j < 2)(lambda: store(send_out))
    pl.when(j >= 2)(lambda: store(keep_out))


def outer_grad(where, active, grad):
    rows, width = grad.shape
    ff = active.shape[1]
    shape = (2, PIECES, width // PIECES, width)
    return pl.pallas_call(
        outer_grad_kernel,
        grid=(4,),
        in_specs=[
            SMEM,
            vmem((rows, ff), lambda j: (0, 0)),
            vmem((rows, width), lambda j: (0, 0)),
        ],
        out_specs=[
            vmem((1,) + shape[1:], lambda j: (jnp.minimum(j, 1), 0, 0, 0)),
            vmem((1,) + shape[1:], lambda j: (jnp.maximum(j - 2, 0), 0, 0, 0)),
        ],
        out_shape=[jax.ShapeDtypeStruct(shape, LOW)] * 2,
        compiler_params=pltpu.CompilerParams(vmem_limit_bytes=32 * MIB),
        cost_estimate=pl.CostEstimate(flops=2 * rows * ff * width, bytes_accessed=8 * 10**6, transcendentals=0),
        name="outer_grad",
    )(where, active, grad)


def inner_grad_kernel(where, hidden, grad_inner, c0, c1, c2, c3, grad_attn, send_out, keep_out, left):
    c = pl.program_id(0)
    me = where[0]
    hw = c0.shape[1]
    n = hw // PIECES
    width = hidden.shape[1]

    @pl.when(c == 0)
    def _():
        flipped = hidden[...].astype(F32).T.astype(LOW)
        left[...] = flipped

    def store(j, rows, value):
        out = send_out if j % 2 else keep_out
        out[j // 2, 0, rows, :] = value

    for j in range(4):
        rows = pl.ds(pl.multiple_of((me ^ j) * hw, 64), hw)
        store(j, slice(0, hw), dot(left[rows, :], grad_inner[...]).astype(LOW))
    for j, part in enumerate((c0, c1, c2, c3)):
        half = width // 2
        mine = dot_tn(part[...], grad_attn[...])
        for e in range(PIECES):
            @pl.when(c == e)
            def _(e=e, j=j, mine=mine):
                piece = mine[e * n : (e + 1) * n]
                store(j, slice(hw, hw + 2 * n), jnp.concatenate([piece[:, :half], piece[:, half:]], 0).astype(LOW))


def inner_grad(where, hidden, grad_inner, context, grad_attn):
    rows, width = hidden.shape
    ff = grad_inner.shape[1]
    hw = context[0].shape[1]
    n = hw // PIECES
    cols = ff // PIECES
    shape = (2, PIECES, hw + 2 * n, cols)
    whole = lambda *s: vmem(s, lambda c: (0,) * len(s))
    return pl.pallas_call(
        inner_grad_kernel,
        grid=(PIECES,),
        in_specs=[SMEM, whole(rows, width), vmem((rows, cols), lambda c: (0, c))]
        + [whole(rows, hw)] * 4
        + [whole(rows, width)],
        out_specs=[vmem((2, 1, hw + 2 * n, cols), lambda c: (0, c, 0, 0))] * 2,
        out_shape=[jax.ShapeDtypeStruct(shape, LOW)] * 2,
        scratch_shapes=[pltpu.VMEM((width, rows), LOW)],
        compiler_params=pltpu.CompilerParams(vmem_limit_bytes=32 * MIB),
        cost_estimate=pl.CostEstimate(flops=2 * rows * ff * width, bytes_accessed=8 * 10**6, transcendentals=0),
        name="inner_grad",
    )(where, hidden, grad_inner, *context, grad_attn)


def outer_place_kernel(place, piece, out):
    out[...] = piece[0].astype(F32)


def outer_place(place, pieces):
    count, n, width = pieces.shape
    return pl.pallas_call(
        outer_place_kernel,
        grid_spec=pltpu.PrefetchScalarGridSpec(
            num_scalar_prefetch=1,
            grid=(count,),
            in_specs=[vmem((1, n, width), lambda a, place: (a ^ place[0], 0, 0))],
            out_specs=vmem((n, width), lambda a, place: (a, 0)),
        ),
        out_shape=jax.ShapeDtypeStruct((count * n, width), F32),
        name="outer_place",
    )(place, pieces)


def inner_place_kernel(place, piece, inner, attn):
    hw = inner.shape[0]
    n = attn.shape[0]
    inner[...] = piece[0, :hw, :].astype(F32)
    rest = piece[0, hw:, :].astype(F32)
    attn[...] = jnp.concatenate([rest[:n], rest[n:]], 1)


def inner_place(place, pieces, hw):
    count, tall, cols = pieces.shape
    n = (tall - hw) // 2
    return pl.pallas_call(
        inner_place_kernel,
        grid_spec=pltpu.PrefetchScalarGridSpec(
            num_scalar_prefetch=1,
            grid=(count,),
            in_specs=[vmem((1, tall, cols), lambda a, place: (a ^ place[0], 0, 0))],
            out_specs=[
                vmem((hw, cols), lambda a, place: (0, a)),
                vmem((n, 2 * cols), lambda a, place: (a, 0)),
            ],
        ),
        out_shape=[
            jax.ShapeDtypeStruct((hw, count * cols), F32),
            jax.ShapeDtypeStruct((count * n, 2 * cols), F32),
        ],
        name="inner_place",
    )(place, pieces)


def project_place_kernel(place, piece, out):
    hw = piece.shape[3] // 3
    for owner in range(4):
        block = piece[0, owner ^ place[1]].astype(F32)
        for t in range(3):
            start = t * 4 * hw + owner * hw
            out[:, start : start + hw] = block[:, t * hw : (t + 1) * hw]


def project_place(place, pieces):
    count, groups, n, wide = pieces.shape
    return pl.pallas_call(
        project_place_kernel,
        grid_spec=pltpu.PrefetchScalarGridSpec(
            num_scalar_prefetch=1,
            grid=(count,),
            in_specs=[vmem((1, groups, n, wide), lambda a, place: (a ^ place[0], 0, 0, 0))],
            out_specs=vmem((n, groups * wide), lambda a, place: (a, 0)),
        ),
        out_shape=jax.ShapeDtypeStruct((count * n, groups * wide), F32),
        name="project_place",
    )(place, pieces)


def swap(field, axis, bit):
    count = lax.axis_size(axis)
    return lax.ppermute(field, axis, [(i, i ^ bit) for i in range(count)])


def halve(left, right, axis, bit, dim=0):
    n = left.shape[dim] // 2
    mine = jnp.where(lax.axis_index(axis) & bit, 1, 0)
    cut = lambda f, i: lax.dynamic_slice_in_dim(f, i * n, n, dim)
    both = lambda i: cut(left, i) if right is None else (cut(left, i).astype(F32) + cut(right, i).astype(F32)).astype(LOW)
    got = swap(both(1 - mine), axis, bit)
    return both(mine), got


def spread(piece, bits):
    for bit in reversed(bits):
        piece = jnp.concatenate([piece, swap(piece, "dp", bit)], 0)
    return piece


def add(left, right):
    return (left.astype(F32) + right.astype(F32)).astype(LOW)


def sum_lanes(left, right, bits, rest):
    for bit in bits:
        left, right = halve(left, right, "dp", bit)
    total = add(left, right)
    for bit in rest:
        total = add(total, swap(total, "dp", bit))
    return total


def local(
    tokens, lengths, query_key_value, query_bias, value_bias, attn_weight, attn_bias, attn_gain,
    attn_shift, inner_weight, inner_bias, outer_weight, outer_bias, ffn_gain, ffn_shift, cotangent,
):
    groups = lax.axis_size("seq")
    lanes = lax.axis_size("dp")
    me = lax.axis_index("seq")
    lane = lax.axis_index("dp")
    passages, quarter, width = tokens.shape
    hw = H // groups * HD
    rows = passages * quarter
    ff = inner_bias.shape[0]
    bits = [1, 2, 4]
    rest = [1 << i for i in range(3, lanes.bit_length() - 1)]
    where = me.astype(jnp.int32).reshape(1)
    piece_of = ((lane & 1) * 4 + (lane & 2) + (lane >> 2 & 1)).astype(jnp.int32)
    place = jnp.stack([piece_of, me.astype(jnp.int32)])

    across = swap(tokens, "seq", 2)
    beside = swap(tokens, "seq", 1)
    corner = swap(across, "seq", 1)
    shards = (tokens, beside, across, corner)

    cut = lambda f, start: lax.dynamic_slice_in_dim(f, start + me * hw, hw, f.ndim - 1)
    w = jnp.concatenate([cut(query_key_value, t * width) for t in range(3)], 1)
    qb = cut(query_bias, 0).astype(F32).reshape(1, hw)
    vb = cut(value_bias, 0).astype(F32).reshape(1, hw)
    qkv, lse, *context_h = attend(where, lengths, shards, w, qb, vb)
    context = [context_h[0]] + [swap(context_h[j], "seq", j) for j in (1, 2, 3)]
    context = [part.reshape(rows, hw) for part in context]

    vec = jnp.stack([attn_bias, attn_gain, attn_shift, outer_bias, ffn_gain, ffn_shift, ffn_shift, ffn_shift])
    (
        layer_out, grad_one, hidden, active, grad_inner, grad_outer, grad_attn,
        h0, h1, h2, h3, sums, inner_sums,
    ) = rows_pass(
        where,
        tokens.reshape(rows, width),
        context,
        cotangent.reshape(rows, width),
        attn_weight.reshape(groups, hw, width),
        vec.astype(F32),
        inner_bias.astype(F32).reshape(1, ff),
        inner_weight,
        outer_weight,
    )
    grads_h = [h0] + [swap(part, "seq", j) for j, part in ((1, h1), (2, h2), (3, h3))]
    grads_h = [part.reshape(passages, quarter, hw) for part in grads_h]

    outer_send, outer_keep = outer_grad(where, active, grad_outer)
    inner_send, inner_keep = inner_grad(where, hidden, grad_inner, context, grad_attn)

    keep, send, project_grad, bias_sums = attend_back(where, lengths, shards, w, qkv, lse, grads_h)

    def sum_groups(kept, sent):
        got = swap(sent, "seq", 1)
        over = swap(add(kept[1], got[1]), "seq", 2)
        return add(kept[0], got[0]), over

    outer_total = spread(sum_lanes(*sum_groups(outer_keep, outer_send), bits, rest), bits)
    inner_total = spread(sum_lanes(*sum_groups(inner_keep, inner_send), bits, rest), bits)
    project = sum_lanes(project_grad, None, bits, rest)
    got = [project[:, 0]] + [swap(project[:, j], "seq", j) for j in (1, 2, 3)]
    project_total = spread(jnp.stack(got, 1), bits)

    grad_outer_weight = outer_place(place, outer_total)
    grad_inner_weight, grad_attn_weight = inner_place(place, inner_total, hw)
    grad_query_key_value = project_place(place, project_total)

    back, over = sum_groups(keep, send)
    input_grad = (
        grad_one.reshape(passages, quarter, width) + back.astype(F32) + over.astype(F32)
    ).astype(LOW)

    vectors = lax.psum(jnp.concatenate([sums[:6].reshape(-1), inner_sums.reshape(-1)]), ("dp", "seq"))
    mine = lambda r: lax.dynamic_slice(vectors, (r * width + me * hw,), (hw,))
    inner_bias_sum = lax.dynamic_slice(vectors, (6 * width + me * (ff // groups),), (ff // groups,))
    head_sums = lax.psum(bias_sums, "dp")
    return (
        layer_out.reshape(passages, quarter, width),
        input_grad,
        grad_query_key_value,
        head_sums[0],
        head_sums[1],
        grad_attn_weight,
        mine(0),
        mine(1),
        mine(2),
        grad_inner_weight,
        inner_bias_sum,
        grad_outer_weight,
        mine(3),
        mine(4),
        mine(5),
    )


def solution(mesh):
    rows = P("dp", "seq", None)
    return jax.shard_map(
        local,
        mesh=mesh,
        in_specs=(rows, P("dp")) + (P(),) * 13 + (rows,),
        out_specs=(
            rows,
            rows,
            P("seq", None),
            P("seq"),
            P("seq"),
            P("seq", None),
            P("seq"),
            P("seq"),
            P("seq"),
            P("seq", None),
            P("seq"),
            P("seq", None),
            P("seq"),
            P("seq"),
            P("seq"),
        ),
        check_vma=False,
    )
```

```python
import jax
import jax.numpy as jnp
from jax import lax
from jax.experimental import pallas as pl
from jax.experimental.pallas import tpu as pltpu
from jax.sharding import PartitionSpec as P

H = 12
HD = 64
EPS = 1e-12
F32 = jnp.float32
LOW = jnp.bfloat16
MIB = 1 << 20
PIECES = 8


def cost(us):
    return pl.CostEstimate(flops=int(us * 1.15e9), bytes_accessed=int(us * 3.69e6), transcendentals=0)


def dot(a, b):
    return lax.dot_general(a, b, (((1,), (0,)), ((), ())), preferred_element_type=F32)


def dot_nt(a, b):
    return lax.dot_general(a, b, (((1,), (1,)), ((), ())), preferred_element_type=F32)


def dot_tn(a, b):
    return lax.dot_general(a, b, (((0,), (0,)), ((), ())), preferred_element_type=F32)


def vmem(shape=None, index=None):
    if shape is None:
        return pl.BlockSpec(memory_space=pltpu.VMEM)
    return pl.BlockSpec(shape, index)


SMEM = pl.BlockSpec(memory_space=pltpu.SMEM)
HBM = pl.BlockSpec(memory_space=pltpu.HBM)


def far(array):
    return pltpu.with_memory_space_constraint(array, pltpu.HBM)


def key_mask(me, length, rows, quarter):
    slot = lax.broadcasted_iota(jnp.int32, (rows, 1), 0)
    block = slot // quarter
    return ((block ^ me) * quarter + (slot - block * quarter)) < length


def attend_kernel(where, lengths, x0, x1, x2, x3, w_hbm, qb, vb, qkv_out, lse_out, w, *refs):
    near_out, across_out, wide, sem = refs
    p = pl.program_id(0)
    me = where[0]
    quarter, width = x0.shape[1:]
    rows = 4 * quarter
    hw = w.shape[1] // 3
    window = wide.shape[2]
    odd = (me & 1) == 1
    first = pl.multiple_of(me * hw - (me & 1) * HD, 128)
    choose = lambda f: jnp.where(odd, f[:, HD : HD + hw], f[:, :hw])

    @pl.when(p == 0)
    def _():
        copies = [
            pltpu.make_async_copy(
                w_hbm.at[:, pl.ds(pl.multiple_of(t * width + first, 128), window)], wide.at[t], sem.at[t]
            )
            for t in range(3)
        ]
        for copy in copies:
            copy.start()
        for t, copy in enumerate(copies):
            copy.wait()
            w[:, t * hw : (t + 1) * hw] = choose(wide[t])

    heads = hw // HD
    x = jnp.concatenate([x0[0], x1[0], x2[0], x3[0]], 0)
    proj = dot(x, w[...])
    here = pl.ds(first, window)
    q = ((proj[:, :hw] + choose(qb[:, here].astype(F32))).astype(LOW).astype(F32) * HD ** (-0.5)).astype(LOW)
    k = proj[:, hw : 2 * hw].astype(LOW)
    v = (proj[:, 2 * hw :] + choose(vb[:, here].astype(F32))).astype(LOW)
    qkv_out[0] = jnp.concatenate([q, k, v], 1)
    usable = key_mask(me, lengths[p], rows, quarter)
    parts = []
    for h in range(heads):
        cols = slice(h * HD, (h + 1) * HD)
        logits = jnp.where(usable, dot_nt(k[:, cols], q[:, cols]), -1e9)
        highest = jnp.max(logits, 0, keepdims=True)
        weight = jnp.exp(logits - highest)
        total = jnp.sum(weight, 0, keepdims=True)
        lse_out[0, h : h + 1, :] = highest + jnp.log(total)
        parts.append(dot_tn(v[:, cols], weight.astype(LOW)) * (1.0 / total))
    context = jnp.concatenate(parts, 0).T.astype(LOW)
    for j in range(4):
        out = across_out if j > 1 else near_out
        out[j & 1, 0] = context[j * quarter : (j + 1) * quarter]


def attend(where, lengths, shards, w, qb, vb):
    passages, quarter, width = shards[0].shape
    rows = 4 * quarter
    hw = width // 4
    window = hw + HD
    heads = hw // HD
    block = vmem((1, quarter, width), lambda p: (p, 0, 0))
    whole = lambda *shape: vmem(shape, lambda p: (0,) * len(shape))
    return pl.pallas_call(
        attend_kernel,
        grid=(passages,),
        in_specs=[SMEM, SMEM] + [block] * 4 + [HBM, whole(1, width), whole(1, width)],
        out_specs=[
            vmem((1, rows, 3 * hw), lambda p: (p, 0, 0)),
            vmem((1, heads, rows), lambda p: (p, 0, 0)),
            whole(width, 3 * hw),
        ]
        + [vmem((2, 1, quarter, hw), lambda p: (0, p, 0, 0))] * 2,
        out_shape=[
            pltpu.HBM((passages, rows, 3 * hw), LOW),
            pltpu.HBM((passages, heads, rows), F32),
            pltpu.HBM((width, 3 * hw), LOW),
        ]
        + [jax.ShapeDtypeStruct((2, passages, quarter, hw), LOW)] * 2,
        scratch_shapes=[pltpu.VMEM((3, width, window), LOW), pltpu.SemaphoreType.DMA((3,))],
        compiler_params=pltpu.CompilerParams(vmem_limit_bytes=16 * MIB),
        cost_estimate=cost(5.5),
        name="attend",
    )(where, lengths, *map(far, shards), far(w), qb, vb)


def attend_back_kernel(
    place, lengths, x0, x1, x2, x3, w, qkv, lse, near, near_got, far_got, vectors, *refs
):
    keep_out, send_out, weight_send, weight_keep, acc, bias = refs[-6:]
    p = pl.program_id(0)
    me = place[1]
    quarter = x0.shape[1]
    rows = 4 * quarter
    hw = w.shape[1] // 3
    heads = hw // HD
    scale = HD ** (-0.5)
    x = jnp.concatenate([x0[0], x1[0], x2[0], x3[0]], 0)
    g = jnp.concatenate([near[0, 0], near_got[0, 0], far_got[0, 0], near_got[1, 0]], 0)
    usable = key_mask(me, lengths[p], rows, quarter)
    q = qkv[0, :, :hw]
    k = qkv[0, :, hw : 2 * hw]
    v = qkv[0, :, 2 * hw :]
    grad_q, grad_k, grad_v = [], [], []
    for h in range(heads):
        cols = slice(h * HD, (h + 1) * HD)
        qh, kh, vh, gh = q[:, cols], k[:, cols], v[:, cols], g[:, cols]
        logits = jnp.where(usable, dot_nt(kh, qh), -1e9)
        chance = jnp.exp(logits - lse[0, h : h + 1, :])
        grad_chance = dot_nt(vh, gh)
        inner = jnp.sum(grad_chance * chance, 0, keepdims=True)
        grad_logits = (chance * (grad_chance - inner)).astype(LOW)
        grad_q.append(dot_tn(kh, grad_logits) * scale)
        grad_k.append(dot(grad_logits, qh))
        grad_v.append(dot(chance.astype(LOW), gh))
    gq = jnp.concatenate(grad_q, 0).T.astype(LOW)
    gk = jnp.concatenate(grad_k, 1).astype(LOW)
    gv = jnp.concatenate(grad_v, 1).astype(LOW)
    joined = jnp.concatenate([gq, gk, gv], 1)
    part = dot_tn(x, joined)
    sums = [jnp.sum(f.astype(F32), 0, keepdims=True) for f in (gq, gv)]
    wide = 3 * hw

    @pl.when(p == 0)
    def _():
        acc[:, :wide] = part
        bias[...] = jnp.zeros_like(bias)

    @pl.when(p > 0)
    def _():
        acc[:, :wide] += part

    here = pl.ds(pl.multiple_of(me * 256, 128), hw)
    for i in range(2):
        bias[i : i + 1, here] += sums[i]

    back = dot_nt(joined, w[...]).astype(LOW)
    for j in range(4):
        out = send_out if j % 2 else keep_out
        out[j // 2, 0] = back[j * quarter : (j + 1) * quarter]

    @pl.when(p == pl.num_programs(0) - 1)
    def _():
        n = weight_send.shape[2] // 4
        rows_of = jnp.concatenate([bias[:, i * 256 : i * 256 + hw] for i in range(4)], 1)
        extra = jnp.concatenate([vectors[:10, :], rows_of[:2, :], jnp.zeros((52, vectors.shape[1]), F32)], 0)
        acc[:, wide:] = extra.T
        half = PIECES // 2
        spot = place[0] & half
        for out, first in ((weight_send, spot ^ half), (weight_keep, spot)):
            for j in range(4):
                for e in range(half):
                    start = pl.multiple_of((me ^ j) * (n * PIECES) + (first + e) * n, 8)
                    out[0, e, j * n : (j + 1) * n, :] = acc[pl.ds(start, n), :].astype(LOW)


def attend_back(place, lengths, shards, w, qkv, lse, grads, vectors, after=()):
    passages, quarter, width = shards[0].shape
    rows = 4 * quarter
    hw = w.shape[1] // 3
    heads = hw // HD
    n = width // (4 * PIECES)
    block = vmem((1, quarter, width), lambda p: (p, 0, 0))
    gblock = vmem((2, 1, quarter, hw), lambda p: (0, p, 0, 0))
    whole = lambda *shape: vmem(shape, lambda p: (0,) * len(shape))
    return pl.pallas_call(
        attend_back_kernel,
        grid=(passages,),
        in_specs=[SMEM, SMEM]
        + [block] * 4
        + [
            whole(width, 3 * hw),
            vmem((1, rows, 3 * hw), lambda p: (p, 0, 0)),
            vmem((1, heads, rows), lambda p: (p, 0, 0)),
        ]
        + [gblock] * 3
        + [whole(*vectors.shape)]
        + [ANYWHERE] * len(after),
        out_specs=[
            vmem((2, 1, quarter, width), lambda p: (0, p, 0, 0)),
            vmem((2, 1, quarter, width), lambda p: (0, p, 0, 0)),
            whole(1, PIECES // 2, 4 * n, 3 * hw + 64),
            whole(1, PIECES // 2, 4 * n, 3 * hw + 64),
        ],
        out_shape=[
            jax.ShapeDtypeStruct((2, passages, quarter, width), LOW),
            jax.ShapeDtypeStruct((2, passages, quarter, width), LOW),
            jax.ShapeDtypeStruct((1, PIECES // 2, 4 * n, 3 * hw + 64), LOW),
            jax.ShapeDtypeStruct((1, PIECES // 2, 4 * n, 3 * hw + 64), LOW),
        ],
        scratch_shapes=[pltpu.VMEM((width, 3 * hw + 64), F32), pltpu.VMEM((8, 1024), F32)],
        compiler_params=pltpu.CompilerParams(vmem_limit_bytes=24 * MIB),
        cost_estimate=cost(11),
        name="attend_back",
    )(place, lengths, *map(far, shards), far(w), far(qkv), far(lse), *grads, vectors, *after)


def normalise(field):
    centre = field - jnp.mean(field, -1, keepdims=True)
    scale = lax.rsqrt(jnp.mean(centre * centre, -1, keepdims=True) + EPS)
    return centre * scale, scale


def normalise_back(grad, normal, scale):
    return (
        grad
        - jnp.mean(grad, -1, keepdims=True)
        - normal * jnp.mean(grad * normal, -1, keepdims=True)
    ) * scale


def rows_kernel(
    where, x, near, near_got, far_got, cot, wa, vec, ib, wi_hbm, wo_hbm,
    layer_out, hidden_own, hidden_send, active_own, active_send, slope, outer_out, grad_out, normal_out, scale_out,
    sums_out, wi, wo, flipped, sem,
):
    me = where[0]
    width = x.shape[1]
    chunk = width
    hw = near.shape[2]

    def copies(c):
        cols = pl.ds(pl.multiple_of((me ^ c) * chunk, 128), chunk)
        return (
            pltpu.make_async_copy(wi_hbm.at[:, cols], wi.at[:, cols], sem.at[2 * c]),
            pltpu.make_async_copy(wo_hbm.at[cols, :], wo.at[cols, :], sem.at[2 * c + 1]),
        )

    for c in range(4):
        for copy in copies(c):
            copy.start()
    row = lambda r: vec[r : r + 1, :]
    attn_bias, attn_gain, attn_shift, outer_bias, ffn_gain, ffn_shift = (row(r) for r in range(6))
    attended = attn_bias + x[...].astype(F32)
    for j, part in enumerate((near[0], near_got[0], far_got[0], near_got[1])):
        attended += dot(part, wa[me ^ j])
    normal_one, scale_one = normalise(attended)
    normal_out[...] = normal_one
    scale_out[...] = scale_one
    hidden = normal_one * attn_gain + attn_shift
    hidden_low = hidden.astype(LOW)
    pre_two = hidden + outer_bias
    for c in range(4):
        cols = pl.ds(pl.multiple_of((me ^ c) * chunk, 128), chunk)
        first, second = copies(c)
        first.wait()
        u = dot(hidden_low, wi[:, cols]) + ib[:, cols]
        below = 0.5 * (1.0 + lax.erf(u * (0.5**0.5)))
        density = jnp.exp(-0.5 * u * u) * 0.3989422804014327
        active = (u * below).astype(LOW)
        slope[c] = below + u * density
        here = active_send if c & 1 else active_own
        here[:, (c >> 1) * chunk : ((c >> 1) + 1) * chunk] = active
        second.wait()
        pre_two += dot(active, wo[cols, :])
    flipped[...] = hidden.T
    for j in range(4):
        start = pl.multiple_of((me ^ j) * hw, 64)
        here = hidden_send if j & 1 else hidden_own
        here[j >> 1] = flipped[pl.ds(start, hw), :].astype(LOW)
    normal_two, scale_two = normalise(pre_two)
    layer_out[...] = (normal_two * ffn_gain + ffn_shift).astype(LOW)
    dy = cot[...].astype(F32)
    sums_out[...] = jnp.zeros_like(sums_out)
    sums_out[4:5, :] = jnp.sum(dy * normal_two, 0, keepdims=True)
    sums_out[5:6, :] = jnp.sum(dy, 0, keepdims=True)
    grad_two = normalise_back(dy * ffn_gain, normal_two, scale_two)
    grad_outer = grad_two.astype(LOW)
    outer_out[...] = grad_outer
    sums_out[3:4, :] = jnp.sum(grad_outer.astype(F32), 0, keepdims=True)
    grad_out[...] = grad_two


def rows_pass(where, x, near, near_got, far_got, cot, wa, vec, ib, wi, wo):
    rows, width = x.shape
    ff = ib.shape[1]
    hw = near.shape[2]
    low = lambda *s: jax.ShapeDtypeStruct(s, LOW)
    full = lambda *s: jax.ShapeDtypeStruct(s, F32)
    return pl.pallas_call(
        rows_kernel,
        in_specs=[SMEM] + [vmem()] * 8 + [HBM, HBM],
        out_specs=[vmem()] * 13,
        out_shape=[
            low(rows, width), low(2, hw, rows), low(2, hw, rows), low(rows, 2 * width), low(rows, 2 * width),
            full(4, rows, width), low(rows, width), full(rows, width), full(rows, width), full(rows, 1),
            full(8, width), low(width, ff), low(ff, width),
        ],
        scratch_shapes=[pltpu.VMEM((width, rows), F32), pltpu.SemaphoreType.DMA((8,))],
        compiler_params=pltpu.CompilerParams(vmem_limit_bytes=16 * MIB),
        cost_estimate=cost(7),
        name="rows_pass",
    )(where, x, near, near_got, far_got, cot, wa, vec, ib, far(wi), far(wo))


def rows_back_kernel(
    where, slope, outer, grad_two, normal, scale, sums, wa, gain, wi, wo,
    grad_one_out, inner_out, attn_out, near_out, across_out, sums_out,
):
    me = where[0]
    rows, width = outer.shape
    chunk = width
    hw = wa.shape[1]
    sums_out[...] = jnp.zeros_like(sums_out)
    sums_out[3:6, :] = sums[3:6, :]
    grad_outer = outer[...]
    grad_hidden = grad_two[...]
    for c in range(4):
        cols = slice(c * chunk, (c + 1) * chunk)
        grad_inner = (dot_nt(grad_outer, wo[cols, :]) * slope[me ^ c]).astype(LOW)
        inner_out[:, cols] = grad_inner
        column = jnp.sum(grad_inner.astype(F32), 0, keepdims=True)
        for i in range(4):
            sums_out[6 + i : 7 + i, c * hw : (c + 1) * hw] = column[:, i * hw : (i + 1) * hw]
        grad_hidden += dot_nt(grad_inner, wi[:, cols])
    normal_one = normal[...]
    sums_out[1:2, :] = jnp.sum(grad_hidden * normal_one, 0, keepdims=True)
    sums_out[2:3, :] = jnp.sum(grad_hidden, 0, keepdims=True)
    grad_one = normalise_back(grad_hidden * gain[1:2, :], normal_one, scale[...])
    grad_one_out[...] = grad_one
    grad_attn = grad_one.astype(LOW)
    attn_out[...] = grad_attn
    sums_out[0:1, :] = jnp.sum(grad_attn.astype(F32), 0, keepdims=True)
    for j in range(4):
        out = across_out if j > 1 else near_out
        out[j & 1] = dot_nt(grad_attn, wa[me ^ j]).astype(LOW)


def rows_back(where, slope, outer, grad_two, normal, scale, sums, wa, vec, wi, wo):
    rows, width = outer.shape
    ff = wi.shape[1]
    hw = wa.shape[1]
    low = lambda *s: jax.ShapeDtypeStruct(s, LOW)
    full = lambda *s: jax.ShapeDtypeStruct(s, F32)
    return pl.pallas_call(
        rows_back_kernel,
        in_specs=[SMEM] + [vmem()] * 10,
        out_specs=[vmem()] * 6,
        out_shape=[
            full(rows, width), low(rows, ff), low(rows, width), low(2, rows, hw), low(2, rows, hw), full(16, width),
        ],
        compiler_params=pltpu.CompilerParams(vmem_limit_bytes=12 * MIB),
        cost_estimate=cost(5),
        name="rows_back",
    )(where, slope, outer, grad_two, normal, scale, sums, wa, vec, wi, wo)


def outer_grad_kernel(active, active_got, grad, grad_got, send_out, keep_out):
    width = grad.shape[1]
    n = width // PIECES
    right = jnp.concatenate([grad[...], grad_got[...]], 0)
    for y, out in ((1, send_out), (0, keep_out)):
        cols = slice(y * width, (y + 1) * width)
        product = dot_tn(jnp.concatenate([active[:, cols], active_got[:, cols]], 0), right)
        for e in range(PIECES):
            out[0, e] = product[e * n : (e + 1) * n].astype(LOW)


def outer_grad(active, active_got, grad, grad_got):
    width = grad.shape[1]
    shape = (1, PIECES, width // PIECES, width)
    return pl.pallas_call(
        outer_grad_kernel,
        in_specs=[vmem()] * 4,
        out_specs=[vmem()] * 2,
        out_shape=[jax.ShapeDtypeStruct(shape, LOW)] * 2,
        compiler_params=pltpu.CompilerParams(vmem_limit_bytes=12 * MIB),
        cost_estimate=cost(3),
        name="outer_grad",
    )(active, active_got, grad, grad_got)


def inner_grad_kernel(
    place, hidden, hidden_got, inner, inner_got, near, far_got, context_got, attn, attn_got, send_out, keep_out, rest
):
    hw = hidden.shape[1]
    rows, width = attn.shape
    half = PIECES // 2
    n = hw // PIECES
    cols = inner.shape[1] // PIECES
    left = jnp.concatenate(
        [jnp.concatenate([hidden[y], hidden_got[y]], 1) for y in range(2)], 0
    )
    grads = jnp.concatenate([attn[...], attn_got[...]], 0)
    for y, mine in enumerate((near[0], far_got[0])):
        rest[y] = dot_tn(jnp.concatenate([mine, context_got[y]], 0), grads)
    me = place[0] & half
    for out, first in ((send_out, me ^ half), (keep_out, me)):
        for e in range(half):
            piece = first + e
            here = pl.ds(pl.multiple_of(piece * cols, 128), cols)
            product = dot(left, jnp.concatenate([inner[:, here], inner_got[:, here]], 0))
            for y in range(2):
                out[y, e, :hw, :] = product[y * hw : (y + 1) * hw].astype(LOW)
                more = rest[y, pl.ds(pl.multiple_of(piece * n, 8), n), :]
                more = jnp.concatenate([more[:, : width // 2], more[:, width // 2 :]], 0)
                out[y, e, hw:, :] = more.astype(LOW)


def inner_grad(place, hidden, hidden_got, inner, inner_got, near, far_got, context_got, attn, attn_got):
    hw = hidden.shape[1]
    width = attn.shape[1]
    shape = (2, PIECES // 2, hw + 2 * hw // PIECES, inner.shape[1] // PIECES)
    return pl.pallas_call(
        inner_grad_kernel,
        in_specs=[SMEM] + [vmem()] * 9,
        out_specs=[vmem()] * 2,
        out_shape=[jax.ShapeDtypeStruct(shape, LOW)] * 2,
        scratch_shapes=[pltpu.VMEM((2, hw, width), F32)],
        compiler_params=pltpu.CompilerParams(vmem_limit_bytes=12 * MIB),
        cost_estimate=cost(3),
        name="inner_grad",
    )(place, hidden, hidden_got, inner, inner_got, near, far_got, context_got, attn, attn_got)


ANYWHERE = pl.BlockSpec(memory_space=pl.ANY)


def sum_kernel(spec, place, *refs):
    leads, count, flip, inputs, splits = spec
    ins = refs[: len(inputs)]
    outs = refs[-splits:]
    first = (place[0] // count) * count
    if flip:
        first = first ^ count
    for y, lead in enumerate(leads):
        for r in range(count):
            total = None
            for ref in ins:
                pieces = ref.shape[1]
                base = first & (pieces - 1) if count < pieces else 0
                term = ref[lead if ref.shape[0] > 1 else 0, base + r].astype(F32)
                total = term if total is None else total + term
            if splits == 1:
                outs[0][y, r] = total.astype(LOW)
            else:
                n = total.shape[0] // splits
                for j in range(splits):
                    outs[j][...] = total[j * n : (j + 1) * n].astype(LOW)


def sum_pieces(place, inputs, leads, count, flip, after=(), splits=1, name="sum_pieces"):
    tall, wide = inputs[0].shape[2:]
    spec = (tuple(leads), count, flip, tuple(range(len(inputs))), splits)
    if splits == 1:
        out_shape = [jax.ShapeDtypeStruct((len(leads), count, tall, wide), LOW)]
    else:
        out_shape = [jax.ShapeDtypeStruct((tall // splits, wide), LOW)] * splits
    return pl.pallas_call(
        lambda *refs: sum_kernel(spec, *refs),
        in_specs=[SMEM] + [vmem()] * len(inputs) + [ANYWHERE] * len(after),
        out_specs=[vmem()] * splits,
        out_shape=out_shape,
        compiler_params=pltpu.CompilerParams(vmem_limit_bytes=4 * MIB),
        cost_estimate=cost(0.3 + 0.3 * len(leads) * count * len(inputs) / 4),
        name=name,
    )(place, *inputs, *after)


def outer_place_kernel(spots, place, own, got, *refs):
    out = refs[-1]
    n = own.shape[1]
    for i, spot in enumerate(spots):
        piece = own[i] if i < 4 else got[i - 4]
        out[pl.ds(pl.multiple_of((place[0] ^ spot) * n, 8), n), :] = piece.astype(F32)


def outer_place(spots, place, own, got, after=()):
    n, width = own.shape[1:]
    return pl.pallas_call(
        lambda *refs: outer_place_kernel(spots, *refs),
        in_specs=[SMEM, vmem(), vmem()] + [ANYWHERE] * len(after),
        out_specs=vmem(),
        out_shape=jax.ShapeDtypeStruct((PIECES * n, width), F32),
        compiler_params=pltpu.CompilerParams(vmem_limit_bytes=4 * MIB),
        cost_estimate=cost(2),
        name="outer_place",
    )(place, own, got, *after)


def inner_place_kernel(spots, place, own, got, *refs):
    inner, attn = refs[-2:]
    hw, cols = inner.shape[0], own.shape[2]
    n = attn.shape[0] // PIECES
    for i, spot in enumerate(spots):
        piece = (own[i] if i < 4 else got[i - 4]).astype(F32)
        here = place[0] ^ spot
        inner[:, pl.ds(pl.multiple_of(here * cols, 128), cols)] = piece[:hw]
        attn[pl.ds(pl.multiple_of(here * n, 8), n), :] = jnp.concatenate([piece[hw : hw + n], piece[hw + n :]], 1)


def inner_place(spots, place, own, got, hw, after=()):
    _, tall, cols = own.shape
    n = (tall - hw) // 2
    return pl.pallas_call(
        lambda *refs: inner_place_kernel(spots, *refs),
        in_specs=[SMEM, vmem(), vmem()] + [ANYWHERE] * len(after),
        out_specs=[vmem(), vmem()],
        out_shape=[
            jax.ShapeDtypeStruct((hw, PIECES * cols), F32),
            jax.ShapeDtypeStruct((PIECES * n, 2 * cols), F32),
        ],
        compiler_params=pltpu.CompilerParams(vmem_limit_bytes=4 * MIB),
        cost_estimate=cost(2),
        name="inner_place",
    )(place, own, got, *after)


def project_place_kernel(spots, place, own, got, *refs):
    out, vectors, tall = refs[-3:]
    n = own.shape[1] // 4
    hw = out.shape[1] // 12
    wide = 3 * hw
    for i, spot in enumerate(spots):
        ref, k = (own, i) if i < 4 else (got, i - 4)
        rows = pl.ds(pl.multiple_of((place[0] ^ spot) * n, 8), n)
        total = None
        for owner in range(4):
            start = pl.multiple_of((owner ^ place[1]) * n, 8)
            block = ref[k, pl.ds(start, n), :].astype(F32)
            for t in range(3):
                at = t * 4 * hw + owner * hw
                out[rows, at : at + hw] = block[:, t * hw : (t + 1) * hw]
            extra = block[:, wide:]
            total = extra if total is None else total + extra
        tall[rows, : total.shape[1]] = total
    vectors[...] = tall[...].T[: vectors.shape[0]]


def project_place(spots, place, own, got, hw, after=()):
    _, tall, wide = own.shape
    n = tall // 4
    return pl.pallas_call(
        lambda *refs: project_place_kernel(spots, *refs),
        in_specs=[SMEM, vmem(), vmem()] + [ANYWHERE] * len(after),
        out_specs=[vmem(), vmem()],
        out_shape=[
            jax.ShapeDtypeStruct((PIECES * n, 12 * hw), F32),
            jax.ShapeDtypeStruct((16, PIECES * n), F32),
        ],
        scratch_shapes=[pltpu.VMEM((PIECES * n, 128), F32)],
        compiler_params=pltpu.CompilerParams(vmem_limit_bytes=4 * MIB),
        cost_estimate=cost(2),
        name="project_place",
    )(place, own, got, *after)


def pair_kernel(near, far, *refs):
    out = refs[len(refs) // 2]
    out[0] = near[1]
    out[1] = far[1]


def pair(near, far, gated):
    return pl.pallas_call(
        pair_kernel,
        in_specs=[vmem(), vmem()] + [ANYWHERE] * len(gated),
        out_specs=[vmem()] + [ANYWHERE] * len(gated),
        out_shape=[jax.ShapeDtypeStruct(f.shape, f.dtype) for f in (near, *gated)],
        input_output_aliases={2 + i: 1 + i for i in range(len(gated))},
        compiler_params=pltpu.CompilerParams(vmem_limit_bytes=2 * MIB),
        cost_estimate=cost(0.5),
        name="pair",
    )(near, far, *gated)


def swap(field, axis, bit):
    count = lax.axis_size(axis)
    return lax.ppermute(field, axis, [(i, i ^ bit) for i in range(count)])


def add(left, right):
    return (left.astype(F32) + right.astype(F32)).astype(LOW)


class Reduction:
    def __init__(self, order, back, lane, me, rest):
        self.order = list(order)
        self.back = list(back)
        self.rest = rest
        bits = [o for o in order if o != "y"]
        weight = {bit: PIECES >> (k + 1) for k, bit in enumerate(bits)}
        spot = sum(jnp.where(lane & bit, w, 0) for bit, w in weight.items())
        self.spots = [sum(weight[bit] for t, bit in enumerate(back) if i >> t & 1) for i in range(PIECES)]
        self.place = jnp.stack([spot.astype(jnp.int32), me.astype(jnp.int32)])

    def begin(self, keep, send):
        axis = self.order.pop(0)
        got = swap(send, "seq", 2) if axis == "y" else swap(send, "dp", axis)
        self.arrays = [keep, got]
        self.left = keep.shape[1]
        self.folded = keep.shape[0] == 1

    def step(self, after=(), splits=1, name="sum"):
        leads = [0] if self.folded else [0, 1]
        if not self.order:
            return sum_pieces(self.place, self.arrays, [0], 1, False, after, splits, name)
        axis = self.order.pop(0)
        if axis == "y":
            (sent,) = sum_pieces(self.place, self.arrays, [1], self.left, False, after, name=name)
            self.folded = True
            got = swap(sent, "seq", 2)
        else:
            self.left //= 2
            (sent,) = sum_pieces(self.place, self.arrays, leads, self.left, True, after, name=name)
            got = swap(sent, "dp", axis)
        self.arrays = self.arrays + [got]
        return sent


def local(
    tokens, lengths, query_key_value, query_bias, value_bias, attn_weight, attn_bias, attn_gain,
    attn_shift, inner_weight, inner_bias, outer_weight, outer_bias, ffn_gain, ffn_shift, cotangent,
):
    groups = lax.axis_size("seq")
    lanes = lax.axis_size("dp")
    me = lax.axis_index("seq")
    lane = lax.axis_index("dp")
    passages, quarter, width = tokens.shape
    hw = H // groups * HD
    rows = passages * quarter
    ff = inner_bias.shape[0]
    rest = [1 << i for i in range(3, lanes.bit_length() - 1)]
    where = me.astype(jnp.int32).reshape(1)

    across = swap(tokens, "seq", 2)
    beside = swap(tokens, "seq", 1)
    corner = swap(across, "seq", 1)
    shards = (tokens, beside, across, corner)
    vec = jnp.stack([attn_bias, attn_gain, attn_shift, outer_bias, ffn_gain, ffn_shift, ffn_shift, ffn_shift])
    vec = vec.astype(F32)
    ib = inner_bias.astype(F32).reshape(1, ff)

    biases = (query_bias.reshape(1, width), value_bias.reshape(1, width))
    qkv, lse, w, near, across_heads = attend(where, lengths, shards, query_key_value, *biases)
    far_got = swap(across_heads, "seq", 2)
    (near_send,) = pair(near, far_got, [])
    near_got = swap(near_send, "seq", 1)
    context_got = swap(near_got, "seq", 1)
    flat = lambda f: f.reshape(2, rows, hw)
    context = [flat(f) for f in (near, near_got, far_got)]

    wa = attn_weight.reshape(groups, hw, width)
    (
        layer_out, hidden_own, hidden_send, active_own, active_send, slope, grad_outer, grad_two, normal, scale,
        row_sums, wi, wo,
    ) = rows_pass(
        where, tokens.reshape(rows, width), *context, cotangent.reshape(rows, width), wa, vec, ib, inner_weight,
        outer_weight,
    )
    active_got = swap(active_send, "seq", 1)
    outer_got = swap(grad_outer, "seq", 1)
    hidden_got = swap(hidden_send, "seq", 1)
    grad_one, grad_inner, grad_attn, near, across_heads, vectors = rows_back(
        where, slope, grad_outer, grad_two, normal, scale, row_sums, wa, vec, wi, wo
    )
    a = Reduction(["y", 1, 2, 4], [4, 2, 1], lane, me, rest)
    b = Reduction([2, "y", 1, 4], [4, 1, 2], lane, me, rest)
    d = Reduction([1, 2, 4], [4, 2, 1], lane, me, rest)
    far_got = swap(across_heads, "seq", 2)
    inner_got = swap(grad_inner, "seq", 1)
    attn_got = swap(grad_attn, "seq", 1)
    outer_send, outer_keep = outer_grad(active_own, active_got, grad_outer, outer_got)
    near_send, outer_send = pair(near, far_got, [outer_send])
    near_got = swap(near_send, "seq", 1)
    a.begin(outer_keep, outer_send)
    inner_send, inner_keep = inner_grad(
        b.place, hidden_own, hidden_got, grad_inner, inner_got, context[0], context[2], flat(context_got),
        grad_attn, attn_got,
    )
    b.begin(inner_keep, inner_send)
    grads_h = [f.reshape(2, passages, quarter, hw) for f in (near, near_got, far_got)]
    back_keep, back_send, project_send, project_keep = attend_back(
        d.place, lengths, shards, w, qkv, lse, grads_h, vectors, [inner_send]
    )
    d.begin(project_keep, project_send)
    back_got = swap(back_send, "seq", 1)
    (back_sum,) = sum_pieces(
        d.place,
        [f.reshape(2, 1, rows, width) for f in (back_keep, back_got)],
        [1], 1, False, name="back_y",
    )
    back_over = swap(back_sum, "seq", 2)
    t = a.step([back_sum], name="outer_x")
    t = d.step([t], name="project_z")
    t = b.step([t], name="inner_y")
    t = a.step([t], name="outer_z")
    t = d.step([t], name="project_zz")
    t = b.step([t], name="inner_x")
    t = a.step([t], name="outer_zz")
    project = d.step([t], splits=4, name="project_sum")
    t = b.step([project[0]], name="inner_zz")
    (outer_total,) = a.step([t], name="outer_sum")

    def finish(total):
        for bit in rest:
            total = add(total, swap(total, "dp", bit))
        return total

    def spread(piece, back):
        for bit in back[:-1]:
            piece = jnp.concatenate([piece, swap(piece, "dp", bit)], 0)
        return piece, swap(piece, "dp", back[-1])

    outer_total = spread(finish(outer_total)[0], a.back)
    project = [finish(p) for p in project]
    project = [project[0]] + [swap(project[j], "seq", j) for j in (1, 2, 3)]
    project_total = spread(jnp.concatenate(project, 0)[None], d.back)
    (inner_total,) = b.step(name="inner_sum")
    inner_total = spread(finish(inner_total)[0], b.back)

    grad_query_key_value, summed = project_place(d.spots, d.place, *project_total, hw)
    grad_outer_weight = outer_place(a.spots, a.place, *outer_total)
    grad_inner_weight, grad_attn_weight = inner_place(b.spots, b.place, *inner_total, hw)
    input_grad = (
        grad_one + back_keep[0].reshape(rows, width).astype(F32)
        + back_got[0].reshape(rows, width).astype(F32)
        + back_over[0, 0].astype(F32)
    ).astype(LOW)
    return (
        layer_out.reshape(passages, quarter, width),
        input_grad.reshape(passages, quarter, width),
        grad_query_key_value,
        summed[10],
        summed[11],
        grad_attn_weight,
        summed[0],
        summed[1],
        summed[2],
        grad_inner_weight,
        summed[6:10].reshape(-1),
        grad_outer_weight,
        summed[3],
        summed[4],
        summed[5],
    )


def solution(mesh):
    rows = P("dp", "seq", None)
    return jax.shard_map(
        local,
        mesh=mesh,
        in_specs=(rows, P("dp")) + (P(),) * 13 + (rows,),
        out_specs=(
            rows,
            rows,
            P("seq", None),
            P("seq"),
            P("seq"),
            P("seq", None),
            P("seq"),
            P("seq"),
            P("seq"),
            P("seq", None),
            P("seq"),
            P("seq", None),
            P("seq"),
            P("seq"),
            P("seq"),
        ),
        check_vma=False,
    )
```

```python
import jax
import jax.numpy as jnp
from jax import lax
from jax.experimental import pallas as pl
from jax.experimental.pallas import tpu as pltpu
from jax.sharding import PartitionSpec as P

H = 12
HD = 64
EPS = 1e-12
F32 = jnp.float32
LOW = jnp.bfloat16
MIB = 1 << 20
PIECES = 8
STEP = 5.0


def cost(us):
    return pl.CostEstimate(flops=int(us * 1.15e9), bytes_accessed=int(us * 3.69e6), transcendentals=0)


def dot(a, b):
    return lax.dot_general(a, b, (((1,), (0,)), ((), ())), preferred_element_type=F32)


def dot_nt(a, b):
    return lax.dot_general(a, b, (((1,), (1,)), ((), ())), preferred_element_type=F32)


def dot_tn(a, b):
    return lax.dot_general(a, b, (((0,), (0,)), ((), ())), preferred_element_type=F32)


def vmem(shape=None, index=None):
    if shape is None:
        return pl.BlockSpec(memory_space=pltpu.VMEM)
    return pl.BlockSpec(shape, index)


SMEM = pl.BlockSpec(memory_space=pltpu.SMEM)
HBM = pl.BlockSpec(memory_space=pltpu.HBM)


def far(array):
    return pltpu.with_memory_space_constraint(array, pltpu.HBM)


def key_mask(me, length, rows, quarter):
    slot = lax.broadcasted_iota(jnp.int32, (rows, 1), 0)
    block = slot // quarter
    return ((block ^ me) * quarter + (slot - block * quarter)) < length


def attend_kernel(where, lengths, x0, x1, x2, x3, w_hbm, qb, vb, qkv_out, lse_out, w, *refs):
    near_out, across_out, own_out, wide, sem = refs
    p = pl.program_id(0)
    me = where[0]
    quarter, width = x0.shape[1:]
    rows = 4 * quarter
    hw = w.shape[1] // 3
    window = wide.shape[2]
    odd = (me & 1) == 1
    first = pl.multiple_of(me * hw - (me & 1) * HD, 128)
    choose = lambda f: jnp.where(odd, f[:, HD : HD + hw], f[:, :hw])

    @pl.when(p == 0)
    def _():
        copies = [
            pltpu.make_async_copy(
                w_hbm.at[:, pl.ds(pl.multiple_of(t * width + first, 128), window)], wide.at[t], sem.at[t]
            )
            for t in range(3)
        ]
        for copy in copies:
            copy.start()
        for t, copy in enumerate(copies):
            copy.wait()
            w[:, t * hw : (t + 1) * hw] = choose(wide[t])

    heads = hw // HD
    x = jnp.concatenate([x0[0], x1[0], x2[0], x3[0]], 0)
    proj = dot(x, w[...])
    here = pl.ds(first, window)
    q = ((proj[:, :hw] + choose(qb[:, here].astype(F32))).astype(LOW).astype(F32) * HD ** (-0.5)).astype(LOW)
    k = proj[:, hw : 2 * hw].astype(LOW)
    v = (proj[:, 2 * hw :] + choose(vb[:, here].astype(F32))).astype(LOW)
    qkv_out[0] = jnp.concatenate([q, k, v], 1)
    usable = key_mask(me, lengths[p], rows, quarter)
    parts = []
    for h in range(heads):
        cols = slice(h * HD, (h + 1) * HD)
        logits = jnp.where(usable, dot_nt(k[:, cols], q[:, cols]), -1e9)
        highest = jnp.max(logits, 0, keepdims=True)
        weight = jnp.exp(logits - highest)
        total = jnp.sum(weight, 0, keepdims=True)
        lse_out[0, h : h + 1, :] = highest + jnp.log(total)
        parts.append(dot_tn(v[:, cols], weight.astype(LOW)) * (1.0 / total))
    context = jnp.concatenate(parts, 0).T.astype(LOW)
    for j in range(4):
        out = across_out if j > 1 else near_out
        out[j & 1, 0] = context[j * quarter : (j + 1) * quarter]
    own_out[0] = context[:quarter]


def attend(where, lengths, shards, w, qb, vb):
    passages, quarter, width = shards[0].shape
    rows = 4 * quarter
    hw = width // 4
    window = hw + HD
    heads = hw // HD
    block = vmem((1, quarter, width), lambda p: (p, 0, 0))
    whole = lambda *shape: vmem(shape, lambda p: (0,) * len(shape))
    return pl.pallas_call(
        attend_kernel,
        grid=(passages,),
        in_specs=[SMEM, SMEM] + [block] * 4 + [HBM, whole(1, width), whole(1, width)],
        out_specs=[
            vmem((1, rows, 3 * hw), lambda p: (p, 0, 0)),
            vmem((1, heads, rows), lambda p: (p, 0, 0)),
            whole(width, 3 * hw),
        ]
        + [vmem((2, 1, quarter, hw), lambda p: (0, p, 0, 0))] * 2
        + [vmem((1, quarter, hw), lambda p: (p, 0, 0))],
        out_shape=[
            pltpu.HBM((passages, rows, 3 * hw), LOW),
            pltpu.HBM((passages, heads, rows), F32),
            pltpu.HBM((width, 3 * hw), LOW),
        ]
        + [jax.ShapeDtypeStruct((2, passages, quarter, hw), LOW)] * 2
        + [pltpu.HBM((passages, quarter, hw), LOW)],
        scratch_shapes=[pltpu.VMEM((3, width, window), LOW), pltpu.SemaphoreType.DMA((3,))],
        compiler_params=pltpu.CompilerParams(vmem_limit_bytes=16 * MIB),
        cost_estimate=cost(5.5),
        name="attend",
    )(where, lengths, *map(far, shards), far(w), qb, vb)


def attend_back_kernel(
    place, lengths, x0, x1, x2, x3, w, qkv, lse, near, near_got, far_got, vectors, *refs
):
    keep_out, send_out, weight_send, weight_keep, acc, bias = refs[-6:]
    p = pl.program_id(0)
    me = place[1]
    quarter = x0.shape[1]
    rows = 4 * quarter
    hw = w.shape[1] // 3
    heads = hw // HD
    scale = HD ** (-0.5)
    x = jnp.concatenate([x0[0], x1[0], x2[0], x3[0]], 0)
    g = jnp.concatenate([near[0, 0], near_got[0, 0], far_got[0, 0], near_got[1, 0]], 0)
    usable = key_mask(me, lengths[p], rows, quarter)
    q = qkv[0, :, :hw]
    k = qkv[0, :, hw : 2 * hw]
    v = qkv[0, :, 2 * hw :]
    grad_q, grad_k, grad_v = [], [], []
    for h in range(heads):
        cols = slice(h * HD, (h + 1) * HD)
        qh, kh, vh, gh = q[:, cols], k[:, cols], v[:, cols], g[:, cols]
        logits = jnp.where(usable, dot_nt(kh, qh), -1e9)
        chance = jnp.exp(logits - lse[0, h : h + 1, :])
        grad_chance = dot_nt(vh, gh)
        inner = jnp.sum(grad_chance * chance, 0, keepdims=True)
        grad_logits = (chance * (grad_chance - inner)).astype(LOW)
        grad_q.append(dot_tn(kh, grad_logits) * scale)
        grad_k.append(dot(grad_logits, qh))
        grad_v.append(dot(chance.astype(LOW), gh))
    gq = jnp.concatenate(grad_q, 0).T.astype(LOW)
    gk = jnp.concatenate(grad_k, 1).astype(LOW)
    gv = jnp.concatenate(grad_v, 1).astype(LOW)
    joined = jnp.concatenate([gq, gk, gv], 1)
    part = dot_tn(x, joined)
    sums = [jnp.sum(f.astype(F32), 0, keepdims=True) for f in (gq, gv)]
    wide = 3 * hw

    @pl.when(p == 0)
    def _():
        acc[:, :wide] = part
        bias[...] = jnp.zeros_like(bias)

    @pl.when(p > 0)
    def _():
        acc[:, :wide] += part

    here = pl.ds(pl.multiple_of(me * 256, 128), hw)
    for i in range(2):
        bias[i : i + 1, here] += sums[i]

    back = dot_nt(joined, w[...]).astype(LOW)
    for j in range(4):
        out = send_out if j % 2 else keep_out
        out[j // 2, 0] = back[j * quarter : (j + 1) * quarter]

    @pl.when(p == pl.num_programs(0) - 1)
    def _():
        n = weight_send.shape[2] // 4
        rows_of = jnp.concatenate([bias[:, i * 256 : i * 256 + hw] for i in range(4)], 1)
        extra = jnp.concatenate([vectors[:10, :], rows_of[:2, :], jnp.zeros((52, vectors.shape[1]), F32)], 0)
        acc[:, wide:] = extra.T
        half = PIECES // 2
        spot = place[0] & half
        for out, first in ((weight_send, spot ^ half), (weight_keep, spot)):
            for j in range(4):
                for e in range(half):
                    start = pl.multiple_of((me ^ j) * (n * PIECES) + (first + e) * n, 8)
                    out[0, e, j * n : (j + 1) * n, :] = acc[pl.ds(start, n), :].astype(LOW)


def attend_back(place, lengths, shards, w, qkv, lse, grads, vectors, after=()):
    passages, quarter, width = shards[0].shape
    rows = 4 * quarter
    hw = w.shape[1] // 3
    heads = hw // HD
    n = width // (4 * PIECES)
    block = vmem((1, quarter, width), lambda p: (p, 0, 0))
    gblock = vmem((2, 1, quarter, hw), lambda p: (0, p, 0, 0))
    whole = lambda *shape: vmem(shape, lambda p: (0,) * len(shape))
    return pl.pallas_call(
        attend_back_kernel,
        grid=(passages,),
        in_specs=[SMEM, SMEM]
        + [block] * 4
        + [
            whole(width, 3 * hw),
            vmem((1, rows, 3 * hw), lambda p: (p, 0, 0)),
            vmem((1, heads, rows), lambda p: (p, 0, 0)),
        ]
        + [gblock] * 3
        + [whole(*vectors.shape)]
        + [ANYWHERE] * len(after),
        out_specs=[
            vmem((2, 1, quarter, width), lambda p: (0, p, 0, 0)),
            vmem((2, 1, quarter, width), lambda p: (0, p, 0, 0)),
            whole(1, PIECES // 2, 4 * n, 3 * hw + 64),
            whole(1, PIECES // 2, 4 * n, 3 * hw + 64),
        ],
        out_shape=[
            jax.ShapeDtypeStruct((2, passages, quarter, width), LOW),
            jax.ShapeDtypeStruct((2, passages, quarter, width), LOW),
            jax.ShapeDtypeStruct((1, PIECES // 2, 4 * n, 3 * hw + 64), LOW),
            jax.ShapeDtypeStruct((1, PIECES // 2, 4 * n, 3 * hw + 64), LOW),
        ],
        scratch_shapes=[pltpu.VMEM((width, 3 * hw + 64), F32), pltpu.VMEM((8, 1024), F32)],
        compiler_params=pltpu.CompilerParams(vmem_limit_bytes=24 * MIB),
        cost_estimate=cost(11),
        name="attend_back",
    )(place, lengths, *map(far, shards), far(w), far(qkv), far(lse), *map(far, grads), far(vectors), *after)


def normalise(field):
    centre = field - jnp.mean(field, -1, keepdims=True)
    scale = lax.rsqrt(jnp.mean(centre * centre, -1, keepdims=True) + EPS)
    return centre * scale, scale


def normalise_back(grad, normal, scale):
    return (
        grad
        - jnp.mean(grad, -1, keepdims=True)
        - normal * jnp.mean(grad * normal, -1, keepdims=True)
    ) * scale


def rows_kernel(
    where, x, near_hbm, near_got_hbm, far_got_hbm, cot, wa, vec, ib, wi_hbm, wo_hbm,
    layer_out, hidden_own, hidden_send, active_own, active_send, slope, outer_out, grad_out, normal_out, scale_out,
    sums_out, wi, wo, parts, hidden_here, active_here, flipped, sem,
):
    me = where[0]
    width = x.shape[1]
    chunk = width
    hw = parts.shape[2]
    loads = [
        pltpu.make_async_copy(f, parts.at[pl.ds(first, count)], sem.at[i])
        for i, (f, first, count) in enumerate(
            ((near_hbm.at[pl.ds(0, 1)], 0, 1), (near_got_hbm, 1, 2), (far_got_hbm.at[pl.ds(0, 1)], 3, 1))
        )
    ]
    order = (0, 2, 1, 3)
    weights = []
    for k, c in enumerate(order):
        cols = pl.ds(pl.multiple_of((me ^ c) * chunk, 128), chunk)
        weights.append(pltpu.make_async_copy(wi_hbm.at[:, cols], wi.at[:, cols], sem.at[5 + 2 * k]))
        weights.append(pltpu.make_async_copy(wo_hbm.at[cols, :], wo.at[cols, :], sem.at[6 + 2 * k]))
    for copy in loads + weights[:2]:
        copy.start()
    stores = [
        pltpu.make_async_copy(hidden_here, hidden_own, sem.at[3]),
        pltpu.make_async_copy(active_here, active_own, sem.at[4]),
    ]
    row = lambda r: vec[r : r + 1, :]
    attn_bias, attn_gain, attn_shift, outer_bias, ffn_gain, ffn_shift = (row(r) for r in range(6))
    attended = attn_bias + x[...].astype(F32)
    for copy in loads:
        copy.wait()
    weights[2].start()
    weights[3].start()
    for j, k in enumerate((0, 1, 3, 2)):
        attended += dot(parts[k], wa[me ^ j])
    normal_one, scale_one = normalise(attended)
    normal_out[...] = normal_one
    scale_out[...] = scale_one
    hidden = normal_one * attn_gain + attn_shift
    hidden_low = hidden.astype(LOW)
    flipped[...] = hidden.T
    for j in range(4):
        start = pl.multiple_of((me ^ j) * hw, 64)
        here = hidden_send if j & 1 else hidden_here
        here[j >> 1] = flipped[pl.ds(start, hw), :].astype(LOW)
    stores[0].start()
    pre_two = hidden + outer_bias
    for k, c in enumerate(order):
        cols = pl.ds(pl.multiple_of((me ^ c) * chunk, 128), chunk)
        for copy in weights[2 * k + 4 : 2 * k + 6]:
            copy.start()
        weights[2 * k].wait()
        u = dot(hidden_low, wi[:, cols]) + ib[:, cols]
        below = 0.5 * (1.0 + lax.erf(u * (0.5**0.5)))
        density = jnp.exp(-0.5 * u * u) * 0.3989422804014327
        active = (u * below).astype(LOW)
        slope[c] = below + u * density
        here = active_send if c & 1 else active_here
        here[:, (c >> 1) * chunk : ((c >> 1) + 1) * chunk] = active
        weights[2 * k + 1].wait()
        pre_two += dot(active, wo[cols, :])
        if c == 2:
            stores[1].start()
    normal_two, scale_two = normalise(pre_two)
    layer_out[...] = (normal_two * ffn_gain + ffn_shift).astype(LOW)
    dy = cot[...].astype(F32)
    sums_out[...] = jnp.zeros_like(sums_out)
    sums_out[4:5, :] = jnp.sum(dy * normal_two, 0, keepdims=True)
    sums_out[5:6, :] = jnp.sum(dy, 0, keepdims=True)
    grad_two = normalise_back(dy * ffn_gain, normal_two, scale_two)
    grad_outer = grad_two.astype(LOW)
    outer_out[...] = grad_outer
    sums_out[3:4, :] = jnp.sum(grad_outer.astype(F32), 0, keepdims=True)
    grad_out[...] = grad_two
    for copy in stores:
        copy.wait()


def rows_pass(where, x, near, near_got, far_got, cot, wa, vec, ib, wi, wo):
    rows, width = x.shape
    ff = ib.shape[1]
    hw = near.shape[2]
    low = lambda *s: jax.ShapeDtypeStruct(s, LOW)
    full = lambda *s: jax.ShapeDtypeStruct(s, F32)
    return pl.pallas_call(
        rows_kernel,
        in_specs=[SMEM, vmem(), HBM, HBM, HBM] + [vmem()] * 4 + [HBM, HBM],
        out_specs=[vmem(), HBM, vmem(), HBM] + [vmem()] * 9,
        out_shape=[
            low(rows, width), pltpu.HBM((2, hw, rows), LOW), low(2, hw, rows),
            pltpu.HBM((rows, 2 * width), LOW), low(rows, 2 * width),
            full(4, rows, width), low(rows, width), full(rows, width), full(rows, width), full(rows, 1),
            full(8, width), low(width, ff), low(ff, width),
        ],
        scratch_shapes=[
            pltpu.VMEM((4, rows, hw), LOW),
            pltpu.VMEM((2, hw, rows), LOW),
            pltpu.VMEM((rows, 2 * width), LOW),
            pltpu.VMEM((width, rows), F32),
            pltpu.SemaphoreType.DMA((13,)),
        ],
        compiler_params=pltpu.CompilerParams(vmem_limit_bytes=14 * MIB),
        cost_estimate=cost(6),
        name="rows_pass",
    )(where, x, far(near), far(near_got), far(far_got), cot, wa, vec, ib, far(wi), far(wo))


def rows_back_kernel(
    where, slope, outer, grad_two, normal, scale, sums, wa, gain, wi, wo,
    grad_one_out, inner_out, attn_out, near_out, across_out, sums_out,
    grad_one_here, inner_here, attn_here, near_here, sums_here, sem,
):
    me = where[0]
    rows, width = outer.shape
    chunk = width
    hw = wa.shape[1]
    pairs = ((grad_one_here, grad_one_out), (attn_here, attn_out), (near_here, near_out), (sums_here, sums_out))
    stores = [pltpu.make_async_copy(here, out, sem.at[4 + i]) for i, (here, out) in enumerate(pairs)]
    sums_here[...] = jnp.zeros_like(sums_here)
    sums_here[3:6, :] = sums[3:6, :]
    grad_outer = outer[...]
    grad_hidden = grad_two[...]
    moved = []
    for c in range(4):
        cols = slice(c * chunk, (c + 1) * chunk)
        grad_inner = (dot_nt(grad_outer, wo[cols, :]) * slope[me ^ c]).astype(LOW)
        inner_here[:, cols] = grad_inner
        some = pl.ds(c * chunk, chunk)
        moved.append(pltpu.make_async_copy(inner_here.at[:, some], inner_out.at[:, some], sem.at[c]))
        moved[c].start()
        column = jnp.sum(grad_inner.astype(F32), 0, keepdims=True)
        for i in range(4):
            sums_here[6 + i : 7 + i, c * hw : (c + 1) * hw] = column[:, i * hw : (i + 1) * hw]
        grad_hidden += dot_nt(grad_inner, wi[:, cols])
    normal_one = normal[...]
    sums_here[1:2, :] = jnp.sum(grad_hidden * normal_one, 0, keepdims=True)
    sums_here[2:3, :] = jnp.sum(grad_hidden, 0, keepdims=True)
    grad_one = normalise_back(grad_hidden * gain[1:2, :], normal_one, scale[...])
    grad_one_here[...] = grad_one
    stores[0].start()
    grad_attn = grad_one.astype(LOW)
    attn_here[...] = grad_attn
    stores[1].start()
    sums_here[0:1, :] = jnp.sum(grad_attn.astype(F32), 0, keepdims=True)
    stores[3].start()
    for j in range(2):
        near_here[j] = dot_nt(grad_attn, wa[me ^ j]).astype(LOW)
    stores[2].start()
    for j in range(2):
        across_out[j] = dot_nt(grad_attn, wa[me ^ (j + 2)]).astype(LOW)
    for copy in moved + stores:
        copy.wait()


def rows_back(where, slope, outer, grad_two, normal, scale, sums, wa, vec, wi, wo):
    rows, width = outer.shape
    ff = wi.shape[1]
    hw = wa.shape[1]
    kinds = [((rows, width), F32), ((rows, ff), LOW), ((rows, width), LOW), ((2, rows, hw), LOW), ((16, width), F32)]
    outs = [pltpu.HBM(*kind) for kind in kinds]
    return pl.pallas_call(
        rows_back_kernel,
        in_specs=[SMEM] + [vmem()] * 10,
        out_specs=[HBM] * 4 + [vmem(), HBM],
        out_shape=outs[:4] + [jax.ShapeDtypeStruct((2, rows, hw), LOW)] + outs[4:],
        scratch_shapes=[pltpu.VMEM(*kind) for kind in kinds] + [pltpu.SemaphoreType.DMA((8,))],
        compiler_params=pltpu.CompilerParams(vmem_limit_bytes=14 * MIB),
        cost_estimate=cost(5),
        name="rows_back",
    )(where, slope, outer, grad_two, normal, scale, sums, wa, vec, wi, wo)


def outer_grad_kernel(place, active, active_got, grad, grad_got, send_out, keep_out):
    half = PIECES // 2
    n = grad.shape[1] // PIECES
    right = jnp.concatenate([grad[...], grad_got[...]], 0)
    product = dot_tn(jnp.concatenate([active[...], active_got[...]], 0), right)

    def store(low_out, high_out):
        for e in range(PIECES):
            out = high_out if e >= half else low_out
            out[0, e % half] = product[e * n : (e + 1) * n].astype(LOW)

    high = (place[0] & half) > 0
    pl.when(high)(lambda: store(send_out, keep_out))
    pl.when(jnp.logical_not(high))(lambda: store(keep_out, send_out))


def outer_grad(place, active, active_got, grad, grad_got):
    rows, width = grad.shape
    block = (1, PIECES // 2, width // PIECES, width)
    side = vmem((rows, width), lambda y: (0, y))
    whole = lambda *s: vmem(s, lambda y: (0,) * len(s))
    return pl.pallas_call(
        outer_grad_kernel,
        grid=(2,),
        in_specs=[SMEM, side, side, whole(rows, width), whole(rows, width)],
        out_specs=[vmem(block, lambda y: (y, 0, 0, 0))] * 2,
        out_shape=[jax.ShapeDtypeStruct((2,) + block[1:], LOW)] * 2,
        compiler_params=pltpu.CompilerParams(vmem_limit_bytes=16 * MIB),
        cost_estimate=cost(6),
        name="outer_grad",
    )(place, far(active), far(active_got), far(grad), far(grad_got))


SPLIT = 128


def inner_grad_kernel(
    place, hidden, hidden_got, inner, inner_got, near, far_got, context_got, attn, attn_got, *refs
):
    first_send, first_keep, second_send, second_keep, left, rest = refs[-6:]
    step = pl.program_id(0)
    hw = hidden.shape[1]
    rows, width = attn.shape
    half = PIECES // 2
    n = hw // PIECES
    cols = inner.shape[1] // 2

    @pl.when(step == 0)
    def _():
        grads = jnp.concatenate([attn[...], attn_got[...]], 0)
        for y, mine in enumerate((near, far_got)):
            left[y * hw : (y + 1) * hw, :rows] = hidden[y]
            left[y * hw : (y + 1) * hw, rows:] = hidden_got[y]
            rest[y] = dot_tn(jnp.concatenate([mine[0], context_got[y]], 0), grads)

    product = dot(left[...], jnp.concatenate([inner[...], inner_got[...]], 0))

    def store_first(out):
        for k in range(2):
            for y in range(2):
                piece = product[y * hw : y * hw + SPLIT, k * cols : (k + 1) * cols]
                out[y, 2 * (step & 1) + k] = piece.astype(LOW)

    mine = (place[0] & half) == (step >> 1) * half
    pl.when(mine)(lambda: store_first(first_keep))
    pl.when(jnp.logical_not(mine))(lambda: store_first(first_send))
    for k in range(2):
        for y, out in enumerate((second_keep, second_send)):
            piece = 2 * step + k
            some = product[y * hw + SPLIT : (y + 1) * hw, k * cols : (k + 1) * cols]
            more = rest[y, pl.ds(pl.multiple_of(piece * n, 8), n), :]
            some = jnp.concatenate([some, more[:, : width // 2], more[:, width // 2 :]], 0)
            out[0, piece] = some.astype(LOW)


def inner_grad(place, hidden, hidden_got, inner, inner_got, near, far_got, context_got, attn, attn_got, after):
    hw = hidden.shape[1]
    rows, width = attn.shape
    half = PIECES // 2
    cols = inner.shape[1] // PIECES
    first = (2, half, SPLIT, cols)
    second = (1, PIECES, hw - SPLIT + 2 * hw // PIECES, cols)
    whole = lambda *s: vmem(s, lambda t: (0,) * len(s))
    side = vmem((rows, 2 * cols), lambda t: (0, t))
    one = vmem((1, rows, hw), lambda t: (0, 0, 0))
    return pl.pallas_call(
        inner_grad_kernel,
        grid=(half,),
        in_specs=[SMEM, whole(2, hw, rows), whole(2, hw, rows), side, side, one, one, whole(2, rows, hw)]
        + [whole(rows, width)] * 2
        + [ANYWHERE] * len(after),
        out_specs=[whole(*first)] * 2 + [whole(*second)] * 2,
        out_shape=[jax.ShapeDtypeStruct(s, LOW) for s in (first, first, second, second)],
        scratch_shapes=[pltpu.VMEM((2 * hw, 2 * rows), LOW), pltpu.VMEM((2, hw, width), F32)],
        compiler_params=pltpu.CompilerParams(vmem_limit_bytes=20 * MIB),
        cost_estimate=cost(4),
        name="inner_grad",
    )(place, *map(far, (hidden, hidden_got, inner, inner_got, near, far_got, context_got, attn, attn_got)), *after)


ANYWHERE = pl.BlockSpec(memory_space=pl.ANY)


def sum_kernel(spec, place, *refs):
    leads, count, flip, inputs, splits = spec
    ins = refs[: len(inputs)]
    outs = refs[-splits:]
    first = (place[0] // count) * count
    if flip:
        first = first ^ count
    for y, lead in enumerate(leads):
        for r in range(count):
            total = None
            for ref in ins:
                pieces = ref.shape[1]
                base = first & (pieces - 1) if count < pieces else 0
                term = ref[lead if ref.shape[0] > 1 else 0, base + r].astype(F32)
                total = term if total is None else total + term
            if splits == 1:
                outs[0][y, r] = total.astype(LOW)
            else:
                n = total.shape[0] // splits
                for j in range(splits):
                    outs[j][...] = total[j * n : (j + 1) * n].astype(LOW)


def sum_pieces(place, inputs, leads, count, flip, after=(), splits=1, name="sum_pieces"):
    tall, wide = inputs[0].shape[2:]
    spec = (tuple(leads), count, flip, tuple(range(len(inputs))), splits)
    if splits == 1:
        out_shape = [jax.ShapeDtypeStruct((len(leads), count, tall, wide), LOW)]
    else:
        out_shape = [jax.ShapeDtypeStruct((tall // splits, wide), LOW)] * splits
    return pl.pallas_call(
        lambda *refs: sum_kernel(spec, *refs),
        in_specs=[SMEM] + [vmem()] * len(inputs) + [ANYWHERE] * len(after),
        out_specs=[vmem()] * splits,
        out_shape=out_shape,
        compiler_params=pltpu.CompilerParams(vmem_limit_bytes=4 * MIB),
        cost_estimate=cost(STEP),
        name=name,
    )(place, *inputs, *after)


def outer_place_kernel(spots, place, own, got, *refs):
    out = refs[-1]
    n = own.shape[1]
    for i, spot in enumerate(spots):
        piece = own[i] if i < 4 else got[i - 4]
        out[pl.ds(pl.multiple_of((place[0] ^ spot) * n, 8), n), :] = piece.astype(F32)


def outer_place(spots, place, own, got, after=()):
    n, width = own.shape[1:]
    return pl.pallas_call(
        lambda *refs: outer_place_kernel(spots, *refs),
        in_specs=[SMEM, vmem(), vmem()] + [ANYWHERE] * len(after),
        out_specs=vmem(),
        out_shape=jax.ShapeDtypeStruct((PIECES * n, width), F32),
        compiler_params=pltpu.CompilerParams(vmem_limit_bytes=4 * MIB),
        cost_estimate=cost(2),
        name="outer_place",
    )(place, own, got, *after)


def inner_place_kernel(spots_one, spots_two, one, two, own, got, own_two, got_two, *refs):
    inner, attn = refs[-2:]
    hw, cols = inner.shape[0], own.shape[2]
    n = attn.shape[0] // PIECES
    for i in range(PIECES):
        piece = (own[i] if i < 4 else got[i - 4]).astype(F32)
        here = one[0] ^ spots_one[i]
        inner[:SPLIT, pl.ds(pl.multiple_of(here * cols, 128), cols)] = piece
        piece = (own_two[i] if i < 4 else got_two[i - 4]).astype(F32)
        here = two[0] ^ spots_two[i]
        some = hw - SPLIT
        inner[SPLIT:, pl.ds(pl.multiple_of(here * cols, 128), cols)] = piece[:some]
        more = jnp.concatenate([piece[some : some + n], piece[some + n :]], 1)
        attn[pl.ds(pl.multiple_of(here * n, 8), n), :] = more


def inner_place(spots_one, spots_two, one, two, parts_one, parts_two, hw, after=()):
    cols = parts_one[0].shape[2]
    n = hw // PIECES
    return pl.pallas_call(
        lambda *refs: inner_place_kernel(spots_one, spots_two, *refs),
        in_specs=[SMEM, SMEM] + [vmem()] * 4 + [ANYWHERE] * len(after),
        out_specs=[vmem(), vmem()],
        out_shape=[
            jax.ShapeDtypeStruct((hw, PIECES * cols), F32),
            jax.ShapeDtypeStruct((PIECES * n, 2 * cols), F32),
        ],
        compiler_params=pltpu.CompilerParams(vmem_limit_bytes=4 * MIB),
        cost_estimate=cost(2),
        name="inner_place",
    )(one, two, *parts_one, *parts_two, *after)


def project_place_kernel(spots, place, own, got, *refs):
    out, vectors, tall = refs[-3:]
    n = own.shape[1] // 4
    hw = out.shape[1] // 12
    wide = 3 * hw
    for i, spot in enumerate(spots):
        ref, k = (own, i) if i < 4 else (got, i - 4)
        rows = pl.ds(pl.multiple_of((place[0] ^ spot) * n, 8), n)
        total = None
        for owner in range(4):
            start = pl.multiple_of((owner ^ place[1]) * n, 8)
            block = ref[k, pl.ds(start, n), :].astype(F32)
            for t in range(3):
                at = t * 4 * hw + owner * hw
                out[rows, at : at + hw] = block[:, t * hw : (t + 1) * hw]
            extra = block[:, wide:]
            total = extra if total is None else total + extra
        tall[rows, : total.shape[1]] = total
    vectors[...] = tall[...].T[: vectors.shape[0]]


def project_place(spots, place, own, got, hw, after=()):
    _, tall, wide = own.shape
    n = tall // 4
    return pl.pallas_call(
        lambda *refs: project_place_kernel(spots, *refs),
        in_specs=[SMEM, vmem(), vmem()] + [ANYWHERE] * len(after),
        out_specs=[vmem(), vmem()],
        out_shape=[
            jax.ShapeDtypeStruct((PIECES * n, 12 * hw), F32),
            jax.ShapeDtypeStruct((16, PIECES * n), F32),
        ],
        scratch_shapes=[pltpu.VMEM((PIECES * n, 128), F32)],
        compiler_params=pltpu.CompilerParams(vmem_limit_bytes=4 * MIB),
        cost_estimate=cost(2),
        name="project_place",
    )(place, own, got, *after)


def join_kernel(*refs):
    out, sem = refs[-2:]
    own, got = refs[:2]
    n = own.shape[0]
    copies = [pltpu.make_async_copy(f, out.at[pl.ds(i * n, n)], sem.at[i]) for i, f in enumerate((own, got))]
    for copy in copies:
        copy.start()
    for copy in copies:
        copy.wait()


def join(own, got, after):
    shape = (2 * own.shape[0],) + own.shape[1:]
    return pl.pallas_call(
        join_kernel,
        in_specs=[ANYWHERE] * (2 + len(after)),
        out_specs=ANYWHERE,
        out_shape=jax.ShapeDtypeStruct(shape, own.dtype),
        scratch_shapes=[pltpu.SemaphoreType.DMA((2,))],
        compiler_params=pltpu.CompilerParams(vmem_limit_bytes=2 * MIB),
        cost_estimate=cost(STEP),
        name="join",
    )(own, got, *after)


def pair_kernel(gates, near, far, *refs):
    out, sem = refs[-1 - gates - 1], refs[-1]
    copies = [pltpu.make_async_copy(f.at[1], out.at[i], sem.at[i]) for i, f in enumerate((near, far))]
    for copy in copies:
        copy.start()
    for copy in copies:
        copy.wait()


def pair(near, far, gated, after=()):
    return pl.pallas_call(
        lambda *refs: pair_kernel(len(gated), *refs),
        in_specs=[ANYWHERE] * (2 + len(gated) + len(after)),
        out_specs=[ANYWHERE] * (1 + len(gated)),
        out_shape=[jax.ShapeDtypeStruct(f.shape, f.dtype) for f in (near, *gated)],
        input_output_aliases={2 + i: 1 + i for i in range(len(gated))},
        scratch_shapes=[pltpu.SemaphoreType.DMA((2,))],
        compiler_params=pltpu.CompilerParams(vmem_limit_bytes=2 * MIB),
        cost_estimate=cost(0.5),
        name="pair",
    )(near, far, *gated, *after)


def swap(field, axis, bit):
    count = lax.axis_size(axis)
    return lax.ppermute(field, axis, [(i, i ^ bit) for i in range(count)])


def add(left, right):
    return (left.astype(F32) + right.astype(F32)).astype(LOW)


class Reduction:
    def __init__(self, order, back, lane, me, rest):
        self.order = list(order)
        self.back = list(back)
        self.rest = rest
        bits = [o for o in order if o != "y"]
        weight = {bit: PIECES >> (k + 1) for k, bit in enumerate(bits)}
        spot = sum(jnp.where(lane & bit, w, 0) for bit, w in weight.items())
        self.spots = [sum(weight[bit] for t, bit in enumerate(back) if i >> t & 1) for i in range(PIECES)]
        self.place = jnp.stack([spot.astype(jnp.int32), me.astype(jnp.int32)])

    def begin(self, keep, send):
        axis = self.order.pop(0)
        got = swap(send, "seq", 2) if axis == "y" else swap(send, "dp", axis)
        self.arrays = [keep, got]
        self.left = keep.shape[1]
        self.folded = keep.shape[0] == 1

    def step(self, after=(), splits=1, name="sum"):
        leads = [0] if self.folded else [0, 1]
        if not self.order:
            return sum_pieces(self.place, self.arrays, [0], 1, False, after, splits, name)
        axis = self.order.pop(0)
        if axis == "y":
            (sent,) = sum_pieces(self.place, self.arrays, [1], self.left, False, after, name=name)
            self.folded = True
            got = swap(sent, "seq", 2)
        else:
            self.left //= 2
            (sent,) = sum_pieces(self.place, self.arrays, leads, self.left, True, after, name=name)
            got = swap(sent, "dp", axis)
        self.arrays = self.arrays + [got]
        return sent

    def start(self, piece):
        for bit in self.rest:
            piece = add(piece, swap(piece, "dp", bit))
        self.own = piece
        self.got = swap(piece, "dp", self.back[0])
        self.done = 1

    def grow(self, after):
        self.own = join(self.own, self.got, after)
        self.got = swap(self.own, "dp", self.back[self.done])
        self.done += 1
        return self.own


def local(
    tokens, lengths, query_key_value, query_bias, value_bias, attn_weight, attn_bias, attn_gain,
    attn_shift, inner_weight, inner_bias, outer_weight, outer_bias, ffn_gain, ffn_shift, cotangent,
):
    groups = lax.axis_size("seq")
    lanes = lax.axis_size("dp")
    me = lax.axis_index("seq")
    lane = lax.axis_index("dp")
    passages, quarter, width = tokens.shape
    hw = H // groups * HD
    rows = passages * quarter
    ff = inner_bias.shape[0]
    rest = [1 << i for i in range(3, lanes.bit_length() - 1)]
    where = me.astype(jnp.int32).reshape(1)

    across = swap(tokens, "seq", 2)
    beside = swap(tokens, "seq", 1)
    corner = swap(across, "seq", 1)
    shards = (tokens, beside, across, corner)
    vec = jnp.stack([attn_bias, attn_gain, attn_shift, outer_bias, ffn_gain, ffn_shift, ffn_shift, ffn_shift])
    vec = vec.astype(F32)
    ib = inner_bias.astype(F32).reshape(1, ff)

    biases = (query_bias.reshape(1, width), value_bias.reshape(1, width))
    qkv, lse, w, near, across_heads, own_context = attend(where, lengths, shards, query_key_value, *biases)
    far_got = swap(across_heads, "seq", 2)
    (near_send,) = pair(near, far_got, [])
    near_got = swap(near_send, "seq", 1)
    context_got = swap(near_got, "seq", 1)
    flat = lambda f: f.reshape(2, rows, hw)
    context = [flat(f) for f in (near, near_got, far_got)]

    wa = attn_weight.reshape(groups, hw, width)
    (
        layer_out, hidden_own, hidden_send, active_own, active_send, slope, grad_outer, grad_two, normal, scale,
        row_sums, wi, wo,
    ) = rows_pass(
        where, tokens.reshape(rows, width), *context, cotangent.reshape(rows, width), wa, vec, ib, inner_weight, outer_weight,
    )
    active_got = swap(active_send, "seq", 1)
    outer_got = swap(grad_outer, "seq", 1)
    hidden_got = swap(hidden_send, "seq", 1)
    grad_one, grad_inner, grad_attn, near, across_heads, vectors = rows_back(
        where, slope, grad_outer, grad_two, normal, scale, row_sums, wa, vec, wi, wo
    )
    a = Reduction([2, "y", 1, 4], [4, 2, 1], lane, me, rest)
    b = Reduction([1, 2, "y", 4], [1, 2, 4], lane, me, rest)
    c = Reduction(["y", 4, 1, 2], [4, 1, 2], lane, me, rest)
    d = Reduction([2, 1, 4], [4, 1, 2], lane, me, rest)
    far_got = swap(across_heads, "seq", 2)
    inner_got = swap(grad_inner, "seq", 1)
    attn_got = swap(grad_attn, "seq", 1)
    outer_send, outer_keep = outer_grad(a.place, active_own, active_got, grad_outer, outer_got)
    near_send, outer_send = pair(near, far_got, [outer_send])
    near_got = swap(near_send, "seq", 1)
    a.begin(outer_keep, outer_send)
    first_send, first_keep, second_send, second_keep = inner_grad(
        b.place, hidden_own, hidden_got, grad_inner, inner_got, own_context.reshape(1, rows, hw), context[2],
        flat(context_got),
        grad_attn, attn_got, [near_send],
    )
    b.begin(first_keep, first_send)
    c.begin(second_keep, second_send)
    grads_h = [f.reshape(2, passages, quarter, hw) for f in (near, near_got, far_got)]
    back_keep, back_send, project_send, project_keep = attend_back(
        d.place, lengths, shards, w, qkv, lse, grads_h, vectors, [second_send]
    )
    d.begin(project_keep, project_send)
    back_got = swap(back_send, "seq", 1)
    t = a.step([back_keep], name="outer_y")
    t = b.step([t], name="first_z")
    t = c.step([t], name="second_m")
    t = d.step([t], name="project_x")
    t = a.step([t], name="outer_x")
    t = b.step([t], name="first_y")
    t = d.step([t], name="project_m")
    t = c.step([t], name="second_x")
    t = a.step([t], name="outer_m")
    t = b.step([t], name="first_m")
    project = d.step([t], splits=4, name="project_sum")
    parts = [project[0]] + [swap(project[j], "seq", j) for j in (1, 2, 3)]
    t = c.step([project[0]], name="second_z")
    (t,) = a.step([t], name="outer_sum")
    a.start(t[0])
    (t,) = b.step([t], name="first_sum")
    b.start(t[0])
    (back_sum,) = sum_pieces(
        d.place,
        [f.reshape(2, 1, rows, width) for f in (back_keep, back_got)],
        [1], 1, False, [t], name="back_y",
    )
    back_over = swap(back_sum, "seq", 2)
    d.start(jnp.concatenate(parts, 0)[None])
    (t,) = c.step([t], name="second_sum")
    c.start(t[0])
    t = b.grow([t])
    t = a.grow([t])
    t = d.grow([t])
    t = c.grow([t])
    t = b.grow([t])
    t = d.grow([t])
    t = a.grow([t])
    t = c.grow([t])
    grad_query_key_value, summed = project_place(d.spots, d.place, d.own, d.got, hw)
    grad_outer_weight = outer_place(a.spots, a.place, a.own, a.got)
    grad_inner_weight, grad_attn_weight = inner_place(
        b.spots, c.spots, b.place, c.place, (b.own, b.got), (c.own, c.got), hw
    )
    input_grad = (
        grad_one + back_keep[0].reshape(rows, width).astype(F32)
        + back_got[0].reshape(rows, width).astype(F32)
        + back_over[0, 0].astype(F32)
    ).astype(LOW)
    return (
        layer_out.reshape(passages, quarter, width),
        input_grad.reshape(passages, quarter, width),
        grad_query_key_value,
        summed[10],
        summed[11],
        grad_attn_weight,
        summed[0],
        summed[1],
        summed[2],
        grad_inner_weight,
        summed[6:10].reshape(-1),
        grad_outer_weight,
        summed[3],
        summed[4],
        summed[5],
    )


def solution(mesh):
    rows = P("dp", "seq", None)
    return jax.shard_map(
        local,
        mesh=mesh,
        in_specs=(rows, P("dp")) + (P(),) * 13 + (rows,),
        out_specs=(
            rows,
            rows,
            P("seq", None),
            P("seq"),
            P("seq"),
            P("seq", None),
            P("seq"),
            P("seq"),
            P("seq"),
            P("seq", None),
            P("seq"),
            P("seq", None),
            P("seq"),
            P("seq"),
            P("seq"),
        ),
        check_vma=False,
    )
```

```python
import jax
import jax.numpy as jnp
from jax import lax
from jax.experimental import pallas as pl
from jax.experimental.pallas import tpu as pltpu
from jax.sharding import PartitionSpec as P

H = 12
HD = 64
EPS = 1e-12
F32 = jnp.float32
LOW = jnp.bfloat16
MIB = 1 << 20
PIECES = 8
STEP = 1.0
BACK = 1.0
FORE = 0.1


def cost(us):
    return pl.CostEstimate(flops=int(us * 1.15e9), bytes_accessed=int(us * 3.69e6), transcendentals=0)


def dot(a, b):
    return lax.dot_general(a, b, (((1,), (0,)), ((), ())), preferred_element_type=F32)


def dot_nt(a, b):
    return lax.dot_general(a, b, (((1,), (1,)), ((), ())), preferred_element_type=F32)


def dot_tn(a, b):
    return lax.dot_general(a, b, (((0,), (0,)), ((), ())), preferred_element_type=F32)


def vmem(shape=None, index=None):
    if shape is None:
        return pl.BlockSpec(memory_space=pltpu.VMEM)
    return pl.BlockSpec(shape, index)


SMEM = pl.BlockSpec(memory_space=pltpu.SMEM)
HBM = pl.BlockSpec(memory_space=pltpu.HBM)


def far(array):
    return pltpu.with_memory_space_constraint(array, pltpu.HBM)


def key_mask(me, length, rows, quarter):
    slot = lax.broadcasted_iota(jnp.int32, (rows, 1), 0)
    block = slot // quarter
    return ((block ^ me) * quarter + (slot - block * quarter)) < length


BLOCK = 128


def choose_kernel(where, w_hbm, qb, vb, w_out, bias_out, wide, w_here, sem):
    me = where[0]
    hw = bias_out.shape[1]
    width = wide.shape[1]
    window = wide.shape[2]
    first = pl.multiple_of(me * hw - (me & 1) * HD, 128)
    choose = lambda f: jnp.where((me & 1) == 1, f[:, HD : HD + hw], f[:, :hw])
    copies = []
    for t in range(3):
        at = pl.ds(pl.multiple_of(t * width + first, 128), window)
        copies.append(pltpu.make_async_copy(w_hbm.at[:, at], wide.at[t], sem.at[t]))
        copies[t].start()
    for i, bias in enumerate((qb, vb)):
        bias_out[i : i + 1, :] = choose(bias[:, pl.ds(first, window)].astype(F32))
    for t in range(3):
        copies[t].wait()
        w_here[:, t * hw : (t + 1) * hw] = choose(wide[t])
    copy = pltpu.make_async_copy(w_here, w_out, sem.at[3])
    copy.start()
    copy.wait()


def choose_heads(where, w, qb, vb):
    width = w.shape[0]
    hw = width // 4
    return pl.pallas_call(
        choose_kernel,
        in_specs=[SMEM, HBM, vmem(), vmem()],
        out_specs=[HBM, vmem()],
        out_shape=[pltpu.HBM((width, 3 * hw), LOW), jax.ShapeDtypeStruct((2, hw), F32)],
        scratch_shapes=[
            pltpu.VMEM((3, width, hw + HD), LOW),
            pltpu.VMEM((width, 3 * hw), LOW),
            pltpu.SemaphoreType.DMA((4,)),
        ],
        compiler_params=pltpu.CompilerParams(vmem_limit_bytes=6 * MIB),
        cost_estimate=cost(1.5),
        name="choose_heads",
    )(where, far(w), qb, vb)


def attend_kernel(where, lengths, x0, x1, x2, x3, w_hbm, bias, *refs):
    qkv_out, chance_out, own_out, c1, c2, c3 = refs[:6]
    x, w, qkv_here, chance_here, own_here, load_sem, store_sem = refs[6:]
    me = where[0]
    passages, quarter, width = x0.shape
    rows = 4 * quarter
    hw = w.shape[1] // 3
    heads = hw // HD
    loads = [pltpu.make_async_copy(w_hbm, w, load_sem.at[4 * passages])]
    for p in range(passages):
        for j, shard in enumerate((x0, x1, x2, x3)):
            here = x.at[p, pl.ds(j * quarter, quarter)]
            loads.append(pltpu.make_async_copy(shard.at[p], here, load_sem.at[p * 4 + j]))
    for copy in loads:
        copy.start()
    loads[0].wait()
    stores = []

    def store(here, out):
        stores.append(pltpu.make_async_copy(here, out, store_sem.at[len(stores)]))
        stores[-1].start()

    for p in range(passages):
        for copy in loads[1 + 4 * p : 5 + 4 * p]:
            copy.wait()
        proj = dot(x[p], w[...])
        q = ((proj[:, :hw] + bias[0:1, :]).astype(LOW).astype(F32) * HD ** (-0.5)).astype(LOW)
        k = proj[:, hw : 2 * hw].astype(LOW)
        v = (proj[:, 2 * hw :] + bias[1:2, :]).astype(LOW)
        qkv_here[p] = jnp.concatenate([q, k, v], 1)
        store(qkv_here.at[p], qkv_out.at[p])
        usable = key_mask(me, lengths[p], rows, quarter)
        parts = []
        for h in range(heads):
            cols = slice(h * HD, (h + 1) * HD)
            some = []
            for b in range(rows // BLOCK):
                mine = slice(b * BLOCK, (b + 1) * BLOCK)
                logits = jnp.where(usable, dot_nt(k[:, cols], q[mine, cols]), -1e9)
                highest = jnp.max(logits, 0, keepdims=True)
                weight = jnp.exp(logits - highest)
                total = jnp.sum(weight, 0, keepdims=True)
                chance = (weight * (1.0 / total)).astype(LOW)
                chance_here[p, h, :, mine] = chance
                some.append(dot_tn(chance, v[:, cols]))
            store(chance_here.at[p, h], chance_out.at[p, h])
            parts.append(jnp.concatenate(some, 0))
        context = jnp.concatenate(parts, 1).astype(LOW)
        own_here[p] = context[:quarter]
        store(own_here.at[p], own_out.at[p])
        for j, out in enumerate((c1, c2, c3)):
            out[p] = context[(j + 1) * quarter : (j + 2) * quarter]
    for copy in stores:
        copy.wait()


def attend(where, lengths, shards, w, bias):
    passages, quarter, width = shards[0].shape
    rows = 4 * quarter
    hw = width // 4
    heads = hw // HD
    kinds = [((passages, rows, 3 * hw), LOW), ((passages, heads, rows, rows), LOW), ((passages, quarter, hw), LOW)]
    return pl.pallas_call(
        attend_kernel,
        in_specs=[SMEM, SMEM] + [HBM] * 5 + [vmem()],
        out_specs=[HBM] * 3 + [vmem()] * 3,
        out_shape=[pltpu.HBM(*kind) for kind in kinds] + [jax.ShapeDtypeStruct(*kinds[2])] * 3,
        scratch_shapes=[pltpu.VMEM((passages, rows, width), LOW), pltpu.VMEM((width, 3 * hw), LOW)]
        + [pltpu.VMEM(*kind) for kind in kinds]
        + [pltpu.SemaphoreType.DMA((4 * passages + 1,)), pltpu.SemaphoreType.DMA((passages * (heads + 2),))],
        compiler_params=pltpu.CompilerParams(vmem_limit_bytes=24 * MIB),
        cost_estimate=cost(FORE),
        name="attend",
    )(where, lengths, *map(far, shards), far(w), bias)


def attend_back_kernel(place, *refs):
    x0, x1, x2, x3, w_hbm, qkv_hbm, chance_hbm, near, near_got, far_got, vectors = refs[:11]
    keep_out, send_out, weight_send, weight_keep = refs[-16:-12]
    x, w, qkv, chance, g, extra_here, joined, back, keep_here, acc, load_sem, store_sem = refs[-12:]
    me = place[1]
    quarter, hw = near.shape[2:]
    rows = 4 * quarter
    heads = hw // HD
    wide = 3 * hw
    scale = HD ** (-0.5)
    made = []

    def load(source, here):
        made.append(pltpu.make_async_copy(source, here, load_sem.at[len(made)]))
        return made[-1]

    needs = []
    for p in range(2):
        mine = [load(qkv_hbm.at[p], qkv.at[p])]
        for j, source in enumerate((near.at[0, p], near_got.at[0, p], far_got.at[0, p], near_got.at[1, p])):
            mine.append(load(source, g.at[p, pl.ds(j * quarter, quarter)]))
        needs.append((mine, [load(chance_hbm.at[p, h], chance.at[p, h]) for h in range(heads)]))
    last = [load(w_hbm, w)]
    late = [load(vectors, extra_here)]
    for p in range(2):
        for j, shard in enumerate((x0, x1, x2, x3)):
            late.append(load(shard.at[p], x.at[pl.ds(p * rows + j * quarter, quarter)]))
    for copy in needs[0][0] + needs[0][1]:
        copy.start()
    stores = []
    sums = [0.0, 0.0]
    for p in range(2):
        for copy in needs[p][0]:
            copy.wait()
        for copy in last + needs[1][0] + needs[1][1] if p == 0 else late:
            copy.start()
        grad_q, grad_k, grad_v = [], [], []
        for h in range(heads):
            cols = slice(h * HD, (h + 1) * HD)
            qh, kh, vh = (qkv[p, :, t * hw + h * HD : t * hw + (h + 1) * HD] for t in range(3))
            gh = g[p, :, cols]
            grad_chance = dot_nt(vh, gh)
            needs[p][1][h].wait()
            low = chance[p, h]
            full = low.astype(F32)
            inner = jnp.sum(grad_chance * full, 0, keepdims=True)
            grad_logits = (full * (grad_chance - inner)).astype(LOW)
            grad_q.append(dot_tn(grad_logits, kh) * scale)
            grad_k.append(dot(grad_logits, qh))
            grad_v.append(dot(low, gh))
        some = jnp.concatenate([jnp.concatenate(f, 1).astype(LOW) for f in (grad_q, grad_k, grad_v)], 1)
        joined[p * rows : (p + 1) * rows, :] = some
        sums = [
            total + jnp.sum(some[:, at : at + hw].astype(F32), 0, keepdims=True)
            for total, at in zip(sums, (0, 2 * hw))
        ]
        if p == 0:
            last[0].wait()
        back[p] = dot_nt(some, w[...]).astype(LOW)
        for j in range(4):
            out = send_out if j % 2 else keep_out
            piece = back.at[p, pl.ds(j * quarter, quarter)]
            stores.append(pltpu.make_async_copy(piece, out.at[j // 2, p], store_sem.at[len(stores)]))
            stores[-1].start()
    for copy in late:
        copy.wait()
    acc[:, :wide] = dot_tn(x[...], joined[...])
    spread = []
    for total in sums:
        blank = jnp.zeros_like(total)
        spread.append(jnp.concatenate([jnp.where(me == i, total, blank) for i in range(4)], 1))
    extra = jnp.concatenate([extra_here[:10, :]] + spread + [jnp.zeros((52, extra_here.shape[1]), F32)], 0)
    acc[:, wide:] = extra.T
    half = PIECES // 2
    n = weight_send.shape[2] // 4
    spot = place[0] & half
    for out, first in ((weight_send, spot ^ half), (keep_here, spot)):
        for j in range(4):
            for e in range(half):
                start = pl.multiple_of((me ^ j) * (n * PIECES) + (first + e) * n, 8)
                out[0, e, j * n : (j + 1) * n, :] = acc[pl.ds(start, n), :].astype(LOW)
    stores.append(pltpu.make_async_copy(keep_here, weight_keep, store_sem.at[len(stores)]))
    stores[-1].start()
    for copy in stores:
        copy.wait()


def attend_back(place, shards, w, qkv, chance, grads, vectors, after=()):
    passages, quarter, width = shards[0].shape
    rows = 4 * quarter
    hw = width // 4
    heads = hw // HD
    n = width // (4 * PIECES)
    weight = ((1, PIECES // 2, 4 * n, 3 * hw + 64), LOW)
    back = ((2, passages, quarter, width), LOW)
    scratch = [
        ((passages * rows, width), LOW), ((width, 3 * hw), LOW), ((passages, rows, 3 * hw), LOW),
        ((passages, heads, rows, rows), LOW), ((passages, rows, hw), LOW), (vectors.shape, F32),
        ((passages * rows, 3 * hw), LOW), ((passages, rows, width), LOW), weight, ((width, 3 * hw + 64), F32),
    ]
    arrays = [*shards, w, qkv, chance, *grads, vectors]
    return pl.pallas_call(
        attend_back_kernel,
        in_specs=[SMEM] + [HBM] * len(arrays) + [ANYWHERE] * len(after),
        out_specs=[HBM, HBM, vmem(), HBM],
        out_shape=[pltpu.HBM(*back), pltpu.HBM(*back), jax.ShapeDtypeStruct(*weight), pltpu.HBM(*weight)],
        scratch_shapes=[pltpu.VMEM(*kind) for kind in scratch]
        + [pltpu.SemaphoreType.DMA((passages * (heads + 9) + 2,)), pltpu.SemaphoreType.DMA((4 * passages + 1,))],
        compiler_params=pltpu.CompilerParams(vmem_limit_bytes=32 * MIB),
        cost_estimate=cost(BACK),
        name="attend_back",
    )(place, *map(far, arrays), *after)


def normalise(field):
    centre = field - jnp.mean(field, -1, keepdims=True)
    scale = lax.rsqrt(jnp.mean(centre * centre, -1, keepdims=True) + EPS)
    return centre * scale, scale


def normalise_back(grad, normal, scale):
    return (
        grad
        - jnp.mean(grad, -1, keepdims=True)
        - normal * jnp.mean(grad * normal, -1, keepdims=True)
    ) * scale


def rows_kernel(
    where, x, c0, c1, c2, c3, cot, wa, vec, ib, wi_hbm, wo_hbm,
    layer_out, grad_one_out, active_out, first_out, second_out, left_out, left_send, near_out, sums_out, across_out,
    wi, wo, slope, parts, layer_here, grad_one_here, active_here, first_here, second_here, left_here, near_here,
    sums_here, flipped, load_sem, weight_sem, store_sem, inner_sem,
):
    me = where[0]
    rows, width = x.shape
    chunk = width
    hw = wa.shape[1]
    loads = [pltpu.make_async_copy(f, parts.at[j], load_sem.at[j]) for j, f in enumerate((c0, c1, c2, c3))]
    order = (0, 1, 2, 3)
    weights = []
    for k, c in enumerate(order):
        cols = pl.ds(pl.multiple_of((me ^ c) * chunk, 128), chunk)
        weights.append(pltpu.make_async_copy(wi_hbm.at[:, cols], wi.at[:, cols], weight_sem.at[2 * k]))
        weights.append(pltpu.make_async_copy(wo_hbm.at[cols, :], wo.at[cols, :], weight_sem.at[2 * k + 1]))
    for copy in loads + weights[:2]:
        copy.start()
    stores = [
        pltpu.make_async_copy(here, out, store_sem.at[i])
        for i, (here, out) in enumerate(
            (
                (left_here.at[0], left_out), (left_here.at[1], left_send), (active_here, active_out),
                (first_here, first_out), (layer_here, layer_out), (grad_one_here, grad_one_out),
                (near_here, near_out), (sums_here, sums_out),
            )
        )
    ]
    row = lambda r: vec[r : r + 1, :]
    attn_bias, attn_gain, attn_shift, outer_bias, ffn_gain, ffn_shift = (row(r) for r in range(6))
    sums_here[...] = jnp.zeros_like(sums_here)
    attended = attn_bias + x[...].astype(F32)
    for copy in loads:
        copy.wait()
    for copy in weights[2:4]:
        copy.start()
    for j in range(4):
        attended += dot(parts[j], wa[me ^ j])
    for j in range(4):
        left_here[j & 1, 2 + (j >> 1)] = parts[j].astype(F32).T.astype(LOW)
    normal_one, scale_one = normalise(attended)
    hidden = normal_one * attn_gain + attn_shift
    hidden_low = hidden.astype(LOW)
    flipped[...] = hidden.T
    for j in range(4):
        start = pl.multiple_of((me ^ j) * hw, 64)
        left_here[j & 1, j >> 1] = flipped[pl.ds(start, hw), :].astype(LOW)
    stores[0].start()
    stores[1].start()
    pre_two = hidden + outer_bias
    for k, c in enumerate(order):
        cols = pl.ds(pl.multiple_of((me ^ c) * chunk, 128), chunk)
        for copy in weights[2 * k + 4 : 2 * k + 6]:
            copy.start()
        weights[2 * k].wait()
        u = dot(hidden_low, wi[:, cols]) + ib[:, cols]
        below = 0.5 * (1.0 + lax.erf(u * (0.5**0.5)))
        density = jnp.exp(-0.5 * u * u) * 0.3989422804014327
        active = (u * below).astype(LOW)
        slope[c] = below + u * density
        here = first_here if c & 1 else active_here
        here[:, (c >> 1) * chunk : ((c >> 1) + 1) * chunk] = active
        weights[2 * k + 1].wait()
        pre_two += dot(active, wo[cols, :])
    stores[2].start()
    normal_two, scale_two = normalise(pre_two)
    layer_here[...] = (normal_two * ffn_gain + ffn_shift).astype(LOW)
    stores[4].start()
    dy = cot[...].astype(F32)
    sums_here[4:5, :] = jnp.sum(dy * normal_two, 0, keepdims=True)
    sums_here[5:6, :] = jnp.sum(dy, 0, keepdims=True)
    grad_two = normalise_back(dy * ffn_gain, normal_two, scale_two)
    grad_outer = grad_two.astype(LOW)
    first_here[:, 2 * chunk :] = grad_outer
    stores[3].start()
    sums_here[3:4, :] = jnp.sum(grad_outer.astype(F32), 0, keepdims=True)
    grad_hidden = grad_two
    moved = []
    for c in range(5):
        some = pl.ds(c * chunk, chunk)
        moved.append(pltpu.make_async_copy(second_here.at[:, some], second_out.at[:, some], inner_sem.at[c]))
    for c in range(4):
        cols = slice(c * chunk, (c + 1) * chunk)
        grad_inner = (dot_nt(grad_outer, wo[cols, :]) * slope[me ^ c]).astype(LOW)
        second_here[:, cols] = grad_inner
        moved[c].start()
        column = jnp.sum(grad_inner.astype(F32), 0, keepdims=True)
        for i in range(4):
            sums_here[6 + i : 7 + i, c * hw : (c + 1) * hw] = column[:, i * hw : (i + 1) * hw]
        grad_hidden += dot_nt(grad_inner, wi[:, cols])
    sums_here[1:2, :] = jnp.sum(grad_hidden * normal_one, 0, keepdims=True)
    sums_here[2:3, :] = jnp.sum(grad_hidden, 0, keepdims=True)
    grad_one = normalise_back(grad_hidden * attn_gain, normal_one, scale_one)
    grad_one_here[...] = grad_one
    stores[5].start()
    grad_attn = grad_one.astype(LOW)
    second_here[:, 4 * chunk :] = grad_attn
    moved[4].start()
    sums_here[0:1, :] = jnp.sum(grad_attn.astype(F32), 0, keepdims=True)
    stores[7].start()
    for j in range(2):
        near_here[j] = dot_nt(grad_attn, wa[me ^ j]).astype(LOW)
    stores[6].start()
    for j in range(2):
        across_out[j] = dot_nt(grad_attn, wa[me ^ (j + 2)]).astype(LOW)
    for copy in moved + stores:
        copy.wait()


def rows_pass(where, x, context, cot, wa, vec, ib, wi, wo):
    rows, width = x.shape
    ff = ib.shape[1]
    hw = wa.shape[1]
    kinds = [
        ((rows, width), LOW), ((rows, width), F32), ((rows, 2 * width), LOW), ((rows, 3 * width), LOW),
        ((rows, ff + width), LOW), ((4, hw, rows), LOW), ((4, hw, rows), LOW), ((2, rows, hw), LOW), ((16, width), F32),
    ]
    here = kinds[:5] + [((2, 4, hw, rows), LOW)] + kinds[7:]
    return pl.pallas_call(
        rows_kernel,
        in_specs=[SMEM, vmem()] + [HBM] * 4 + [vmem()] * 4 + [HBM, HBM],
        out_specs=[HBM] * 9 + [vmem()],
        out_shape=[pltpu.HBM(*kind) for kind in kinds] + [jax.ShapeDtypeStruct((2, rows, hw), LOW)],
        scratch_shapes=[
            pltpu.VMEM(wi.shape, LOW),
            pltpu.VMEM(wo.shape, LOW),
            pltpu.VMEM((4, rows, width), F32),
            pltpu.VMEM((4, rows, hw), LOW),
        ]
        + [pltpu.VMEM(*kind) for kind in here]
        + [pltpu.VMEM((width, rows), F32)]
        + [pltpu.SemaphoreType.DMA((n,)) for n in (4, 8, 8, 5)],
        compiler_params=pltpu.CompilerParams(vmem_limit_bytes=36 * MIB),
        cost_estimate=cost(11),
        name="rows_pass",
    )(where, x, *map(far, context), cot, wa, vec, ib, far(wi), far(wo))


def outer_grad_kernel(place, active, active_got, grad, grad_got, send_out, keep_out):
    half = PIECES // 2
    n = grad.shape[1] // PIECES
    right = jnp.concatenate([grad[...], grad_got[...]], 0)
    product = dot_tn(jnp.concatenate([active[...], active_got[...]], 0), right)

    def store(low_out, high_out):
        for e in range(PIECES):
            out = high_out if e >= half else low_out
            out[0, e % half] = product[e * n : (e + 1) * n].astype(LOW)

    high = (place[0] & half) > 0
    pl.when(high)(lambda: store(send_out, keep_out))
    pl.when(jnp.logical_not(high))(lambda: store(keep_out, send_out))


def outer_grad(place, active, first, first_got):
    rows, width = first.shape
    width //= 3
    block = (1, PIECES // 2, width // PIECES, width)
    side = vmem((rows, width), lambda y: (0, y))
    last = vmem((rows, width), lambda y: (0, 2))
    return pl.pallas_call(
        outer_grad_kernel,
        grid=(2,),
        in_specs=[SMEM, side, side, last, last],
        out_specs=[vmem(block, lambda y: (y, 0, 0, 0))] * 2,
        out_shape=[jax.ShapeDtypeStruct((2,) + block[1:], LOW)] * 2,
        compiler_params=pltpu.CompilerParams(vmem_limit_bytes=16 * MIB),
        cost_estimate=cost(30),
        name="outer_grad",
    )(place, far(active), *map(far, (first_got, first, first_got)))


SPLIT = 128
ORDERS = {
    "a": ([2, 1, "y"], 4, [2, 1]),
    "b": ([4, "y", 2], 1, [2, 4]),
    "c": ([1, "y", 2], 4, [2, 1]),
    "d": ([1, 2], 4, [1, 2]),
}
SEQUENCE = "cacdbcadbcabdcbdabda"


def inner_grad_kernel(
    mine, mine_got, inner, inner_got, attn, attn_got, *refs
):
    first_send, first_keep, second_send, second_keep, left, rest = refs[-6:]
    step = pl.program_id(0)
    hw = mine.shape[1]
    rows, width = attn.shape
    half = PIECES // 2
    n = hw // PIECES
    cols = inner.shape[1] // 2

    @pl.when(step == 0)
    def _():
        grads = jnp.concatenate([attn[...], attn_got[...]], 0)
        for y in range(2):
            left[y * hw : (y + 1) * hw, :rows] = mine[y]
            left[y * hw : (y + 1) * hw, rows:] = mine_got[y]
            rest[y] = dot(jnp.concatenate([mine[2 + y], mine_got[2 + y]], 1), grads)

    product = dot(left[...], jnp.concatenate([inner[...], inner_got[...]], 0))

    bits = refs[:2]

    def store(part, send_out, keep_out, which):
        def put(out, y, at, k):
            some = product[y * hw : (y + 1) * hw, k * cols : (k + 1) * cols]
            if part == 0:
                some = some[:SPLIT]
            else:
                more = rest[y, pl.ds(pl.multiple_of((2 * step + k) * n, 8), n), :]
                some = jnp.concatenate([some[SPLIT:], more[:, : width // 2], more[:, width // 2 :]], 0)
            out[at[0], at[1]] = some.astype(LOW)

        if ORDERS[which][0][0] == "y":
            for k in range(2):
                for y, out in enumerate((keep_out, send_out)):
                    put(out, y, (0, 2 * step + k), k)
        else:
            kept = (bits[part][0] & half) == (step >> 1) * half
            for here, out in ((kept, keep_out), (jnp.logical_not(kept), send_out)):

                @pl.when(here)
                def _(out=out):
                    for k in range(2):
                        for y in range(2):
                            put(out, y, (y, 2 * (step & 1) + k), k)

    store(0, first_send, first_keep, "b")
    store(1, second_send, second_keep, "c")


def inner_grad(places, mine, mine_got, second, second_got, after):
    hw = mine.shape[1]
    rows = second.shape[0]
    width = 4 * hw
    half = PIECES // 2
    cols = 4 * width // PIECES
    counts = [(1, PIECES) if ORDERS[which][0][0] == "y" else (2, half) for which in "bc"]
    first = counts[0] + (SPLIT, cols)
    rest = counts[1] + (hw - SPLIT + 2 * hw // PIECES, cols)
    whole = lambda *s: vmem(s, lambda t: (0,) * len(s))
    side = vmem((rows, 2 * cols), lambda t: (0, t))
    last = vmem((rows, width), lambda t: (0, 4))
    return pl.pallas_call(
        inner_grad_kernel,
        grid=(half,),
        in_specs=[whole(4, hw, rows), whole(4, hw, rows), side, side, last, last, SMEM, SMEM]
        + [ANYWHERE] * len(after),
        out_specs=[whole(*first)] * 2 + [whole(*rest)] * 2,
        out_shape=[jax.ShapeDtypeStruct(s, LOW) for s in (first, first, rest, rest)],
        scratch_shapes=[pltpu.VMEM((2 * hw, 2 * rows), LOW), pltpu.VMEM((2, hw, width), F32)],
        compiler_params=pltpu.CompilerParams(vmem_limit_bytes=20 * MIB),
        cost_estimate=cost(4),
        name="inner_grad",
    )(*map(far, (mine, mine_got, second, second_got, second, second_got)), *places, *after)


ANYWHERE = pl.BlockSpec(memory_space=pl.ANY)


def sum_kernel(spec, place, *refs):
    leads, count, flip, inputs, splits = spec
    ins = refs[: len(inputs)]
    outs = refs[-splits:]
    first = (place[0] // count) * count
    if flip:
        first = first ^ count
    for y, lead in enumerate(leads):
        for r in range(count):
            total = None
            for ref in ins:
                pieces = ref.shape[1]
                base = first & (pieces - 1) if count < pieces else 0
                term = ref[lead if ref.shape[0] > 1 else 0, base + r].astype(F32)
                total = term if total is None else total + term
            if splits == 1:
                outs[0][y, r] = total.astype(LOW)
            else:
                n = total.shape[0] // splits
                for j in range(splits):
                    outs[j][r] = total[j * n : (j + 1) * n].astype(LOW)


def sum_pieces(place, inputs, leads, count, flip, after=(), splits=1, name="sum_pieces"):
    tall, wide = inputs[0].shape[2:]
    spec = (tuple(leads), count, flip, tuple(range(len(inputs))), splits)
    if splits == 1:
        out_shape = [jax.ShapeDtypeStruct((len(leads), count, tall, wide), LOW)]
    else:
        out_shape = [jax.ShapeDtypeStruct((count, tall // splits, wide), LOW)] * splits
    return pl.pallas_call(
        lambda *refs: sum_kernel(spec, *refs),
        in_specs=[SMEM] + [vmem()] * len(inputs) + [ANYWHERE] * len(after),
        out_specs=[vmem()] * splits,
        out_shape=out_shape,
        compiler_params=pltpu.CompilerParams(vmem_limit_bytes=4 * MIB),
        cost_estimate=cost(STEP),
        name=name,
    )(place, *inputs, *after)


def outer_place_kernel(spots, place, own, got, *refs):
    out = refs[-1]
    n = own.shape[1]
    for i, spot in enumerate(spots):
        piece = own[i] if i < 4 else got[i - 4]
        out[pl.ds(pl.multiple_of((place[0] ^ spot) * n, 8), n), :] = piece.astype(F32)


def outer_place(spots, place, own, got, after=()):
    n, width = own.shape[1:]
    return pl.pallas_call(
        lambda *refs: outer_place_kernel(spots, *refs),
        in_specs=[SMEM, vmem(), vmem()] + [ANYWHERE] * len(after),
        out_specs=vmem(),
        out_shape=jax.ShapeDtypeStruct((PIECES * n, width), F32),
        compiler_params=pltpu.CompilerParams(vmem_limit_bytes=4 * MIB),
        cost_estimate=cost(2),
        name="outer_place",
    )(place, own, got, *after)


def inner_place_kernel(spots_one, spots_two, one, two, own, got, own_two, got_two, *refs):
    inner, attn = refs[-2:]
    hw, cols = inner.shape[0], own.shape[2]
    n = attn.shape[0] // PIECES
    for i in range(PIECES):
        piece = (own[i] if i < 4 else got[i - 4]).astype(F32)
        here = one[0] ^ spots_one[i]
        inner[:SPLIT, pl.ds(pl.multiple_of(here * cols, 128), cols)] = piece
        piece = (own_two[i] if i < 4 else got_two[i - 4]).astype(F32)
        here = two[0] ^ spots_two[i]
        some = hw - SPLIT
        inner[SPLIT:, pl.ds(pl.multiple_of(here * cols, 128), cols)] = piece[:some]
        more = jnp.concatenate([piece[some : some + n], piece[some + n :]], 1)
        attn[pl.ds(pl.multiple_of(here * n, 8), n), :] = more


def inner_place(spots_one, spots_two, one, two, parts_one, parts_two, hw, after=()):
    cols = parts_one[0].shape[2]
    n = hw // PIECES
    return pl.pallas_call(
        lambda *refs: inner_place_kernel(spots_one, spots_two, *refs),
        in_specs=[SMEM, SMEM] + [vmem()] * 4 + [ANYWHERE] * len(after),
        out_specs=[vmem(), vmem()],
        out_shape=[
            jax.ShapeDtypeStruct((hw, PIECES * cols), F32),
            jax.ShapeDtypeStruct((PIECES * n, 2 * cols), F32),
        ],
        compiler_params=pltpu.CompilerParams(vmem_limit_bytes=4 * MIB),
        cost_estimate=cost(2),
        name="inner_place",
    )(one, two, *parts_one, *parts_two, *after)


def project_place_kernel(spots, place, own, got, *refs):
    out, vectors, tall = refs[-3:]
    n = own.shape[1] // 4
    hw = out.shape[1] // 12
    wide = 3 * hw
    for i, spot in enumerate(spots):
        ref, k = (own, i) if i < 4 else (got, i - 4)
        rows = pl.ds(pl.multiple_of((place[0] ^ spot) * n, 8), n)
        total = None
        for owner in range(4):
            start = pl.multiple_of((owner ^ place[1]) * n, 8)
            block = ref[k, pl.ds(start, n), :].astype(F32)
            for t in range(3):
                at = t * 4 * hw + owner * hw
                out[rows, at : at + hw] = block[:, t * hw : (t + 1) * hw]
            extra = block[:, wide:]
            total = extra if total is None else total + extra
        tall[rows, : total.shape[1]] = total
    vectors[...] = tall[...].T[: vectors.shape[0]]


def project_place(spots, place, own, got, hw, after=()):
    _, tall, wide = own.shape
    n = tall // 4
    return pl.pallas_call(
        lambda *refs: project_place_kernel(spots, *refs),
        in_specs=[SMEM, vmem(), vmem()] + [ANYWHERE] * len(after),
        out_specs=[vmem(), vmem()],
        out_shape=[
            jax.ShapeDtypeStruct((PIECES * n, 12 * hw), F32),
            jax.ShapeDtypeStruct((16, PIECES * n), F32),
        ],
        scratch_shapes=[pltpu.VMEM((PIECES * n, 128), F32)],
        compiler_params=pltpu.CompilerParams(vmem_limit_bytes=4 * MIB),
        cost_estimate=cost(2),
        name="project_place",
    )(place, own, got, *after)


def join_kernel(*refs):
    out, sem = refs[-2:]
    own, got = refs[:2]
    n = own.shape[0]
    copies = [pltpu.make_async_copy(f, out.at[pl.ds(i * n, n)], sem.at[i]) for i, f in enumerate((own, got))]
    for copy in copies:
        copy.start()
    for copy in copies:
        copy.wait()


def join(own, got, after):
    shape = (2 * own.shape[0],) + own.shape[1:]
    return pl.pallas_call(
        join_kernel,
        in_specs=[ANYWHERE] * (2 + len(after)),
        out_specs=ANYWHERE,
        out_shape=jax.ShapeDtypeStruct(shape, own.dtype),
        scratch_shapes=[pltpu.SemaphoreType.DMA((2,))],
        compiler_params=pltpu.CompilerParams(vmem_limit_bytes=2 * MIB),
        cost_estimate=cost(STEP),
        name="join",
    )(own, got, *after)


def pair_kernel(gates, near, far, *refs):
    out, sem = refs[-1 - gates - 1], refs[-1]
    copies = [pltpu.make_async_copy(f.at[1], out.at[i], sem.at[i]) for i, f in enumerate((near, far))]
    for copy in copies:
        copy.start()
    for copy in copies:
        copy.wait()


def pair(near, far, gated, after=()):
    return pl.pallas_call(
        lambda *refs: pair_kernel(len(gated), *refs),
        in_specs=[ANYWHERE] * (2 + len(gated) + len(after)),
        out_specs=[ANYWHERE] * (1 + len(gated)),
        out_shape=[jax.ShapeDtypeStruct(f.shape, f.dtype) for f in (near, *gated)],
        input_output_aliases={2 + i: 1 + i for i in range(len(gated))},
        scratch_shapes=[pltpu.SemaphoreType.DMA((2,))],
        compiler_params=pltpu.CompilerParams(vmem_limit_bytes=2 * MIB),
        cost_estimate=cost(0.5),
        name="pair",
    )(near, far, *gated, *after)


def swap(field, axis, bit):
    count = lax.axis_size(axis)
    return lax.ppermute(field, axis, [(i, i ^ bit) for i in range(count)])


def add(left, right):
    return (left.astype(F32) + right.astype(F32)).astype(LOW)


class Reduction:
    def __init__(self, order, last, back, lane, me, rest):
        self.order = list(order)
        self.last = last
        self.back = list(back)
        self.rest = rest
        bits = [o for o in order if o != "y"]
        weight = {bit: PIECES >> (k + 1) for k, bit in enumerate(bits)}
        spot = sum(jnp.where(lane & bit, w, 0) for bit, w in weight.items())
        weight[last] = 0
        self.spots = [
            i % 2 + sum(weight[bit] for t, bit in enumerate(back) if i >> (t + 1) & 1) for i in range(PIECES)
        ]
        self.own = None
        self.place = jnp.stack([spot.astype(jnp.int32), me.astype(jnp.int32)])

    def begin(self, keep, send):
        axis = self.order.pop(0)
        got = swap(send, "seq", 2) if axis == "y" else swap(send, "dp", axis)
        self.arrays = [keep, got]
        self.left = keep.shape[1]
        self.folded = keep.shape[0] == 1

    def step(self, after=(), splits=1, name="sum"):
        if not self.order and self.last is None:
            return sum_pieces(self.place, self.arrays, [0], self.left, False, after, splits, name)
        leads = [0] if self.folded else [0, 1]
        if not self.order:
            (sent,) = sum_pieces(self.place, self.arrays, [0], self.left, False, after, name=name)
            self.arrays = [sent, swap(sent, "dp", self.last)]
            self.last = None
            return sent
        axis = self.order.pop(0)
        if axis == "y":
            (sent,) = sum_pieces(self.place, self.arrays, [1], self.left, False, after, name=name)
            self.folded = True
            got = swap(sent, "seq", 2)
        else:
            self.left //= 2
            (sent,) = sum_pieces(self.place, self.arrays, leads, self.left, True, after, name=name)
            got = swap(sent, "dp", axis)
        self.arrays = self.arrays + [got]
        return sent

    def start(self, piece):
        for bit in self.rest:
            piece = add(piece, swap(piece, "dp", bit))
        self.own = piece
        self.got = swap(piece, "dp", self.back[0])
        self.done = 1

    def grow(self, after):
        self.own = join(self.own, self.got, after)
        self.got = swap(self.own, "dp", self.back[self.done])
        self.done += 1
        return self.own


def local(
    tokens, lengths, query_key_value, query_bias, value_bias, attn_weight, attn_bias, attn_gain,
    attn_shift, inner_weight, inner_bias, outer_weight, outer_bias, ffn_gain, ffn_shift, cotangent,
):
    groups = lax.axis_size("seq")
    lanes = lax.axis_size("dp")
    me = lax.axis_index("seq")
    lane = lax.axis_index("dp")
    passages, quarter, width = tokens.shape
    hw = H // groups * HD
    rows = passages * quarter
    ff = inner_bias.shape[0]
    rest = [1 << i for i in range(3, lanes.bit_length() - 1)]
    where = me.astype(jnp.int32).reshape(1)

    across = swap(tokens, "seq", 2)
    beside = swap(tokens, "seq", 1)
    corner = swap(across, "seq", 1)
    shards = (tokens, beside, across, corner)
    vec = jnp.stack([attn_bias, attn_gain, attn_shift, outer_bias, ffn_gain, ffn_shift, ffn_shift, ffn_shift])
    vec = vec.astype(F32)
    ib = inner_bias.astype(F32).reshape(1, ff)

    w, bias = choose_heads(where, query_key_value, query_bias.reshape(1, width), value_bias.reshape(1, width))
    qkv, chance, own, *context_h = attend(where, lengths, shards, w, bias)
    context = [own] + [swap(part, "seq", j) for j, part in zip((1, 2, 3), context_h)]
    context = [part.reshape(rows, hw) for part in context]

    wa = attn_weight.reshape(groups, hw, width)
    layer_out, grad_one, active, first, second, mine, mine_send, near, vectors, across_heads = rows_pass(
        where, tokens.reshape(rows, width), context, cotangent.reshape(rows, width), wa, vec, ib, inner_weight,
        outer_weight,
    )
    first_got = swap(first, "seq", 1)
    second_got = swap(second, "seq", 1)
    mine_got = swap(mine_send, "seq", 1)
    a, b, c, d = (Reduction(*ORDERS[which], lane, me, rest) for which in "abcd")
    far_got = swap(across_heads, "seq", 2)
    outer_send, outer_keep = outer_grad(a.place, active, first, first_got)
    (near_send,) = pair(near, far_got, [], [outer_send])
    near_got = swap(near_send, "seq", 1)
    a.begin(outer_keep, outer_send)
    first_send, first_keep, second_send, second_keep = inner_grad(
        [b.place, c.place], mine, mine_got, second, second_got, [near_send]
    )
    b.begin(first_keep, first_send)
    c.begin(second_keep, second_send)
    grads_h = [f.reshape(2, passages, quarter, hw) for f in (near, near_got, far_got)]
    back_keep, back_send, project_send, project_keep = attend_back(
        d.place, shards, w, qkv, chance, grads_h, vectors, [second_send]
    )
    d.begin(project_keep, project_send)
    back_got = swap(back_send, "seq", 1)
    (back_sum,) = sum_pieces(
        d.place,
        [f.reshape(2, 1, rows, width) for f in (back_keep, back_got)],
        [1], 1, False, name="back_y",
    )
    back_over = swap(back_sum, "seq", 2)
    token = back_keep
    parts = None
    for letter in SEQUENCE:
        chunk = {"a": a, "b": b, "c": c, "d": d}[letter]
        if chunk.order or chunk.last is not None:
            token = chunk.step([token], name="sum_" + letter)
        elif chunk.own is not None:
            token = chunk.grow([token])
        elif chunk is d and parts is None:
            parts = d.step([token], splits=4, name="total_d")
            token = parts[0]
            parts = [parts[0]] + [swap(parts[j], "seq", j) for j in (1, 2, 3)]
        elif chunk is d:
            d.start(jnp.concatenate(parts, 1))
        else:
            (token,) = chunk.step([token], name="total_" + letter)
            chunk.start(token[0])
    grad_query_key_value, summed = project_place(d.spots, d.place, d.own, d.got, hw)
    grad_outer_weight = outer_place(a.spots, a.place, a.own, a.got)
    grad_inner_weight, grad_attn_weight = inner_place(
        b.spots, c.spots, b.place, c.place, (b.own, b.got), (c.own, c.got), hw
    )
    input_grad = (
        grad_one + back_keep[0].reshape(rows, width).astype(F32)
        + back_got[0].reshape(rows, width).astype(F32)
        + back_over[0, 0].astype(F32)
    ).astype(LOW)
    return (
        layer_out.reshape(passages, quarter, width),
        input_grad.reshape(passages, quarter, width),
        grad_query_key_value,
        summed[10],
        summed[11],
        grad_attn_weight,
        summed[0],
        summed[1],
        summed[2],
        grad_inner_weight,
        summed[6:10].reshape(-1),
        grad_outer_weight,
        summed[3],
        summed[4],
        summed[5],
    )


def solution(mesh):
    rows = P("dp", "seq", None)
    return jax.shard_map(
        local,
        mesh=mesh,
        in_specs=(rows, P("dp")) + (P(),) * 13 + (rows,),
        out_specs=(
            rows,
            rows,
            P("seq", None),
            P("seq"),
            P("seq"),
            P("seq", None),
            P("seq"),
            P("seq"),
            P("seq"),
            P("seq", None),
            P("seq"),
            P("seq", None),
            P("seq"),
            P("seq"),
            P("seq"),
        ),
        check_vma=False,
    )
```

```python
import jax
import jax.numpy as jnp
from jax import lax
from jax.experimental import pallas as pl
from jax.experimental.pallas import tpu as pltpu
from jax.sharding import PartitionSpec as P

H = 12
HD = 64
EPS = 1e-12
F32 = jnp.float32
LOW = jnp.bfloat16
MIB = 1 << 20
PIECES = 8
STEP = 1.0
BACK = 1.0
FORE = 0.1


def cost(us):
    return pl.CostEstimate(flops=int(us * 1.15e9), bytes_accessed=int(us * 3.69e6), transcendentals=0)


def dot(a, b):
    return lax.dot_general(a, b, (((1,), (0,)), ((), ())), preferred_element_type=F32)


def dot_nt(a, b):
    return lax.dot_general(a, b, (((1,), (1,)), ((), ())), preferred_element_type=F32)


def dot_tn(a, b):
    return lax.dot_general(a, b, (((0,), (0,)), ((), ())), preferred_element_type=F32)


def vmem(shape=None, index=None):
    if shape is None:
        return pl.BlockSpec(memory_space=pltpu.VMEM)
    return pl.BlockSpec(shape, index)


SMEM = pl.BlockSpec(memory_space=pltpu.SMEM)
HBM = pl.BlockSpec(memory_space=pltpu.HBM)


TOKEN = pltpu.HBM((8, 128), jnp.float32)


def far(array):
    return pltpu.with_memory_space_constraint(array, pltpu.HBM)


def key_mask(me, length, rows, quarter):
    slot = lax.broadcasted_iota(jnp.int32, (rows, 1), 0)
    block = slot // quarter
    return ((block ^ me) * quarter + (slot - block * quarter)) < length


BLOCK = 128


def choose_kernel(where, w_hbm, qb, vb, w_out, bias_out, token, wide, w_here, sem):
    me = where[0]
    hw = bias_out.shape[1]
    width = wide.shape[1]
    window = wide.shape[2]
    first = pl.multiple_of(me * hw - (me & 1) * HD, 128)
    choose = lambda f: jnp.where((me & 1) == 1, f[:, HD : HD + hw], f[:, :hw])
    copies = []
    for t in range(3):
        at = pl.ds(pl.multiple_of(t * width + first, 128), window)
        copies.append(pltpu.make_async_copy(w_hbm.at[:, at], wide.at[t], sem.at[t]))
        copies[t].start()
    for i, bias in enumerate((qb, vb)):
        bias_out[i : i + 1, :] = choose(bias[:, pl.ds(first, window)].astype(F32))
    for t in range(3):
        copies[t].wait()
        w_here[:, t * hw : (t + 1) * hw] = choose(wide[t])
    copy = pltpu.make_async_copy(w_here, w_out, sem.at[3])
    copy.start()
    copy.wait()


def choose_heads(where, w, qb, vb):
    width = w.shape[0]
    hw = width // 4
    return pl.pallas_call(
        choose_kernel,
        in_specs=[SMEM, HBM, vmem(), vmem()],
        out_specs=[HBM, vmem(), HBM],
        out_shape=[pltpu.HBM((width, 3 * hw), LOW), jax.ShapeDtypeStruct((2, hw), F32), TOKEN],
        scratch_shapes=[
            pltpu.VMEM((3, width, hw + HD), LOW),
            pltpu.VMEM((width, 3 * hw), LOW),
            pltpu.SemaphoreType.DMA((4,)),
        ],
        compiler_params=pltpu.CompilerParams(vmem_limit_bytes=6 * MIB),
        cost_estimate=cost(1.5),
        name="choose_heads",
    )(where, far(w), qb, vb)


def attend_kernel(where, lengths, x0, x1, x2, x3, w_hbm, bias, *refs):
    qkv_out, chance_out, own_out, x_out, c1, c2, c3 = refs[:7]
    x, w, qkv_here, chance_here, own_here, load_sem, store_sem = refs[7:]
    me = where[0]
    passages, quarter, width = x0.shape
    rows = 4 * quarter
    hw = w.shape[1] // 3
    heads = hw // HD
    loads = [pltpu.make_async_copy(w_hbm, w, load_sem.at[4 * passages])]
    for p in range(passages):
        for j, shard in enumerate((x0, x1, x2, x3)):
            here = x.at[p, pl.ds(j * quarter, quarter)]
            loads.append(pltpu.make_async_copy(shard.at[p], here, load_sem.at[p * 4 + j]))
    for copy in loads:
        copy.start()
    loads[0].wait()
    stores = []

    def store(here, out):
        stores.append(pltpu.make_async_copy(here, out, store_sem.at[len(stores)]))
        stores[-1].start()

    for p in range(passages):
        for copy in loads[1 + 4 * p : 5 + 4 * p]:
            copy.wait()
        store(x.at[p], x_out.at[p])
        proj = dot(x[p], w[...])
        q = ((proj[:, :hw] + bias[0:1, :]).astype(LOW).astype(F32) * HD ** (-0.5)).astype(LOW)
        k = proj[:, hw : 2 * hw].astype(LOW)
        v = (proj[:, 2 * hw :] + bias[1:2, :]).astype(LOW)
        qkv_here[p] = jnp.concatenate([q, k, v], 1)
        store(qkv_here.at[p], qkv_out.at[p])
        usable = key_mask(me, lengths[p], rows, quarter)
        parts = []
        for h in range(heads):
            cols = slice(h * HD, (h + 1) * HD)
            some = []
            for b in range(rows // BLOCK):
                mine = slice(b * BLOCK, (b + 1) * BLOCK)
                logits = jnp.where(usable, dot_nt(k[:, cols], q[mine, cols]), -1e9)
                highest = jnp.max(logits, 0, keepdims=True)
                weight = jnp.exp(logits - highest)
                total = jnp.sum(weight, 0, keepdims=True)
                chance = (weight * (1.0 / total)).astype(LOW)
                chance_here[p, h, :, mine] = chance
                some.append(dot_tn(chance, v[:, cols]))
            store(chance_here.at[p, h], chance_out.at[p, h])
            parts.append(jnp.concatenate(some, 0))
        context = jnp.concatenate(parts, 1).astype(LOW)
        own_here[p] = context[:quarter]
        store(own_here.at[p], own_out.at[p])
        for j, out in enumerate((c1, c2, c3)):
            out[p] = context[(j + 1) * quarter : (j + 2) * quarter]
    for copy in stores:
        copy.wait()


def attend(where, lengths, shards, w, bias):
    passages, quarter, width = shards[0].shape
    rows = 4 * quarter
    hw = width // 4
    heads = hw // HD
    kinds = [((passages, rows, 3 * hw), LOW), ((passages, heads, rows, rows), LOW), ((passages, quarter, hw), LOW)]
    whole = ((passages, rows, width), LOW)
    return pl.pallas_call(
        attend_kernel,
        in_specs=[SMEM, SMEM] + [HBM] * 3 + [vmem(), HBM, vmem()],
        out_specs=[HBM] * 4 + [vmem()] * 3,
        out_shape=[pltpu.HBM(*kind) for kind in kinds + [whole]] + [jax.ShapeDtypeStruct(*kinds[2])] * 3,
        scratch_shapes=[pltpu.VMEM(*whole), pltpu.VMEM((width, 3 * hw), LOW)]
        + [pltpu.VMEM(*kind) for kind in kinds]
        + [pltpu.SemaphoreType.DMA((4 * passages + 1,)), pltpu.SemaphoreType.DMA((passages * (heads + 3),))],
        compiler_params=pltpu.CompilerParams(vmem_limit_bytes=24 * MIB),
        cost_estimate=cost(FORE),
        name="attend",
    )(where, lengths, *map(far, shards[:3]), shards[3], far(w), bias)


def attend_back_kernel(place, *refs):
    x_hbm, w_hbm, qkv_hbm, chance_hbm, near, near_got, far_got, vectors = refs[:8]
    keep_out, send_out, weight_send, weight_keep, _ = refs[-17:-12]
    x, w, qkv, chance, g, extra_here, joined, back, keep_here, acc, load_sem, store_sem = refs[-12:]
    me = place[1]
    quarter, hw = near.shape[2:]
    rows = 4 * quarter
    heads = hw // HD
    wide = 3 * hw
    scale = HD ** (-0.5)
    made = []

    def load(source, here):
        made.append(pltpu.make_async_copy(source, here, load_sem.at[len(made)]))
        return made[-1]

    needs = []
    for p in range(2):
        mine = [load(qkv_hbm.at[p], qkv.at[p])]
        for j, source in enumerate((near.at[0, p], near_got.at[0, p], far_got.at[0, p], near_got.at[1, p])):
            mine.append(load(source, g.at[p, pl.ds(j * quarter, quarter)]))
        needs.append((mine, [load(chance_hbm.at[p, h], chance.at[p, h]) for h in range(heads)]))
    last = [load(w_hbm, w)]
    late = [load(vectors, extra_here)]
    for p in range(2):
        late.append(load(x_hbm.at[p], x.at[pl.ds(p * rows, rows)]))
    for copy in needs[0][0] + needs[0][1]:
        copy.start()
    stores = []
    sums = [0.0, 0.0]
    for p in range(2):
        for copy in needs[p][0]:
            copy.wait()
        for copy in last + needs[1][0] + needs[1][1] if p == 0 else late:
            copy.start()
        grad_q, grad_k, grad_v = [], [], []
        for h in range(heads):
            cols = slice(h * HD, (h + 1) * HD)
            qh, kh, vh = (qkv[p, :, t * hw + h * HD : t * hw + (h + 1) * HD] for t in range(3))
            gh = g[p, :, cols]
            grad_chance = dot_nt(vh, gh)
            needs[p][1][h].wait()
            low = chance[p, h]
            full = low.astype(F32)
            inner = jnp.sum(grad_chance * full, 0, keepdims=True)
            grad_logits = (full * (grad_chance - inner)).astype(LOW)
            grad_q.append(dot_tn(grad_logits, kh) * scale)
            grad_k.append(dot(grad_logits, qh))
            grad_v.append(dot(low, gh))
        some = jnp.concatenate([jnp.concatenate(f, 1).astype(LOW) for f in (grad_q, grad_k, grad_v)], 1)
        joined[p * rows : (p + 1) * rows, :] = some
        sums = [
            total + jnp.sum(some[:, at : at + hw].astype(F32), 0, keepdims=True)
            for total, at in zip(sums, (0, 2 * hw))
        ]
        if p == 0:
            last[0].wait()
        back[p] = dot_nt(some, w[...]).astype(LOW)
        for j in range(4):
            out = send_out if j % 2 else keep_out
            piece = back.at[p, pl.ds(j * quarter, quarter)]
            stores.append(pltpu.make_async_copy(piece, out.at[j // 2, p], store_sem.at[len(stores)]))
            stores[-1].start()
    for copy in late:
        copy.wait()
    acc[:, :wide] = dot_tn(x[...], joined[...])
    spread = []
    for total in sums:
        blank = jnp.zeros_like(total)
        spread.append(jnp.concatenate([jnp.where(me == i, total, blank) for i in range(4)], 1))
    extra = jnp.concatenate([extra_here[:10, :]] + spread + [jnp.zeros((52, extra_here.shape[1]), F32)], 0)
    acc[:, wide:] = extra.T
    half = PIECES // 2
    n = weight_send.shape[2] // 4
    spot = place[0] & half
    for out, first in ((keep_here, spot), (weight_send, spot ^ half)):
        for j in range(4):
            for e in range(half):
                start = pl.multiple_of((me ^ j) * (n * PIECES) + (first + e) * n, 8)
                out[0, e, j * n : (j + 1) * n, :] = acc[pl.ds(start, n), :].astype(LOW)
        if out is keep_here:
            stores.append(pltpu.make_async_copy(keep_here, weight_keep, store_sem.at[len(stores)]))
            stores[-1].start()
    for copy in stores:
        copy.wait()


def attend_back(place, x, w, qkv, chance, grads, vectors, after=()):
    passages, rows, width = x.shape
    quarter = rows // 4
    hw = width // 4
    heads = hw // HD
    n = width // (4 * PIECES)
    weight = ((1, PIECES // 2, 4 * n, 3 * hw + 64), LOW)
    back = ((2, passages, quarter, width), LOW)
    scratch = [
        ((passages * rows, width), LOW), ((width, 3 * hw), LOW), ((passages, rows, 3 * hw), LOW),
        ((passages, heads, rows, rows), LOW), ((passages, rows, hw), LOW), (vectors.shape, F32),
        ((passages * rows, 3 * hw), LOW), ((passages, rows, width), LOW), weight, ((width, 3 * hw + 64), F32),
    ]
    arrays = [x, w, qkv, chance, *grads, vectors]
    return pl.pallas_call(
        attend_back_kernel,
        in_specs=[SMEM] + [HBM] * 5 + [vmem()] + [HBM] * 2 + [HBM] * len(after),
        out_specs=[HBM, HBM, vmem(), HBM, HBM],
        out_shape=[pltpu.HBM(*back), pltpu.HBM(*back), jax.ShapeDtypeStruct(*weight), pltpu.HBM(*weight), TOKEN],
        scratch_shapes=[pltpu.VMEM(*kind) for kind in scratch]
        + [pltpu.SemaphoreType.DMA((passages * (heads + 9) + 2,)), pltpu.SemaphoreType.DMA((4 * passages + 1,))],
        compiler_params=pltpu.CompilerParams(vmem_limit_bytes=32 * MIB),
        cost_estimate=cost(BACK),
        name="attend_back",
    )(place, *map(far, arrays[:5]), arrays[5], *map(far, arrays[6:]), *map(far, after))


def normalise(field):
    centre = field - jnp.mean(field, -1, keepdims=True)
    scale = lax.rsqrt(jnp.mean(centre * centre, -1, keepdims=True) + EPS)
    return centre * scale, scale


def normalise_back(grad, normal, scale):
    return (
        grad
        - jnp.mean(grad, -1, keepdims=True)
        - normal * jnp.mean(grad * normal, -1, keepdims=True)
    ) * scale


def rows_kernel(
    where, x, c0, c1, c2, c3, cot, wa, vec, ib, wi_hbm, wo_hbm,
    layer_out, grad_one_out, active_out, first_out, second_out, left_out, left_send, near_out, sums_out, across_out,
    wi, wo, slope, parts, layer_here, grad_one_here, active_here, first_here, second_here, left_here, near_here,
    sums_here, flipped, load_sem, weight_sem, store_sem, inner_sem,
):
    me = where[0]
    rows, width = x.shape
    chunk = width
    hw = wa.shape[1]
    loads = [pltpu.make_async_copy(f, parts.at[j], load_sem.at[j]) for j, f in enumerate((c0, c1, c2, c3))]
    order = (0, 1, 2, 3)
    weights = []
    for k, c in enumerate(order):
        cols = pl.ds(pl.multiple_of((me ^ c) * chunk, 128), chunk)
        weights.append(pltpu.make_async_copy(wi_hbm.at[:, cols], wi.at[:, cols], weight_sem.at[2 * k]))
        weights.append(pltpu.make_async_copy(wo_hbm.at[cols, :], wo.at[cols, :], weight_sem.at[2 * k + 1]))
    for copy in loads + weights[:2]:
        copy.start()
    stores = [
        pltpu.make_async_copy(here, out, store_sem.at[i])
        for i, (here, out) in enumerate(
            (
                (left_here.at[0], left_out), (left_here.at[1], left_send), (active_here, active_out),
                (first_here, first_out), (layer_here, layer_out), (grad_one_here, grad_one_out),
                (near_here, near_out), (sums_here, sums_out),
            )
        )
    ]
    row = lambda r: vec[r : r + 1, :]
    attn_bias, attn_gain, attn_shift, outer_bias, ffn_gain, ffn_shift = (row(r) for r in range(6))
    sums_here[...] = jnp.zeros_like(sums_here)
    attended = attn_bias + x[...].astype(F32)
    for copy in loads:
        copy.wait()
    for copy in weights[2:4]:
        copy.start()
    for j in range(4):
        attended += dot(parts[j], wa[me ^ j])
    for j in range(4):
        left_here[j & 1, 2 + (j >> 1)] = parts[j].astype(F32).T.astype(LOW)
    normal_one, scale_one = normalise(attended)
    hidden = normal_one * attn_gain + attn_shift
    hidden_low = hidden.astype(LOW)
    flipped[...] = hidden.T
    for j in range(4):
        start = pl.multiple_of((me ^ j) * hw, 64)
        left_here[j & 1, j >> 1] = flipped[pl.ds(start, hw), :].astype(LOW)
    stores[0].start()
    stores[1].start()
    pre_two = hidden + outer_bias
    for k, c in enumerate(order):
        cols = pl.ds(pl.multiple_of((me ^ c) * chunk, 128), chunk)
        for copy in weights[2 * k + 4 : 2 * k + 6]:
            copy.start()
        weights[2 * k].wait()
        u = dot(hidden_low, wi[:, cols]) + ib[:, cols]
        below = 0.5 * (1.0 + lax.erf(u * (0.5**0.5)))
        density = jnp.exp(-0.5 * u * u) * 0.3989422804014327
        active = (u * below).astype(LOW)
        slope[c] = below + u * density
        here = first_here if c & 1 else active_here
        here[:, (c >> 1) * chunk : ((c >> 1) + 1) * chunk] = active
        weights[2 * k + 1].wait()
        pre_two += dot(active, wo[cols, :])
    stores[2].start()
    normal_two, scale_two = normalise(pre_two)
    layer_here[...] = (normal_two * ffn_gain + ffn_shift).astype(LOW)
    stores[4].start()
    dy = cot[...].astype(F32)
    sums_here[4:5, :] = jnp.sum(dy * normal_two, 0, keepdims=True)
    sums_here[5:6, :] = jnp.sum(dy, 0, keepdims=True)
    grad_two = normalise_back(dy * ffn_gain, normal_two, scale_two)
    grad_outer = grad_two.astype(LOW)
    first_here[:, 2 * chunk :] = grad_outer
    stores[3].start()
    sums_here[3:4, :] = jnp.sum(grad_outer.astype(F32), 0, keepdims=True)
    grad_hidden = grad_two
    moved = []
    for c in range(5):
        some = pl.ds(c * chunk, chunk)
        moved.append(pltpu.make_async_copy(second_here.at[:, some], second_out.at[:, some], inner_sem.at[c]))
    for c in range(4):
        cols = slice(c * chunk, (c + 1) * chunk)
        grad_inner = (dot_nt(grad_outer, wo[cols, :]) * slope[me ^ c]).astype(LOW)
        second_here[:, cols] = grad_inner
        moved[c].start()
        column = jnp.sum(grad_inner.astype(F32), 0, keepdims=True)
        for i in range(4):
            sums_here[6 + i : 7 + i, c * hw : (c + 1) * hw] = column[:, i * hw : (i + 1) * hw]
        grad_hidden += dot_nt(grad_inner, wi[:, cols])
    sums_here[1:2, :] = jnp.sum(grad_hidden * normal_one, 0, keepdims=True)
    sums_here[2:3, :] = jnp.sum(grad_hidden, 0, keepdims=True)
    grad_one = normalise_back(grad_hidden * attn_gain, normal_one, scale_one)
    grad_one_here[...] = grad_one
    stores[5].start()
    grad_attn = grad_one.astype(LOW)
    second_here[:, 4 * chunk :] = grad_attn
    moved[4].start()
    for j in range(2):
        near_here[j] = dot_nt(grad_attn, wa[me ^ j]).astype(LOW)
    stores[6].start()
    sums_here[0:1, :] = jnp.sum(grad_attn.astype(F32), 0, keepdims=True)
    stores[7].start()
    for j in range(2):
        across_out[j] = dot_nt(grad_attn, wa[me ^ (j + 2)]).astype(LOW)
    for copy in moved + stores:
        copy.wait()


def rows_pass(where, x, context, cot, wa, vec, ib, wi, wo):
    rows, width = x.shape
    ff = ib.shape[1]
    hw = wa.shape[1]
    kinds = [
        ((rows, width), LOW), ((rows, width), F32), ((rows, 2 * width), LOW), ((rows, 3 * width), LOW),
        ((rows, ff + width), LOW), ((4, hw, rows), LOW), ((4, hw, rows), LOW), ((2, rows, hw), LOW), ((16, width), F32),
    ]
    here = kinds[:5] + [((2, 4, hw, rows), LOW)] + kinds[7:]
    return pl.pallas_call(
        rows_kernel,
        in_specs=[SMEM, vmem()] + [HBM] * 3 + [vmem()] * 5 + [HBM, HBM],
        out_specs=[HBM] * 9 + [vmem()],
        out_shape=[pltpu.HBM(*kind) for kind in kinds] + [jax.ShapeDtypeStruct((2, rows, hw), LOW)],
        scratch_shapes=[
            pltpu.VMEM(wi.shape, LOW),
            pltpu.VMEM(wo.shape, LOW),
            pltpu.VMEM((4, rows, width), F32),
            pltpu.VMEM((4, rows, hw), LOW),
        ]
        + [pltpu.VMEM(*kind) for kind in here]
        + [pltpu.VMEM((width, rows), F32)]
        + [pltpu.SemaphoreType.DMA((n,)) for n in (4, 8, 8, 5)],
        compiler_params=pltpu.CompilerParams(vmem_limit_bytes=36 * MIB),
        cost_estimate=cost(11),
        name="rows_pass",
    )(where, x, *map(far, context[:3]), context[3], cot, wa, vec, ib, far(wi), far(wo))


def outer_grad_kernel(place, active, active_got, grad, grad_got, send_out, keep_out, token):
    half = PIECES // 2
    n = grad.shape[1] // PIECES
    right = jnp.concatenate([grad[...], grad_got[...]], 0)
    product = dot_tn(jnp.concatenate([active[...], active_got[...]], 0), right)

    def store(low_out, high_out):
        for e in range(PIECES):
            out = high_out if e >= half else low_out
            out[0, e % half] = product[e * n : (e + 1) * n].astype(LOW)

    high = (place[0] & half) > 0
    pl.when(high)(lambda: store(send_out, keep_out))
    pl.when(jnp.logical_not(high))(lambda: store(keep_out, send_out))


def outer_grad(place, active, first, first_got):
    rows, width = first.shape
    width //= 3
    block = (1, PIECES // 2, width // PIECES, width)
    side = vmem((rows, width), lambda y: (0, y))
    last = vmem((rows, width), lambda y: (0, 2))
    return pl.pallas_call(
        outer_grad_kernel,
        grid=(2,),
        in_specs=[SMEM, side, side, last, last],
        out_specs=[vmem(block, lambda y: (y, 0, 0, 0))] * 2 + [HBM],
        out_shape=[jax.ShapeDtypeStruct((2,) + block[1:], LOW)] * 2 + [TOKEN],
        compiler_params=pltpu.CompilerParams(vmem_limit_bytes=16 * MIB),
        cost_estimate=cost(30),
        name="outer_grad",
    )(place, far(active), first_got, far(first), first_got)


SPLIT = 128
ORDERS = {
    "a": ([1, "y", 2], 4, [2, 1]),
    "b": (["y", 2, 1], 4, [2, 1]),
    "c": ([2, 1, "y"], 4, [2, 1]),
    "d": ([1, 4], 2, [1, 4]),
}
SEQUENCE = "abcdbacbdacbddbcadca"


def inner_grad_kernel(bit_b, bit_c, mine_hbm, second_hbm, mine_got, second_got, *refs):
    outs, (mine, second, left, rest, *heres, load_sem, store_sem) = refs[-13:-9], refs[-8:]
    hw, rows = mine.shape[1:]
    width = 4 * hw
    half = PIECES // 2
    n = hw // PIECES
    cols = width // 2
    loads = [pltpu.make_async_copy(mine_hbm, mine, load_sem.at[5])]
    for c in (4, 0, 1, 2, 3):
        some = pl.ds(c * width, width)
        loads.append(pltpu.make_async_copy(second_hbm.at[:, some], second.at[:, some], load_sem.at[c]))
    for copy in loads:
        copy.start()
    for copy in loads[:2]:
        copy.wait()
    grads = jnp.concatenate([second[:, 4 * width :], second_got[:, 4 * width :]], 0)
    for y in range(2):
        left[y * hw : (y + 1) * hw, :rows] = mine[y]
        left[y * hw : (y + 1) * hw, rows:] = mine_got[y]
        rest[y] = dot(jnp.concatenate([mine[2 + y], mine_got[2 + y]], 1), grads)
    waits = []

    def send(part, piece, y, at, keep):
        here = heres[part]
        out = outs[2 * part + 1] if keep else outs[2 * part]
        spot = (part * PIECES + piece) * 2 + y
        copy = pltpu.make_async_copy(here.at[y, piece], out.at[at[0], at[1]], store_sem.at[spot])
        copy.start()
        return copy

    for c in range(4):
        loads[2 + c].wait()
        here = slice(c * width, (c + 1) * width)
        product = dot(left[...], jnp.concatenate([second[:, here], second_got[:, here]], 0))
        for k in range(2):
            piece = 2 * c + k
            for y in range(2):
                some = product[y * hw : (y + 1) * hw, k * cols : (k + 1) * cols]
                heres[0][y, piece] = some[:SPLIT].astype(LOW)
                more = rest[y, piece * n : (piece + 1) * n, :]
                more = jnp.concatenate([some[SPLIT:], more[:, :cols], more[:, cols:]], 0)
                heres[1][y, piece] = more.astype(LOW)
        for part, (which, bit) in enumerate((("b", bit_b), ("c", bit_c))):
            both = [(2 * c + k, y) for k in range(2) for y in range(2)]
            if ORDERS[which][0][0] == "y":
                for piece, y in both:
                    waits.append(send(part, piece, y, (0, piece), y == 0))
            else:
                kept = (bit[0] & half) == (c >> 1) * half
                for here, keep in ((kept, True), (jnp.logical_not(kept), False)):

                    @pl.when(here)
                    def _(part=part, both=both, keep=keep):
                        for piece, y in both:
                            send(part, piece, y, (y, piece % half), keep)

                for piece, y in both:
                    spot = (part * PIECES + piece) * 2 + y
                    out = outs[2 * part].at[y, piece % half]
                    waits.append(pltpu.make_async_copy(heres[part].at[y, piece], out, store_sem.at[spot]))
    for copy in waits:
        copy.wait()


def inner_grad(places, mine, mine_got, second, second_got, after):
    hw = mine.shape[1]
    width = 4 * hw
    half = PIECES // 2
    counts = [(1, PIECES) if ORDERS[which][0][0] == "y" else (2, half) for which in "bc"]
    talls = [SPLIT, hw - SPLIT + 2 * hw // PIECES]
    shapes = [count + (tall, width // 2) for count, tall in zip(counts, talls)]
    return pl.pallas_call(
        inner_grad_kernel,
        in_specs=[SMEM, SMEM, HBM, HBM, vmem(), vmem()] + [HBM] * len(after),
        out_specs=[HBM] * 5,
        out_shape=[pltpu.HBM(shape, LOW) for shape in shapes for _ in range(2)] + [TOKEN],
        scratch_shapes=[
            pltpu.VMEM(mine.shape, LOW),
            pltpu.VMEM(second.shape, LOW),
            pltpu.VMEM((2 * hw, 2 * mine.shape[2]), LOW),
            pltpu.VMEM((2, hw, width), F32),
        ]
        + [pltpu.VMEM((2, PIECES, tall, width // 2), LOW) for tall in talls]
        + [pltpu.SemaphoreType.DMA((6,)), pltpu.SemaphoreType.DMA((4 * PIECES,))],
        compiler_params=pltpu.CompilerParams(vmem_limit_bytes=20 * MIB),
        cost_estimate=cost(4),
        name="inner_grad",
    )(*places, far(mine), far(second), mine_got, second_got, *map(far, after))


ANYWHERE = pl.BlockSpec(memory_space=pl.ANY)


def sum_kernel(spec, place, *refs):
    leads, count, flip, inputs, splits = spec
    ins = refs[: len(inputs)]
    outs = refs[-1 - splits : -1]
    first = (place[0] // count) * count
    if flip:
        first = first ^ count
    for y, lead in enumerate(leads):
        for r in range(count):
            total = None
            for ref in ins:
                pieces = ref.shape[1]
                base = first & (pieces - 1) if count < pieces else 0
                term = ref[lead if ref.shape[0] > 1 else 0, base + r].astype(F32)
                total = term if total is None else total + term
            if splits == 1:
                outs[0][y, r] = total.astype(LOW)
            else:
                n = total.shape[0] // splits
                for j in range(splits):
                    outs[j][r] = total[j * n : (j + 1) * n].astype(LOW)


def sum_pieces(place, inputs, leads, count, flip, after=(), splits=1, name="sum_pieces"):
    tall, wide = inputs[0].shape[2:]
    spec = (tuple(leads), count, flip, tuple(range(len(inputs))), splits)
    if splits == 1:
        out_shape = [jax.ShapeDtypeStruct((len(leads), count, tall, wide), LOW)]
    else:
        out_shape = [jax.ShapeDtypeStruct((count, tall // splits, wide), LOW)] * splits
    return pl.pallas_call(
        lambda *refs: sum_kernel(spec, *refs),
        in_specs=[SMEM] + [vmem()] * len(inputs) + [HBM] * len(after),
        out_specs=[vmem()] * splits + [HBM],
        out_shape=out_shape + [TOKEN],
        compiler_params=pltpu.CompilerParams(vmem_limit_bytes=4 * MIB),
        cost_estimate=cost(STEP),
        name=name,
    )(place, *inputs, *map(far, after))


def outer_place_kernel(spots, place, own, got, *refs):
    out = refs[-1]
    n = own.shape[1]
    for i, spot in enumerate(spots):
        piece = own[i] if i < 4 else got[i - 4]
        out[pl.ds(pl.multiple_of((place[0] ^ spot) * n, 8), n), :] = piece.astype(F32)


def outer_place(spots, place, own, got, after=()):
    n, width = own.shape[1:]
    return pl.pallas_call(
        lambda *refs: outer_place_kernel(spots, *refs),
        in_specs=[SMEM, vmem(), vmem()] + [HBM] * len(after),
        out_specs=vmem(),
        out_shape=jax.ShapeDtypeStruct((PIECES * n, width), F32),
        compiler_params=pltpu.CompilerParams(vmem_limit_bytes=4 * MIB),
        cost_estimate=cost(2),
        name="outer_place",
    )(place, own, got, *map(far, after))


def inner_place_kernel(spots_one, spots_two, one, two, own, got, own_two, got_two, *refs):
    inner, attn = refs[-2:]
    hw, cols = inner.shape[0], own.shape[2]
    n = attn.shape[0] // PIECES
    for i in range(PIECES):
        piece = (own[i] if i < 4 else got[i - 4]).astype(F32)
        here = one[0] ^ spots_one[i]
        inner[:SPLIT, pl.ds(pl.multiple_of(here * cols, 128), cols)] = piece
        piece = (own_two[i] if i < 4 else got_two[i - 4]).astype(F32)
        here = two[0] ^ spots_two[i]
        some = hw - SPLIT
        inner[SPLIT:, pl.ds(pl.multiple_of(here * cols, 128), cols)] = piece[:some]
        more = jnp.concatenate([piece[some : some + n], piece[some + n :]], 1)
        attn[pl.ds(pl.multiple_of(here * n, 8), n), :] = more


def inner_place(spots_one, spots_two, one, two, parts_one, parts_two, hw, after=()):
    cols = parts_one[0].shape[2]
    n = hw // PIECES
    return pl.pallas_call(
        lambda *refs: inner_place_kernel(spots_one, spots_two, *refs),
        in_specs=[SMEM, SMEM] + [vmem()] * 4 + [HBM] * len(after),
        out_specs=[vmem(), vmem()],
        out_shape=[
            jax.ShapeDtypeStruct((hw, PIECES * cols), F32),
            jax.ShapeDtypeStruct((PIECES * n, 2 * cols), F32),
        ],
        compiler_params=pltpu.CompilerParams(vmem_limit_bytes=4 * MIB),
        cost_estimate=cost(2),
        name="inner_place",
    )(one, two, *parts_one, *parts_two, *map(far, after))


def project_place_kernel(spots, place, own, got, *refs):
    out, vectors, tall = refs[-3:]
    n = own.shape[1] // 4
    hw = out.shape[1] // 12
    wide = 3 * hw
    for i, spot in enumerate(spots):
        ref, k = (own, i) if i < 4 else (got, i - 4)
        rows = pl.ds(pl.multiple_of((place[0] ^ spot) * n, 8), n)
        total = None
        for owner in range(4):
            start = pl.multiple_of((owner ^ place[1]) * n, 8)
            block = ref[k, pl.ds(start, n), :].astype(F32)
            for t in range(3):
                at = t * 4 * hw + owner * hw
                out[rows, at : at + hw] = block[:, t * hw : (t + 1) * hw]
            extra = block[:, wide:]
            total = extra if total is None else total + extra
        tall[rows, : total.shape[1]] = total
    vectors[...] = tall[...].T[: vectors.shape[0]]


def project_place(spots, place, own, got, hw, after=()):
    _, tall, wide = own.shape
    n = tall // 4
    return pl.pallas_call(
        lambda *refs: project_place_kernel(spots, *refs),
        in_specs=[SMEM, vmem(), vmem()] + [HBM] * len(after),
        out_specs=[vmem(), vmem()],
        out_shape=[
            jax.ShapeDtypeStruct((PIECES * n, 12 * hw), F32),
            jax.ShapeDtypeStruct((16, PIECES * n), F32),
        ],
        scratch_shapes=[pltpu.VMEM((PIECES * n, 128), F32)],
        compiler_params=pltpu.CompilerParams(vmem_limit_bytes=4 * MIB),
        cost_estimate=cost(2),
        name="project_place",
    )(place, own, got, *map(far, after))


def join_kernel(*refs):
    out, token, sem = refs[-3:]
    own, got = refs[:2]
    n = own.shape[0]
    copies = [pltpu.make_async_copy(f, out.at[pl.ds(i * n, n)], sem.at[i]) for i, f in enumerate((own, got))]
    for copy in copies:
        copy.start()
    for copy in copies:
        copy.wait()


def join(own, got, after):
    shape = (2 * own.shape[0],) + own.shape[1:]
    return pl.pallas_call(
        join_kernel,
        in_specs=[ANYWHERE] * 2 + [HBM] * len(after),
        out_specs=[ANYWHERE, HBM],
        out_shape=[jax.ShapeDtypeStruct(shape, own.dtype), TOKEN],
        scratch_shapes=[pltpu.SemaphoreType.DMA((2,))],
        compiler_params=pltpu.CompilerParams(vmem_limit_bytes=2 * MIB),
        cost_estimate=cost(STEP),
        name="join",
    )(own, got, *map(far, after))


def pass_on_kernel(source, *refs):
    outs, sem = refs[-3:-1], refs[-1]
    copies = [pltpu.make_async_copy(source, out, sem.at[i]) for i, out in enumerate(outs)]
    for copy in copies:
        copy.start()
    for copy in copies:
        copy.wait()


def pass_on(source, after):
    return pl.pallas_call(
        pass_on_kernel,
        in_specs=[vmem()] + [HBM] * len(after),
        out_specs=[vmem(), HBM],
        out_shape=[jax.ShapeDtypeStruct(source.shape, source.dtype), pltpu.HBM(source.shape, source.dtype)],
        scratch_shapes=[pltpu.SemaphoreType.DMA((2,))],
        compiler_params=pltpu.CompilerParams(vmem_limit_bytes=2 * MIB),
        cost_estimate=cost(0.5),
        name="pass_on",
    )(source, *map(far, after))


def pair_kernel(near, far, *refs):
    out, token, sem = refs[-3:]
    copies = [pltpu.make_async_copy(f.at[1], out.at[i], sem.at[i]) for i, f in enumerate((near, far))]
    for copy in copies:
        copy.start()
    for copy in copies:
        copy.wait()


def pair(near, far_got, after):
    return pl.pallas_call(
        pair_kernel,
        in_specs=[ANYWHERE] * 2 + [HBM] * len(after),
        out_specs=[ANYWHERE, HBM],
        out_shape=[jax.ShapeDtypeStruct(near.shape, near.dtype), TOKEN],
        scratch_shapes=[pltpu.SemaphoreType.DMA((2,))],
        compiler_params=pltpu.CompilerParams(vmem_limit_bytes=2 * MIB),
        cost_estimate=cost(0.5),
        name="pair",
    )(near, far_got, *map(far, after))


def swap(field, axis, bit):
    count = lax.axis_size(axis)
    return lax.ppermute(field, axis, [(i, i ^ bit) for i in range(count)])


def add(left, right):
    return (left.astype(F32) + right.astype(F32)).astype(LOW)


class Reduction:
    def __init__(self, order, last, back, lane, me, rest):
        self.order = list(order)
        self.last = last
        self.back = list(back)
        self.rest = rest
        bits = [o for o in order if o != "y"]
        weight = {bit: PIECES >> (k + 1) for k, bit in enumerate(bits)}
        spot = sum(jnp.where(lane & bit, w, 0) for bit, w in weight.items())
        weight[last] = 0
        self.spots = [
            i % 2 + sum(weight[bit] for t, bit in enumerate(back) if i >> (t + 1) & 1) for i in range(PIECES)
        ]
        self.own = None
        self.place = jnp.stack([spot.astype(jnp.int32), me.astype(jnp.int32)])

    def begin(self, keep, send):
        axis = self.order.pop(0)
        got = swap(send, "seq", 2) if axis == "y" else swap(send, "dp", axis)
        self.arrays = [keep, got]
        self.left = keep.shape[1]
        self.folded = keep.shape[0] == 1

    def step(self, after=(), splits=1, name="sum"):
        if not self.order and self.last is None:
            return sum_pieces(self.place, self.arrays, [0], self.left, False, after, splits, name)
        leads = [0] if self.folded else [0, 1]
        if not self.order:
            sent, token = sum_pieces(self.place, self.arrays, [0], self.left, False, after, name=name)
            self.arrays = [sent, swap(sent, "dp", self.last)]
            self.last = None
            return token
        axis = self.order.pop(0)
        if axis == "y":
            sent, token = sum_pieces(self.place, self.arrays, [1], self.left, False, after, name=name)
            self.folded = True
            got = swap(sent, "seq", 2)
        else:
            self.left //= 2
            sent, token = sum_pieces(self.place, self.arrays, leads, self.left, True, after, name=name)
            got = swap(sent, "dp", axis)
        self.arrays = self.arrays + [got]
        return token

    def start(self, piece):
        for bit in self.rest:
            piece = add(piece, swap(piece, "dp", bit))
        self.own = piece
        self.got = swap(piece, "dp", self.back[0])
        self.done = 1

    def grow(self, after):
        self.own, token = join(self.own, self.got, after)
        self.got = swap(self.own, "dp", self.back[self.done])
        self.done += 1
        return token


def local(
    tokens, lengths, query_key_value, query_bias, value_bias, attn_weight, attn_bias, attn_gain,
    attn_shift, inner_weight, inner_bias, outer_weight, outer_bias, ffn_gain, ffn_shift, cotangent,
):
    groups = lax.axis_size("seq")
    lanes = lax.axis_size("dp")
    me = lax.axis_index("seq")
    lane = lax.axis_index("dp")
    passages, quarter, width = tokens.shape
    hw = H // groups * HD
    rows = passages * quarter
    ff = inner_bias.shape[0]
    rest = [1 << i for i in range(3, lanes.bit_length() - 1)]
    where = me.astype(jnp.int32).reshape(1)

    across = swap(tokens, "seq", 2)
    beside = swap(tokens, "seq", 1)
    biases = (query_bias.reshape(1, width), value_bias.reshape(1, width))
    w, bias, token = choose_heads(where, query_key_value, *biases)
    passed, across = pass_on(across, [token])
    corner = swap(passed, "seq", 1)
    shards = (tokens, beside, across, corner)
    vec = jnp.stack([attn_bias, attn_gain, attn_shift, outer_bias, ffn_gain, ffn_shift, ffn_shift, ffn_shift])
    vec = vec.astype(F32)
    ib = inner_bias.astype(F32).reshape(1, ff)

    qkv, chance, own, x_all, *context_h = attend(where, lengths, shards, w, bias)
    context = [own] + [swap(part, "seq", j) for j, part in zip((1, 2, 3), context_h)]
    context = [part.reshape(rows, hw) for part in context]

    wa = attn_weight.reshape(groups, hw, width)
    layer_out, grad_one, active, first, second, mine, mine_send, near, vectors, across_heads = rows_pass(
        where, tokens.reshape(rows, width), context, cotangent.reshape(rows, width), wa, vec, ib, inner_weight,
        outer_weight,
    )
    first_got = swap(first, "seq", 1)
    second_got = swap(second, "seq", 1)
    mine_got = swap(mine_send, "seq", 1)
    a, b, c, d = (Reduction(*ORDERS[which], lane, me, rest) for which in "abcd")
    far_got = swap(across_heads, "seq", 2)
    outer_send, outer_keep, token = outer_grad(a.place, active, first, first_got)
    near_send, paired = pair(near, far_got, [token])
    near_got = swap(near_send, "seq", 1)
    a.begin(outer_keep, outer_send)
    first_send, first_keep, second_send, second_keep, token = inner_grad(
        [b.place, c.place], mine, mine_got, second, second_got, [paired]
    )
    b.begin(first_keep, first_send)
    c.begin(second_keep, second_send)
    grads_h = [f.reshape(2, passages, quarter, hw) for f in (near, near_got, far_got)]
    back_keep, back_send, project_send, project_keep, token = attend_back(
        d.place, x_all, w, qkv, chance, grads_h, vectors, [token]
    )
    d.begin(project_keep, project_send)
    back_got = swap(back_send, "seq", 1)
    back_sum, _ = sum_pieces(
        d.place,
        [f.reshape(2, 1, rows, width) for f in (back_keep, back_got)],
        [1], 1, False, name="back_y",
    )
    back_over = swap(back_sum, "seq", 2)
    parts = None
    for letter in SEQUENCE:
        chunk = {"a": a, "b": b, "c": c, "d": d}[letter]
        if chunk.order or chunk.last is not None:
            token = chunk.step([token], name="sum_" + letter)
        elif chunk.own is not None:
            token = chunk.grow([token])
        elif chunk is d and parts is None:
            *parts, token = d.step([token], splits=4, name="total_d")
            parts = [parts[0]] + [swap(parts[j], "seq", j) for j in (1, 2, 3)]
        elif chunk is d:
            d.start(jnp.concatenate(parts, 1))
        else:
            total, token = chunk.step([token], name="total_" + letter)
            chunk.start(total[0])
    grad_query_key_value, summed = project_place(d.spots, d.place, d.own, d.got, hw)
    grad_outer_weight = outer_place(a.spots, a.place, a.own, a.got)
    grad_inner_weight, grad_attn_weight = inner_place(
        b.spots, c.spots, b.place, c.place, (b.own, b.got), (c.own, c.got), hw
    )
    input_grad = (
        grad_one + back_keep[0].reshape(rows, width).astype(F32)
        + back_got[0].reshape(rows, width).astype(F32)
        + back_over[0, 0].astype(F32)
    ).astype(LOW)
    return (
        layer_out.reshape(passages, quarter, width),
        input_grad.reshape(passages, quarter, width),
        grad_query_key_value,
        summed[10],
        summed[11],
        grad_attn_weight,
        summed[0],
        summed[1],
        summed[2],
        grad_inner_weight,
        summed[6:10].reshape(-1),
        grad_outer_weight,
        summed[3],
        summed[4],
        summed[5],
    )


def solution(mesh):
    rows = P("dp", "seq", None)
    return jax.shard_map(
        local,
        mesh=mesh,
        in_specs=(rows, P("dp")) + (P(),) * 13 + (rows,),
        out_specs=(
            rows,
            rows,
            P("seq", None),
            P("seq"),
            P("seq"),
            P("seq", None),
            P("seq"),
            P("seq"),
            P("seq"),
            P("seq", None),
            P("seq"),
            P("seq", None),
            P("seq"),
            P("seq"),
            P("seq"),
        ),
        check_vma=False,
    )
```

```python
import jax
import jax.numpy as jnp
from jax import lax
from jax.experimental import pallas as pl
from jax.experimental.pallas import tpu as pltpu
from jax.sharding import PartitionSpec as P

H = 12
HD = 64
EPS = 1e-12
F32 = jnp.float32
LOW = jnp.bfloat16
MIB = 1 << 20
PIECES = 8
STEP = 0.85
JOIN = 1.3
BACK = 1.0
FORE = 0.1


def cost(us):
    return pl.CostEstimate(flops=int(us * 1.15e9), bytes_accessed=int(us * 3.69e6), transcendentals=0)


def dot(a, b):
    return lax.dot_general(a, b, (((1,), (0,)), ((), ())), preferred_element_type=F32)


def dot_nt(a, b):
    return lax.dot_general(a, b, (((1,), (1,)), ((), ())), preferred_element_type=F32)


def dot_tn(a, b):
    return lax.dot_general(a, b, (((0,), (0,)), ((), ())), preferred_element_type=F32)


def vmem(shape=None, index=None):
    if shape is None:
        return pl.BlockSpec(memory_space=pltpu.VMEM)
    return pl.BlockSpec(shape, index)


SMEM = pl.BlockSpec(memory_space=pltpu.SMEM)
HBM = pl.BlockSpec(memory_space=pltpu.HBM)


TOKEN = pltpu.HBM((8, 128), jnp.float32)


def far(array):
    return pltpu.with_memory_space_constraint(array, pltpu.HBM)


def key_mask(me, length, rows, quarter):
    slot = lax.broadcasted_iota(jnp.int32, (rows, 1), 0)
    block = slot // quarter
    return ((block ^ me) * quarter + (slot - block * quarter)) < length


BLOCK = 128


def choose_kernel(where, w_hbm, qb, vb, w_out, bias_out, token, wide, w_here, sem):
    me = where[0]
    hw = bias_out.shape[1]
    width = wide.shape[1]
    window = wide.shape[2]
    first = pl.multiple_of(me * hw - (me & 1) * HD, 128)
    choose = lambda f: jnp.where((me & 1) == 1, f[:, HD : HD + hw], f[:, :hw])
    copies = []
    for t in range(3):
        at = pl.ds(pl.multiple_of(t * width + first, 128), window)
        copies.append(pltpu.make_async_copy(w_hbm.at[:, at], wide.at[t], sem.at[t]))
        copies[t].start()
    for i, bias in enumerate((qb, vb)):
        bias_out[i : i + 1, :] = choose(bias[:, pl.ds(first, window)].astype(F32))
    for t in range(3):
        copies[t].wait()
        w_here[:, t * hw : (t + 1) * hw] = choose(wide[t])
    copy = pltpu.make_async_copy(w_here, w_out, sem.at[3])
    copy.start()
    copy.wait()


def choose_heads(where, w, qb, vb):
    width = w.shape[0]
    hw = width // 4
    return pl.pallas_call(
        choose_kernel,
        in_specs=[SMEM, HBM, vmem(), vmem()],
        out_specs=[HBM, vmem(), HBM],
        out_shape=[pltpu.HBM((width, 3 * hw), LOW), jax.ShapeDtypeStruct((2, hw), F32), TOKEN],
        scratch_shapes=[
            pltpu.VMEM((3, width, hw + HD), LOW),
            pltpu.VMEM((width, 3 * hw), LOW),
            pltpu.SemaphoreType.DMA((4,)),
        ],
        compiler_params=pltpu.CompilerParams(vmem_limit_bytes=6 * MIB),
        cost_estimate=cost(1.5),
        name="choose_heads",
    )(where, far(w), qb, vb)


def attend_kernel(where, lengths, x0, x1, x2, x3, w_hbm, bias, *refs):
    qkv_out, chance_out, own_out, x_out, c1, c2, c3 = refs[:7]
    x, w, qkv_here, chance_here, own_here, load_sem, store_sem = refs[7:]
    me = where[0]
    passages, quarter, width = x0.shape
    rows = 4 * quarter
    hw = w.shape[1] // 3
    heads = hw // HD
    loads = [pltpu.make_async_copy(w_hbm, w, load_sem.at[4 * passages])]
    for p in range(passages):
        for j, shard in enumerate((x0, x1, x2, x3)):
            here = x.at[p, pl.ds(j * quarter, quarter)]
            loads.append(pltpu.make_async_copy(shard.at[p], here, load_sem.at[p * 4 + j]))
    for copy in loads:
        copy.start()
    loads[0].wait()
    stores = []

    def store(here, out):
        stores.append(pltpu.make_async_copy(here, out, store_sem.at[len(stores)]))
        stores[-1].start()

    for p in range(passages):
        for copy in loads[1 + 4 * p : 5 + 4 * p]:
            copy.wait()
        store(x.at[p], x_out.at[p])
        proj = dot(x[p], w[...])
        q = ((proj[:, :hw] + bias[0:1, :]).astype(LOW).astype(F32) * HD ** (-0.5)).astype(LOW)
        k = proj[:, hw : 2 * hw].astype(LOW)
        v = (proj[:, 2 * hw :] + bias[1:2, :]).astype(LOW)
        qkv_here[p] = jnp.concatenate([q, k, v], 1)
        store(qkv_here.at[p], qkv_out.at[p])
        usable = key_mask(me, lengths[p], rows, quarter)
        parts = []
        for h in range(heads):
            cols = slice(h * HD, (h + 1) * HD)
            some = []
            for b in range(rows // BLOCK):
                mine = slice(b * BLOCK, (b + 1) * BLOCK)
                logits = jnp.where(usable, dot_nt(k[:, cols], q[mine, cols]), -1e9)
                highest = jnp.max(logits, 0, keepdims=True)
                weight = jnp.exp(logits - highest)
                total = jnp.sum(weight, 0, keepdims=True)
                chance = (weight * (1.0 / total)).astype(LOW)
                chance_here[p, h, :, mine] = chance
                some.append(dot_tn(chance, v[:, cols]))
            store(chance_here.at[p, h], chance_out.at[p, h])
            parts.append(jnp.concatenate(some, 0))
        context = jnp.concatenate(parts, 1).astype(LOW)
        own_here[p] = context[:quarter]
        store(own_here.at[p], own_out.at[p])
        for j, out in enumerate((c1, c2, c3)):
            out[p] = context[(j + 1) * quarter : (j + 2) * quarter]
    for copy in stores:
        copy.wait()


def attend(where, lengths, shards, w, bias):
    passages, quarter, width = shards[0].shape
    rows = 4 * quarter
    hw = width // 4
    heads = hw // HD
    kinds = [((passages, rows, 3 * hw), LOW), ((passages, heads, rows, rows), LOW), ((passages, quarter, hw), LOW)]
    whole = ((passages, rows, width), LOW)
    return pl.pallas_call(
        attend_kernel,
        in_specs=[SMEM, SMEM, vmem(), HBM, vmem(), vmem(), HBM, vmem()],
        out_specs=[HBM] * 4 + [vmem()] * 3,
        out_shape=[pltpu.HBM(*kind) for kind in kinds + [whole]] + [jax.ShapeDtypeStruct(*kinds[2])] * 3,
        scratch_shapes=[pltpu.VMEM(*whole), pltpu.VMEM((width, 3 * hw), LOW)]
        + [pltpu.VMEM(*kind) for kind in kinds]
        + [pltpu.SemaphoreType.DMA((4 * passages + 1,)), pltpu.SemaphoreType.DMA((passages * (heads + 3),))],
        compiler_params=pltpu.CompilerParams(vmem_limit_bytes=24 * MIB),
        cost_estimate=cost(FORE),
        name="attend",
    )(where, lengths, shards[0], far(shards[1]), shards[2], shards[3], far(w), bias)


def attend_back_kernel(place, *refs):
    x_hbm, w_hbm, qkv_hbm, chance_hbm, near, near_got, far_got, vectors = refs[:8]
    keep_out, send_out, weight_send, weight_keep, _ = refs[-17:-12]
    x, w, qkv, chance, g, extra_here, joined, back, keep_here, acc, load_sem, store_sem = refs[-12:]
    me = place[1]
    quarter, hw = near.shape[2:]
    rows = 4 * quarter
    heads = hw // HD
    wide = 3 * hw
    scale = HD ** (-0.5)
    made = []

    def load(source, here):
        made.append(pltpu.make_async_copy(source, here, load_sem.at[len(made)]))
        return made[-1]

    needs = []
    for p in range(2):
        mine = [load(qkv_hbm.at[p], qkv.at[p])]
        for j, source in enumerate((near.at[0, p], near_got.at[0, p], far_got.at[0, p], near_got.at[1, p])):
            mine.append(load(source, g.at[p, pl.ds(j * quarter, quarter)]))
        needs.append((mine, [load(chance_hbm.at[p, h], chance.at[p, h]) for h in range(heads)]))
    last = [load(w_hbm, w)]
    late = [load(vectors, extra_here)]
    for p in range(2):
        late.append(load(x_hbm.at[p], x.at[pl.ds(p * rows, rows)]))
    for copy in needs[0][0] + needs[0][1]:
        copy.start()
    stores = []
    sums = [0.0, 0.0]
    for p in range(2):
        for copy in needs[p][0]:
            copy.wait()
        for copy in last + needs[1][0] + needs[1][1] if p == 0 else late:
            copy.start()
        grad_q, grad_k, grad_v = [], [], []
        for h in range(heads):
            cols = slice(h * HD, (h + 1) * HD)
            qh, kh, vh = (qkv[p, :, t * hw + h * HD : t * hw + (h + 1) * HD] for t in range(3))
            gh = g[p, :, cols]
            grad_chance = dot_nt(vh, gh)
            needs[p][1][h].wait()
            low = chance[p, h]
            full = low.astype(F32)
            inner = jnp.sum(grad_chance * full, 0, keepdims=True)
            grad_logits = (full * (grad_chance - inner)).astype(LOW)
            grad_q.append(dot_tn(grad_logits, kh) * scale)
            grad_k.append(dot(grad_logits, qh))
            grad_v.append(dot(low, gh))
        some = jnp.concatenate([jnp.concatenate(f, 1).astype(LOW) for f in (grad_q, grad_k, grad_v)], 1)
        joined[p * rows : (p + 1) * rows, :] = some
        sums = [
            total + jnp.sum(some[:, at : at + hw].astype(F32), 0, keepdims=True)
            for total, at in zip(sums, (0, 2 * hw))
        ]
        if p == 0:
            last[0].wait()
        back[p] = dot_nt(some, w[...]).astype(LOW)
        for j in range(4):
            out = send_out if j % 2 else keep_out
            piece = back.at[p, pl.ds(j * quarter, quarter)]
            stores.append(pltpu.make_async_copy(piece, out.at[j // 2, p], store_sem.at[len(stores)]))
            stores[-1].start()
    for copy in late:
        copy.wait()
    acc[:, :wide] = dot_tn(x[...], joined[...])
    spread = []
    for total in sums:
        blank = jnp.zeros_like(total)
        spread.append(jnp.concatenate([jnp.where(me == i, total, blank) for i in range(4)], 1))
    extra = jnp.concatenate([extra_here[:10, :]] + spread + [jnp.zeros((52, extra_here.shape[1]), F32)], 0)
    acc[:, wide:] = extra.T
    half = PIECES // 2
    n = weight_send.shape[2] // 4
    spot = place[0] & half
    for out, first in ((keep_here, spot), (weight_send, spot ^ half)):
        for j in range(4):
            for e in range(half):
                start = pl.multiple_of((me ^ j) * (n * PIECES) + (first + e) * n, 8)
                out[0, e, j * n : (j + 1) * n, :] = acc[pl.ds(start, n), :].astype(LOW)
        if out is keep_here:
            stores.append(pltpu.make_async_copy(keep_here, weight_keep, store_sem.at[len(stores)]))
            stores[-1].start()
    for copy in stores:
        copy.wait()


def attend_back(place, x, w, qkv, chance, grads, vectors, after=()):
    passages, rows, width = x.shape
    quarter = rows // 4
    hw = width // 4
    heads = hw // HD
    n = width // (4 * PIECES)
    weight = ((1, PIECES // 2, 4 * n, 3 * hw + 64), LOW)
    back = ((2, passages, quarter, width), LOW)
    scratch = [
        ((passages * rows, width), LOW), ((width, 3 * hw), LOW), ((passages, rows, 3 * hw), LOW),
        ((passages, heads, rows, rows), LOW), ((passages, rows, hw), LOW), (vectors.shape, F32),
        ((passages * rows, 3 * hw), LOW), ((passages, rows, width), LOW), weight, ((width, 3 * hw + 64), F32),
    ]
    arrays = [x, w, qkv, chance, *grads, vectors]
    return pl.pallas_call(
        attend_back_kernel,
        in_specs=[SMEM] + [HBM] * 5 + [vmem()] + [HBM] * 2 + [HBM] * len(after),
        out_specs=[HBM, HBM, vmem(), HBM, HBM],
        out_shape=[pltpu.HBM(*back), pltpu.HBM(*back), jax.ShapeDtypeStruct(*weight), pltpu.HBM(*weight), TOKEN],
        scratch_shapes=[pltpu.VMEM(*kind) for kind in scratch]
        + [pltpu.SemaphoreType.DMA((passages * (heads + 9) + 2,)), pltpu.SemaphoreType.DMA((4 * passages + 1,))],
        compiler_params=pltpu.CompilerParams(vmem_limit_bytes=32 * MIB),
        cost_estimate=cost(BACK),
        name="attend_back",
    )(place, *map(far, arrays[:5]), arrays[5], *map(far, arrays[6:]), *map(far, after))


def normalise(field):
    centre = field - jnp.mean(field, -1, keepdims=True)
    scale = lax.rsqrt(jnp.mean(centre * centre, -1, keepdims=True) + EPS)
    return centre * scale, scale


def normalise_back(grad, normal, scale):
    return (
        grad
        - jnp.mean(grad, -1, keepdims=True)
        - normal * jnp.mean(grad * normal, -1, keepdims=True)
    ) * scale


def rows_kernel(
    where, x, c0, c1, c2, c3, cot, wa, vec, ib, wi_hbm, wo_hbm,
    layer_out, grad_one_out, active_out, first_out, second_out, left_out, left_send, near_out, sums_out, across_out,
    wi, wo, slope, parts, layer_here, grad_one_here, active_here, first_here, second_here, left_here, near_here,
    sums_here, flipped, load_sem, weight_sem, store_sem, inner_sem,
):
    me = where[0]
    rows, width = x.shape
    chunk = width
    hw = wa.shape[1]
    loads = [pltpu.make_async_copy(f, parts.at[j], load_sem.at[j]) for j, f in enumerate((c0, c1, c2, c3))]
    order = (0, 1, 2, 3)
    weights = []
    for k, c in enumerate(order):
        cols = pl.ds(pl.multiple_of((me ^ c) * chunk, 128), chunk)
        weights.append(pltpu.make_async_copy(wi_hbm.at[:, cols], wi.at[:, cols], weight_sem.at[2 * k]))
        weights.append(pltpu.make_async_copy(wo_hbm.at[cols, :], wo.at[cols, :], weight_sem.at[2 * k + 1]))
    for copy in loads + weights[:2]:
        copy.start()
    stores = [
        pltpu.make_async_copy(here, out, store_sem.at[i])
        for i, (here, out) in enumerate(
            (
                (left_here.at[0], left_out), (left_here.at[1], left_send), (active_here, active_out),
                (first_here, first_out), (layer_here, layer_out), (grad_one_here, grad_one_out),
                (near_here, near_out), (sums_here, sums_out),
            )
        )
    ]
    row = lambda r: vec[r : r + 1, :]
    attn_bias, attn_gain, attn_shift, outer_bias, ffn_gain, ffn_shift = (row(r) for r in range(6))
    sums_here[...] = jnp.zeros_like(sums_here)
    attended = attn_bias + x[...].astype(F32)
    for copy in loads:
        copy.wait()
    for copy in weights[2:4]:
        copy.start()
    for j in range(4):
        attended += dot(parts[j], wa[me ^ j])
    for j in range(4):
        left_here[j & 1, 2 + (j >> 1)] = parts[j].astype(F32).T.astype(LOW)
    normal_one, scale_one = normalise(attended)
    hidden = normal_one * attn_gain + attn_shift
    hidden_low = hidden.astype(LOW)
    flipped[...] = hidden.T
    for j in range(4):
        start = pl.multiple_of((me ^ j) * hw, 64)
        left_here[j & 1, j >> 1] = flipped[pl.ds(start, hw), :].astype(LOW)
    stores[0].start()
    stores[1].start()
    pre_two = hidden + outer_bias
    for k, c in enumerate(order):
        cols = pl.ds(pl.multiple_of((me ^ c) * chunk, 128), chunk)
        for copy in weights[2 * k + 4 : 2 * k + 6]:
            copy.start()
        weights[2 * k].wait()
        u = dot(hidden_low, wi[:, cols]) + ib[:, cols]
        below = 0.5 * (1.0 + lax.erf(u * (0.5**0.5)))
        density = jnp.exp(-0.5 * u * u) * 0.3989422804014327
        active = (u * below).astype(LOW)
        slope[c] = below + u * density
        here = first_here if c & 1 else active_here
        here[:, (c >> 1) * chunk : ((c >> 1) + 1) * chunk] = active
        weights[2 * k + 1].wait()
        pre_two += dot(active, wo[cols, :])
    stores[2].start()
    normal_two, scale_two = normalise(pre_two)
    layer_here[...] = (normal_two * ffn_gain + ffn_shift).astype(LOW)
    stores[4].start()
    dy = cot[...].astype(F32)
    sums_here[4:5, :] = jnp.sum(dy * normal_two, 0, keepdims=True)
    sums_here[5:6, :] = jnp.sum(dy, 0, keepdims=True)
    grad_two = normalise_back(dy * ffn_gain, normal_two, scale_two)
    grad_outer = grad_two.astype(LOW)
    first_here[:, 2 * chunk :] = grad_outer
    stores[3].start()
    sums_here[3:4, :] = jnp.sum(grad_outer.astype(F32), 0, keepdims=True)
    grad_hidden = grad_two
    moved = []
    for c in range(5):
        some = pl.ds(c * chunk, chunk)
        moved.append(pltpu.make_async_copy(second_here.at[:, some], second_out.at[:, some], inner_sem.at[c]))
    for c in range(4):
        cols = slice(c * chunk, (c + 1) * chunk)
        grad_inner = (dot_nt(grad_outer, wo[cols, :]) * slope[me ^ c]).astype(LOW)
        second_here[:, cols] = grad_inner
        moved[c].start()
        column = jnp.sum(grad_inner.astype(F32), 0, keepdims=True)
        for i in range(4):
            sums_here[6 + i : 7 + i, c * hw : (c + 1) * hw] = column[:, i * hw : (i + 1) * hw]
        grad_hidden += dot_nt(grad_inner, wi[:, cols])
    sums_here[1:2, :] = jnp.sum(grad_hidden * normal_one, 0, keepdims=True)
    sums_here[2:3, :] = jnp.sum(grad_hidden, 0, keepdims=True)
    grad_one = normalise_back(grad_hidden * attn_gain, normal_one, scale_one)
    grad_one_here[...] = grad_one
    stores[5].start()
    grad_attn = grad_one.astype(LOW)
    second_here[:, 4 * chunk :] = grad_attn
    moved[4].start()
    for j in range(2):
        near_here[j] = dot_nt(grad_attn, wa[me ^ j]).astype(LOW)
    stores[6].start()
    sums_here[0:1, :] = jnp.sum(grad_attn.astype(F32), 0, keepdims=True)
    stores[7].start()
    for j in range(2):
        across_out[j] = dot_nt(grad_attn, wa[me ^ (j + 2)]).astype(LOW)
    for copy in moved + stores:
        copy.wait()


def rows_pass(where, x, context, cot, wa, vec, ib, wi, wo):
    rows, width = x.shape
    ff = ib.shape[1]
    hw = wa.shape[1]
    kinds = [
        ((rows, width), LOW), ((rows, width), F32), ((rows, 2 * width), LOW), ((rows, 3 * width), LOW),
        ((rows, ff + width), LOW), ((4, hw, rows), LOW), ((4, hw, rows), LOW), ((2, rows, hw), LOW), ((16, width), F32),
    ]
    here = kinds[:5] + [((2, 4, hw, rows), LOW)] + kinds[7:]
    return pl.pallas_call(
        rows_kernel,
        in_specs=[SMEM, vmem()] + [HBM] * 3 + [vmem()] * 5 + [HBM, HBM],
        out_specs=[HBM] * 9 + [vmem()],
        out_shape=[pltpu.HBM(*kind) for kind in kinds] + [jax.ShapeDtypeStruct((2, rows, hw), LOW)],
        scratch_shapes=[
            pltpu.VMEM(wi.shape, LOW),
            pltpu.VMEM(wo.shape, LOW),
            pltpu.VMEM((4, rows, width), F32),
            pltpu.VMEM((4, rows, hw), LOW),
        ]
        + [pltpu.VMEM(*kind) for kind in here]
        + [pltpu.VMEM((width, rows), F32)]
        + [pltpu.SemaphoreType.DMA((n,)) for n in (4, 8, 8, 5)],
        compiler_params=pltpu.CompilerParams(vmem_limit_bytes=36 * MIB),
        cost_estimate=cost(11),
        name="rows_pass",
    )(where, x, *map(far, context[:3]), context[3], cot, wa, vec, ib, far(wi), far(wo))


def outer_grad_kernel(place, active, active_got, grad, grad_got, send_out, keep_out, token):
    half = PIECES // 2
    n = grad.shape[1] // PIECES
    right = jnp.concatenate([grad[...], grad_got[...]], 0)
    product = dot_tn(jnp.concatenate([active[...], active_got[...]], 0), right)

    def store(low_out, high_out):
        for e in range(PIECES):
            out = high_out if e >= half else low_out
            out[0, e % half] = product[e * n : (e + 1) * n].astype(LOW)

    high = (place[0] & half) > 0
    pl.when(high)(lambda: store(send_out, keep_out))
    pl.when(jnp.logical_not(high))(lambda: store(keep_out, send_out))


def outer_grad(place, active, first, first_got):
    rows, width = first.shape
    width //= 3
    block = (1, PIECES // 2, width // PIECES, width)
    side = vmem((rows, width), lambda y: (0, y))
    last = vmem((rows, width), lambda y: (0, 2))
    return pl.pallas_call(
        outer_grad_kernel,
        grid=(2,),
        in_specs=[SMEM, side, side, last, last],
        out_specs=[vmem(block, lambda y: (y, 0, 0, 0))] * 2 + [HBM],
        out_shape=[jax.ShapeDtypeStruct((2,) + block[1:], LOW)] * 2 + [TOKEN],
        compiler_params=pltpu.CompilerParams(vmem_limit_bytes=16 * MIB),
        cost_estimate=cost(30),
        name="outer_grad",
    )(place, far(active), first_got, far(first), first_got)


SPLIT = 128
ORDERS = {
    "a": ([1, "y", 2], 4, [2, 1]),
    "b": (["y", 2, 1], 4, [2, 1]),
    "c": ([2, 1, "y"], 4, [1, 2]),
    "d": ([1, 4], 2, [1, 4]),
}
SEQUENCE = "abcdbacbdacbdedbcadca"


def inner_grad_kernel(bit_b, bit_c, mine_hbm, second_hbm, mine_got, second_got, *refs):
    outs, (mine, second, left, rest, *heres, load_sem, store_sem) = refs[-13:-9], refs[-8:]
    hw, rows = mine.shape[1:]
    width = 4 * hw
    half = PIECES // 2
    n = hw // PIECES
    cols = width // 2
    loads = [pltpu.make_async_copy(mine_hbm, mine, load_sem.at[5])]
    for c in (4, 0, 1, 2, 3):
        some = pl.ds(c * width, width)
        loads.append(pltpu.make_async_copy(second_hbm.at[:, some], second.at[:, some], load_sem.at[c]))
    for copy in loads:
        copy.start()
    for copy in loads[:2]:
        copy.wait()
    grads = jnp.concatenate([second[:, 4 * width :], second_got[:, 4 * width :]], 0)
    for y in range(2):
        left[y * hw : (y + 1) * hw, :rows] = mine[y]
        left[y * hw : (y + 1) * hw, rows:] = mine_got[y]
        rest[y] = dot(jnp.concatenate([mine[2 + y], mine_got[2 + y]], 1), grads)
    waits = []

    def send(part, piece, y, at, keep):
        here = heres[part]
        out = outs[2 * part + 1] if keep else outs[2 * part]
        spot = (part * PIECES + piece) * 2 + y
        copy = pltpu.make_async_copy(here.at[y, piece], out.at[at[0], at[1]], store_sem.at[spot])
        copy.start()
        return copy

    for c in range(4):
        loads[2 + c].wait()
        here = slice(c * width, (c + 1) * width)
        product = dot(left[...], jnp.concatenate([second[:, here], second_got[:, here]], 0))
        for k in range(2):
            piece = 2 * c + k
            for y in range(2):
                some = product[y * hw : (y + 1) * hw, k * cols : (k + 1) * cols]
                heres[0][y, piece] = some[:SPLIT].astype(LOW)
                more = rest[y, piece * n : (piece + 1) * n, :]
                more = jnp.concatenate([some[SPLIT:], more[:, :cols], more[:, cols:]], 0)
                heres[1][y, piece] = more.astype(LOW)
        for part, (which, bit) in enumerate((("b", bit_b), ("c", bit_c))):
            both = [(2 * c + k, y) for k in range(2) for y in range(2)]
            if ORDERS[which][0][0] == "y":
                for piece, y in both:
                    waits.append(send(part, piece, y, (0, piece), y == 0))
            else:
                kept = (bit[0] & half) == (c >> 1) * half
                for here, keep in ((kept, True), (jnp.logical_not(kept), False)):

                    @pl.when(here)
                    def _(part=part, both=both, keep=keep):
                        for piece, y in both:
                            send(part, piece, y, (y, piece % half), keep)

                for piece, y in both:
                    spot = (part * PIECES + piece) * 2 + y
                    out = outs[2 * part].at[y, piece % half]
                    waits.append(pltpu.make_async_copy(heres[part].at[y, piece], out, store_sem.at[spot]))
    for copy in waits:
        copy.wait()


def inner_grad(places, mine, mine_got, second, second_got, after):
    hw = mine.shape[1]
    width = 4 * hw
    half = PIECES // 2
    counts = [(1, PIECES) if ORDERS[which][0][0] == "y" else (2, half) for which in "bc"]
    talls = [SPLIT, hw - SPLIT + 2 * hw // PIECES]
    shapes = [count + (tall, width // 2) for count, tall in zip(counts, talls)]
    return pl.pallas_call(
        inner_grad_kernel,
        in_specs=[SMEM, SMEM, HBM, HBM, vmem(), vmem()] + [HBM] * len(after),
        out_specs=[HBM] * 5,
        out_shape=[pltpu.HBM(shape, LOW) for shape in shapes for _ in range(2)] + [TOKEN],
        scratch_shapes=[
            pltpu.VMEM(mine.shape, LOW),
            pltpu.VMEM(second.shape, LOW),
            pltpu.VMEM((2 * hw, 2 * mine.shape[2]), LOW),
            pltpu.VMEM((2, hw, width), F32),
        ]
        + [pltpu.VMEM((2, PIECES, tall, width // 2), LOW) for tall in talls]
        + [pltpu.SemaphoreType.DMA((6,)), pltpu.SemaphoreType.DMA((4 * PIECES,))],
        compiler_params=pltpu.CompilerParams(vmem_limit_bytes=20 * MIB),
        cost_estimate=cost(4),
        name="inner_grad",
    )(*places, far(mine), far(second), mine_got, second_got, *map(far, after))


ANYWHERE = pl.BlockSpec(memory_space=pl.ANY)


def sum_kernel(spec, place, *refs):
    leads, count, flip, inputs, splits = spec
    ins = refs[: len(inputs)]
    outs = refs[-1 - splits : -1]
    first = (place[0] // count) * count
    if flip:
        first = first ^ count
    for y, lead in enumerate(leads):
        for r in range(count):
            total = None
            for ref in ins:
                pieces = ref.shape[1]
                base = first & (pieces - 1) if count < pieces else 0
                term = ref[lead if ref.shape[0] > 1 else 0, base + r].astype(F32)
                total = term if total is None else total + term
            if splits == 1:
                outs[0][y, r] = total.astype(LOW)
            else:
                n = total.shape[0] // splits
                for j in range(splits):
                    outs[j][r] = total[j * n : (j + 1) * n].astype(LOW)


def sum_pieces(place, inputs, leads, count, flip, after=(), splits=1, name="sum_pieces"):
    tall, wide = inputs[0].shape[2:]
    spec = (tuple(leads), count, flip, tuple(range(len(inputs))), splits)
    if splits == 1:
        out_shape = [jax.ShapeDtypeStruct((len(leads), count, tall, wide), LOW)]
    else:
        out_shape = [jax.ShapeDtypeStruct((count, tall // splits, wide), LOW)] * splits
    return pl.pallas_call(
        lambda *refs: sum_kernel(spec, *refs),
        in_specs=[SMEM] + [vmem()] * len(inputs) + [HBM] * len(after),
        out_specs=[vmem()] * splits + [HBM],
        out_shape=out_shape + [TOKEN],
        compiler_params=pltpu.CompilerParams(vmem_limit_bytes=4 * MIB),
        cost_estimate=cost(STEP),
        name=name,
    )(place, *inputs, *map(far, after))


def outer_place_kernel(spots, place, own, got, *refs):
    out = refs[-1]
    n = own.shape[1]
    for i, spot in enumerate(spots):
        piece = own[i] if i < 4 else got[i - 4]
        out[pl.ds(pl.multiple_of((place[0] ^ spot) * n, 8), n), :] = piece.astype(F32)


def outer_place(spots, place, own, got, after=()):
    n, width = own.shape[1:]
    return pl.pallas_call(
        lambda *refs: outer_place_kernel(spots, *refs),
        in_specs=[SMEM, vmem(), vmem()] + [HBM] * len(after),
        out_specs=vmem(),
        out_shape=jax.ShapeDtypeStruct((PIECES * n, width), F32),
        compiler_params=pltpu.CompilerParams(vmem_limit_bytes=4 * MIB),
        cost_estimate=cost(2),
        name="outer_place",
    )(place, own, got, *map(far, after))


def inner_place_kernel(spots_one, spots_two, one, two, own, got, own_two, got_two, *refs):
    inner, attn = refs[-2:]
    hw, cols = inner.shape[0], own.shape[2]
    n = attn.shape[0] // PIECES
    for i in range(PIECES):
        piece = (own[i] if i < 4 else got[i - 4]).astype(F32)
        here = one[0] ^ spots_one[i]
        inner[:SPLIT, pl.ds(pl.multiple_of(here * cols, 128), cols)] = piece
        piece = (own_two[i] if i < 4 else got_two[i - 4]).astype(F32)
        here = two[0] ^ spots_two[i]
        some = hw - SPLIT
        inner[SPLIT:, pl.ds(pl.multiple_of(here * cols, 128), cols)] = piece[:some]
        more = jnp.concatenate([piece[some : some + n], piece[some + n :]], 1)
        attn[pl.ds(pl.multiple_of(here * n, 8), n), :] = more


def inner_place(spots_one, spots_two, one, two, parts_one, parts_two, hw, after=()):
    cols = parts_one[0].shape[2]
    n = hw // PIECES
    return pl.pallas_call(
        lambda *refs: inner_place_kernel(spots_one, spots_two, *refs),
        in_specs=[SMEM, SMEM] + [vmem()] * 4 + [HBM] * len(after),
        out_specs=[vmem(), vmem()],
        out_shape=[
            jax.ShapeDtypeStruct((hw, PIECES * cols), F32),
            jax.ShapeDtypeStruct((PIECES * n, 2 * cols), F32),
        ],
        compiler_params=pltpu.CompilerParams(vmem_limit_bytes=4 * MIB),
        cost_estimate=cost(2),
        name="inner_place",
    )(one, two, *parts_one, *parts_two, *map(far, after))


def project_place_kernel(spots, place, own, got, *refs):
    out, vectors, tall = refs[-3:]
    n = own.shape[1] // 4
    hw = out.shape[1] // 12
    wide = 3 * hw
    for i, spot in enumerate(spots):
        ref, k = (own, i) if i < 4 else (got, i - 4)
        rows = pl.ds(pl.multiple_of((place[0] ^ spot) * n, 8), n)
        total = None
        for owner in range(4):
            start = pl.multiple_of((owner ^ place[1]) * n, 8)
            block = ref[k, pl.ds(start, n), :].astype(F32)
            for t in range(3):
                at = t * 4 * hw + owner * hw
                out[rows, at : at + hw] = block[:, t * hw : (t + 1) * hw]
            extra = block[:, wide:]
            total = extra if total is None else total + extra
        tall[rows, : total.shape[1]] = total
    vectors[...] = tall[...].T[: vectors.shape[0]]


def project_place(spots, place, own, got, hw, after=()):
    _, tall, wide = own.shape
    n = tall // 4
    return pl.pallas_call(
        lambda *refs: project_place_kernel(spots, *refs),
        in_specs=[SMEM, vmem(), vmem()] + [HBM] * len(after),
        out_specs=[vmem(), vmem()],
        out_shape=[
            jax.ShapeDtypeStruct((PIECES * n, 12 * hw), F32),
            jax.ShapeDtypeStruct((16, PIECES * n), F32),
        ],
        scratch_shapes=[pltpu.VMEM((PIECES * n, 128), F32)],
        compiler_params=pltpu.CompilerParams(vmem_limit_bytes=4 * MIB),
        cost_estimate=cost(2),
        name="project_place",
    )(place, own, got, *map(far, after))


def join_kernel(*refs):
    out, token, sem = refs[-3:]
    own, got = refs[:2]
    n = own.shape[0]
    copies = [pltpu.make_async_copy(f, out.at[pl.ds(i * n, n)], sem.at[i]) for i, f in enumerate((own, got))]
    for copy in copies:
        copy.start()
    for copy in copies:
        copy.wait()


def join(own, got, after):
    shape = (2 * own.shape[0],) + own.shape[1:]
    return pl.pallas_call(
        join_kernel,
        in_specs=[ANYWHERE] * 2 + [HBM] * len(after),
        out_specs=[ANYWHERE, HBM],
        out_shape=[jax.ShapeDtypeStruct(shape, own.dtype), TOKEN],
        scratch_shapes=[pltpu.SemaphoreType.DMA((2,))],
        compiler_params=pltpu.CompilerParams(vmem_limit_bytes=2 * MIB),
        cost_estimate=cost(JOIN),
        name="join",
    )(own, got, *map(far, after))


def pass_on_kernel(source, *refs):
    out, sem = refs[-2:]
    copy = pltpu.make_async_copy(source, out, sem.at[0])
    copy.start()
    copy.wait()


def pass_on(source, after):
    return pl.pallas_call(
        pass_on_kernel,
        in_specs=[vmem()] + [HBM] * len(after),
        out_specs=vmem(),
        out_shape=jax.ShapeDtypeStruct(source.shape, source.dtype),
        scratch_shapes=[pltpu.SemaphoreType.DMA((1,))],
        compiler_params=pltpu.CompilerParams(vmem_limit_bytes=2 * MIB),
        cost_estimate=cost(0.5),
        name="pass_on",
    )(source, *map(far, after))


def pair_kernel(near, far, *refs):
    out, token, sem = refs[-3:]
    copies = [pltpu.make_async_copy(f.at[1], out.at[i], sem.at[i]) for i, f in enumerate((near, far))]
    for copy in copies:
        copy.start()
    for copy in copies:
        copy.wait()


def pair(near, far_got, after):
    return pl.pallas_call(
        pair_kernel,
        in_specs=[ANYWHERE] * 2 + [HBM] * len(after),
        out_specs=[ANYWHERE, HBM],
        out_shape=[jax.ShapeDtypeStruct(near.shape, near.dtype), TOKEN],
        scratch_shapes=[pltpu.SemaphoreType.DMA((2,))],
        compiler_params=pltpu.CompilerParams(vmem_limit_bytes=2 * MIB),
        cost_estimate=cost(0.5),
        name="pair",
    )(near, far_got, *map(far, after))


def swap(field, axis, bit):
    count = lax.axis_size(axis)
    return lax.ppermute(field, axis, [(i, i ^ bit) for i in range(count)])


def add(left, right):
    return (left.astype(F32) + right.astype(F32)).astype(LOW)


class Reduction:
    def __init__(self, order, last, back, lane, me, rest):
        self.order = list(order)
        self.last = last
        self.back = list(back)
        self.rest = rest
        bits = [o for o in order if o != "y"]
        weight = {bit: PIECES >> (k + 1) for k, bit in enumerate(bits)}
        spot = sum(jnp.where(lane & bit, w, 0) for bit, w in weight.items())
        weight[last] = 0
        self.spots = [
            i % 2 + sum(weight[bit] for t, bit in enumerate(back) if i >> (t + 1) & 1) for i in range(PIECES)
        ]
        self.own = None
        self.place = jnp.stack([spot.astype(jnp.int32), me.astype(jnp.int32)])

    def begin(self, keep, send):
        axis = self.order.pop(0)
        got = swap(send, "seq", 2) if axis == "y" else swap(send, "dp", axis)
        self.arrays = [keep, got]
        self.left = keep.shape[1]
        self.folded = keep.shape[0] == 1

    def step(self, after=(), splits=1, name="sum"):
        if not self.order and self.last is None:
            return sum_pieces(self.place, self.arrays, [0], self.left, False, after, splits, name)
        leads = [0] if self.folded else [0, 1]
        if not self.order:
            sent, token = sum_pieces(self.place, self.arrays, [0], self.left, False, after, name=name)
            self.arrays = [sent, swap(sent, "dp", self.last)]
            self.last = None
            return token
        axis = self.order.pop(0)
        if axis == "y":
            sent, token = sum_pieces(self.place, self.arrays, [1], self.left, False, after, name=name)
            self.folded = True
            got = swap(sent, "seq", 2)
        else:
            self.left //= 2
            sent, token = sum_pieces(self.place, self.arrays, leads, self.left, True, after, name=name)
            got = swap(sent, "dp", axis)
        self.arrays = self.arrays + [got]
        return token

    def start(self, piece):
        for bit in self.rest:
            piece = add(piece, swap(piece, "dp", bit))
        self.own = piece
        self.got = swap(piece, "dp", self.back[0])
        self.done = 1

    def grow(self, after):
        self.own, token = join(self.own, self.got, after)
        self.got = swap(self.own, "dp", self.back[self.done])
        self.done += 1
        return token


def local(
    tokens, lengths, query_key_value, query_bias, value_bias, attn_weight, attn_bias, attn_gain,
    attn_shift, inner_weight, inner_bias, outer_weight, outer_bias, ffn_gain, ffn_shift, cotangent,
):
    groups = lax.axis_size("seq")
    lanes = lax.axis_size("dp")
    me = lax.axis_index("seq")
    lane = lax.axis_index("dp")
    passages, quarter, width = tokens.shape
    hw = H // groups * HD
    rows = passages * quarter
    ff = inner_bias.shape[0]
    rest = [1 << i for i in range(3, lanes.bit_length() - 1)]
    where = me.astype(jnp.int32).reshape(1)

    across = swap(tokens, "seq", 2)
    beside = swap(tokens, "seq", 1)
    biases = (query_bias.reshape(1, width), value_bias.reshape(1, width))
    w, bias, token = choose_heads(where, query_key_value, *biases)
    across = pass_on(across, [token])
    corner = swap(across, "seq", 1)
    shards = (tokens, beside, across, corner)
    vec = jnp.stack([attn_bias, attn_gain, attn_shift, outer_bias, ffn_gain, ffn_shift, ffn_shift, ffn_shift])
    vec = vec.astype(F32)
    ib = inner_bias.astype(F32).reshape(1, ff)

    qkv, chance, own, x_all, *context_h = attend(where, lengths, shards, w, bias)
    context = [own] + [swap(part, "seq", j) for j, part in zip((1, 2, 3), context_h)]
    context = [part.reshape(rows, hw) for part in context]

    wa = attn_weight.reshape(groups, hw, width)
    layer_out, grad_one, active, first, second, mine, mine_send, near, vectors, across_heads = rows_pass(
        where, tokens.reshape(rows, width), context, cotangent.reshape(rows, width), wa, vec, ib, inner_weight,
        outer_weight,
    )
    first_got = swap(first, "seq", 1)
    second_got = swap(second, "seq", 1)
    mine_got = swap(mine_send, "seq", 1)
    a, b, c, d = (Reduction(*ORDERS[which], lane, me, rest) for which in "abcd")
    far_got = swap(across_heads, "seq", 2)
    outer_send, outer_keep, token = outer_grad(a.place, active, first, first_got)
    near_send, paired = pair(near, far_got, [token])
    near_got = swap(near_send, "seq", 1)
    a.begin(outer_keep, outer_send)
    first_send, first_keep, second_send, second_keep, token = inner_grad(
        [b.place, c.place], mine, mine_got, second, second_got, [paired]
    )
    b.begin(first_keep, first_send)
    c.begin(second_keep, second_send)
    grads_h = [f.reshape(2, passages, quarter, hw) for f in (near, near_got, far_got)]
    back_keep, back_send, project_send, project_keep, token = attend_back(
        d.place, x_all, w, qkv, chance, grads_h, vectors, [token]
    )
    d.begin(project_keep, project_send)
    back_got = swap(back_send, "seq", 1)

    def begin_back(after):
        total, token = sum_pieces(
            d.place,
            [f.reshape(2, 1, rows, width) for f in (back_keep, back_got)],
            [1], 1, False, after, name="back_y",
        )
        return swap(total, "seq", 2), token

    if "e" not in SEQUENCE:
        back_over, _ = begin_back([])
    parts = None
    for letter in SEQUENCE:
        if letter == "e":
            back_over, token = begin_back([token])
            continue
        chunk = {"a": a, "b": b, "c": c, "d": d}[letter]
        if chunk.order or chunk.last is not None:
            token = chunk.step([token], name="sum_" + letter)
        elif chunk.own is not None:
            token = chunk.grow([token])
        elif chunk is d and parts is None:
            *parts, token = d.step([token], splits=4, name="total_d")
            parts = [parts[0]] + [swap(parts[j], "seq", j) for j in (1, 2, 3)]
        elif chunk is d:
            d.start(jnp.concatenate(parts, 1))
        else:
            total, token = chunk.step([token], name="total_" + letter)
            chunk.start(total[0])
    grad_query_key_value, summed = project_place(d.spots, d.place, d.own, d.got, hw)
    grad_outer_weight = outer_place(a.spots, a.place, a.own, a.got)
    grad_inner_weight, grad_attn_weight = inner_place(
        b.spots, c.spots, b.place, c.place, (b.own, b.got), (c.own, c.got), hw
    )
    input_grad = (
        grad_one + back_keep[0].reshape(rows, width).astype(F32)
        + back_got[0].reshape(rows, width).astype(F32)
        + back_over[0, 0].astype(F32)
    ).astype(LOW)
    return (
        layer_out.reshape(passages, quarter, width),
        input_grad.reshape(passages, quarter, width),
        grad_query_key_value,
        summed[10],
        summed[11],
        grad_attn_weight,
        summed[0],
        summed[1],
        summed[2],
        grad_inner_weight,
        summed[6:10].reshape(-1),
        grad_outer_weight,
        summed[3],
        summed[4],
        summed[5],
    )


def solution(mesh):
    rows = P("dp", "seq", None)
    return jax.shard_map(
        local,
        mesh=mesh,
        in_specs=(rows, P("dp")) + (P(),) * 13 + (rows,),
        out_specs=(
            rows,
            rows,
            P("seq", None),
            P("seq"),
            P("seq"),
            P("seq", None),
            P("seq"),
            P("seq"),
            P("seq"),
            P("seq", None),
            P("seq"),
            P("seq", None),
            P("seq"),
            P("seq"),
            P("seq"),
        ),
        check_vma=False,
    )
```

```python
import jax
import jax.numpy as jnp
from jax import lax
from jax.experimental import pallas as pl
from jax.experimental.pallas import tpu as pltpu
from jax.sharding import PartitionSpec as P

H = 12
HD = 64
EPS = 1e-12
F32 = jnp.float32
LOW = jnp.bfloat16
MIB = 1 << 20
PIECES = 8
STEP = 0.85
JOIN = 1.3
BACK = 1.0
FORE = 0.1


def cost(us):
    return pl.CostEstimate(flops=int(us * 1.15e9), bytes_accessed=int(us * 3.69e6), transcendentals=0)


def dot(a, b):
    return lax.dot_general(a, b, (((1,), (0,)), ((), ())), preferred_element_type=F32)


def dot_nt(a, b):
    return lax.dot_general(a, b, (((1,), (1,)), ((), ())), preferred_element_type=F32)


def dot_tn(a, b):
    return lax.dot_general(a, b, (((0,), (0,)), ((), ())), preferred_element_type=F32)


def vmem(shape=None, index=None):
    if shape is None:
        return pl.BlockSpec(memory_space=pltpu.VMEM)
    return pl.BlockSpec(shape, index)


SMEM = pl.BlockSpec(memory_space=pltpu.SMEM)
HBM = pl.BlockSpec(memory_space=pltpu.HBM)


TOKEN = pltpu.HBM((8, 128), jnp.float32)


def far(array):
    return pltpu.with_memory_space_constraint(array, pltpu.HBM)


def key_mask(me, length, rows, quarter):
    slot = lax.broadcasted_iota(jnp.int32, (rows, 1), 0)
    block = slot // quarter
    return ((block ^ me) * quarter + (slot - block * quarter)) < length


BLOCK = 128


def choose_kernel(where, w_hbm, qb, vb, w_out, bias_out, token, wide, w_here, sem):
    me = where[0]
    hw = bias_out.shape[1]
    width = wide.shape[1]
    window = wide.shape[2]
    first = pl.multiple_of(me * hw - (me & 1) * HD, 128)
    choose = lambda f: jnp.where((me & 1) == 1, f[:, HD : HD + hw], f[:, :hw])
    copies = []
    for t in range(3):
        at = pl.ds(pl.multiple_of(t * width + first, 128), window)
        copies.append(pltpu.make_async_copy(w_hbm.at[:, at], wide.at[t], sem.at[t]))
        copies[t].start()
    for i, bias in enumerate((qb, vb)):
        bias_out[i : i + 1, :] = choose(bias[:, pl.ds(first, window)].astype(F32))
    for t in range(3):
        copies[t].wait()
        w_here[:, t * hw : (t + 1) * hw] = choose(wide[t])
    copy = pltpu.make_async_copy(w_here, w_out, sem.at[3])
    copy.start()
    copy.wait()


def choose_heads(where, w, qb, vb):
    width = w.shape[0]
    hw = width // 4
    return pl.pallas_call(
        choose_kernel,
        in_specs=[SMEM, HBM, vmem(), vmem()],
        out_specs=[HBM, vmem(), HBM],
        out_shape=[pltpu.HBM((width, 3 * hw), LOW), jax.ShapeDtypeStruct((2, hw), F32), TOKEN],
        scratch_shapes=[
            pltpu.VMEM((3, width, hw + HD), LOW),
            pltpu.VMEM((width, 3 * hw), LOW),
            pltpu.SemaphoreType.DMA((4,)),
        ],
        compiler_params=pltpu.CompilerParams(vmem_limit_bytes=6 * MIB),
        cost_estimate=cost(1.5),
        name="choose_heads",
    )(where, far(w), qb, vb)


def attend_kernel(where, lengths, x0, x1, x2, x3, w_hbm, bias, *refs):
    qkv_out, chance_out, own_out, x_out, c1, c2, c3 = refs[:7]
    x, w, qkv_here, chance_here, own_here, load_sem, store_sem = refs[7:]
    me = where[0]
    passages, quarter, width = x0.shape
    rows = 4 * quarter
    hw = w.shape[1] // 3
    heads = hw // HD
    loads = [pltpu.make_async_copy(w_hbm, w, load_sem.at[4 * passages])]
    for p in range(passages):
        for j, shard in enumerate((x0, x1, x2, x3)):
            here = x.at[p, pl.ds(j * quarter, quarter)]
            loads.append(pltpu.make_async_copy(shard.at[p], here, load_sem.at[p * 4 + j]))
    for copy in loads:
        copy.start()
    loads[0].wait()
    stores = []

    def store(here, out):
        stores.append(pltpu.make_async_copy(here, out, store_sem.at[len(stores)]))
        stores[-1].start()

    for p in range(passages):
        for copy in loads[1 + 4 * p : 5 + 4 * p]:
            copy.wait()
        store(x.at[p], x_out.at[p])
        proj = dot(x[p], w[...])
        q = ((proj[:, :hw] + bias[0:1, :]).astype(LOW).astype(F32) * HD ** (-0.5)).astype(LOW)
        k = proj[:, hw : 2 * hw].astype(LOW)
        v = (proj[:, 2 * hw :] + bias[1:2, :]).astype(LOW)
        qkv_here[p] = jnp.concatenate([q, k, v], 1)
        store(qkv_here.at[p], qkv_out.at[p])
        usable = key_mask(me, lengths[p], rows, quarter)
        parts = []
        for h in range(heads):
            cols = slice(h * HD, (h + 1) * HD)
            some = []
            for b in range(rows // BLOCK):
                mine = slice(b * BLOCK, (b + 1) * BLOCK)
                logits = jnp.where(usable, dot_nt(k[:, cols], q[mine, cols]), -1e9)
                highest = jnp.max(logits, 0, keepdims=True)
                weight = jnp.exp(logits - highest)
                total = jnp.sum(weight, 0, keepdims=True)
                chance = (weight * (1.0 / total)).astype(LOW)
                chance_here[p, h, :, mine] = chance
                some.append(dot_tn(chance, v[:, cols]))
            store(chance_here.at[p, h], chance_out.at[p, h])
            parts.append(jnp.concatenate(some, 0))
        context = jnp.concatenate(parts, 1).astype(LOW)
        own_here[p] = context[:quarter]
        store(own_here.at[p], own_out.at[p])
        for j, out in enumerate((c1, c2, c3)):
            out[p] = context[(j + 1) * quarter : (j + 2) * quarter]
    for copy in stores:
        copy.wait()


def attend(where, lengths, shards, w, bias):
    passages, quarter, width = shards[0].shape
    rows = 4 * quarter
    hw = width // 4
    heads = hw // HD
    kinds = [((passages, rows, 3 * hw), LOW), ((passages, heads, rows, rows), LOW), ((passages, quarter, hw), LOW)]
    whole = ((passages, rows, width), LOW)
    return pl.pallas_call(
        attend_kernel,
        in_specs=[SMEM, SMEM, vmem(), HBM, vmem(), vmem(), HBM, vmem()],
        out_specs=[HBM] * 4 + [vmem()] * 3,
        out_shape=[pltpu.HBM(*kind) for kind in kinds + [whole]] + [jax.ShapeDtypeStruct(*kinds[2])] * 3,
        scratch_shapes=[pltpu.VMEM(*whole), pltpu.VMEM((width, 3 * hw), LOW)]
        + [pltpu.VMEM(*kind) for kind in kinds]
        + [pltpu.SemaphoreType.DMA((4 * passages + 1,)), pltpu.SemaphoreType.DMA((passages * (heads + 3),))],
        compiler_params=pltpu.CompilerParams(vmem_limit_bytes=24 * MIB),
        cost_estimate=cost(FORE),
        name="attend",
    )(where, lengths, shards[0], far(shards[1]), shards[2], shards[3], far(w), bias)


def attend_back_kernel(place, *refs):
    x_hbm, w_hbm, qkv_hbm, chance_hbm, near, near_got, far_got, vectors = refs[:8]
    keep_out, send_out, weight_send, weight_keep, _ = refs[-17:-12]
    x, w, qkv, chance, g, extra_here, joined, back, keep_here, acc, load_sem, store_sem = refs[-12:]
    me = place[1]
    quarter, hw = near.shape[2:]
    rows = 4 * quarter
    heads = hw // HD
    wide = 3 * hw
    scale = HD ** (-0.5)
    made = []

    def load(source, here):
        made.append(pltpu.make_async_copy(source, here, load_sem.at[len(made)]))
        return made[-1]

    needs = []
    for p in range(2):
        mine = [load(qkv_hbm.at[p], qkv.at[p])]
        for j, source in enumerate((near.at[0, p], near_got.at[0, p], far_got.at[0, p], near_got.at[1, p])):
            mine.append(load(source, g.at[p, pl.ds(j * quarter, quarter)]))
        needs.append((mine, [load(chance_hbm.at[p, h], chance.at[p, h]) for h in range(heads)]))
    last = [load(w_hbm, w)]
    late = [load(vectors, extra_here)]
    for p in range(2):
        late.append(load(x_hbm.at[p], x.at[pl.ds(p * rows, rows)]))
    for copy in needs[0][0] + needs[0][1] + last + needs[1][0] + needs[1][1]:
        copy.start()
    stores = []
    sums = [0.0, 0.0]
    for p in range(2):
        for copy in needs[p][0]:
            copy.wait()
        if p == 0:
            for copy in late:
                copy.start()
        grad_q, grad_k, grad_v = [], [], []
        for h in range(heads):
            cols = slice(h * HD, (h + 1) * HD)
            qh, kh, vh = (qkv[p, :, t * hw + h * HD : t * hw + (h + 1) * HD] for t in range(3))
            gh = g[p, :, cols]
            grad_chance = dot_nt(vh, gh)
            needs[p][1][h].wait()
            low = chance[p, h]
            full = low.astype(F32)
            inner = jnp.sum(grad_chance * full, 0, keepdims=True)
            grad_logits = (full * (grad_chance - inner)).astype(LOW)
            grad_q.append(dot_tn(grad_logits, kh) * scale)
            grad_k.append(dot(grad_logits, qh))
            grad_v.append(dot(low, gh))
        some = jnp.concatenate([jnp.concatenate(f, 1).astype(LOW) for f in (grad_q, grad_k, grad_v)], 1)
        joined[p * rows : (p + 1) * rows, :] = some
        sums = [
            total + jnp.sum(some[:, at : at + hw].astype(F32), 0, keepdims=True)
            for total, at in zip(sums, (0, 2 * hw))
        ]
        if p == 0:
            last[0].wait()
        back[p] = dot_nt(some, w[...]).astype(LOW)
        for j in range(4):
            out = send_out if j % 2 else keep_out
            piece = back.at[p, pl.ds(j * quarter, quarter)]
            stores.append(pltpu.make_async_copy(piece, out.at[j // 2, p], store_sem.at[len(stores)]))
            stores[-1].start()
    for copy in late:
        copy.wait()
    acc[:, :wide] = dot_tn(x[...], joined[...])
    spread = []
    for total in sums:
        blank = jnp.zeros_like(total)
        spread.append(jnp.concatenate([jnp.where(me == i, total, blank) for i in range(4)], 1))
    extra = jnp.concatenate([extra_here[:10, :]] + spread + [jnp.zeros((52, extra_here.shape[1]), F32)], 0)
    acc[:, wide:] = extra.T
    half = PIECES // 2
    n = weight_send.shape[2] // 4
    spot = place[0] & half
    for out, first in ((keep_here, spot), (weight_send, spot ^ half)):
        for j in range(4):
            for e in range(half):
                start = pl.multiple_of((me ^ j) * (n * PIECES) + (first + e) * n, 8)
                out[0, e, j * n : (j + 1) * n, :] = acc[pl.ds(start, n), :].astype(LOW)
        if out is keep_here:
            stores.append(pltpu.make_async_copy(keep_here, weight_keep, store_sem.at[len(stores)]))
            stores[-1].start()
    for copy in stores:
        copy.wait()


def attend_back(place, x, w, qkv, chance, grads, vectors, after=()):
    passages, rows, width = x.shape
    quarter = rows // 4
    hw = width // 4
    heads = hw // HD
    n = width // (4 * PIECES)
    weight = ((1, PIECES // 2, 4 * n, 3 * hw + 64), LOW)
    back = ((2, passages, quarter, width), LOW)
    scratch = [
        ((passages * rows, width), LOW), ((width, 3 * hw), LOW), ((passages, rows, 3 * hw), LOW),
        ((passages, heads, rows, rows), LOW), ((passages, rows, hw), LOW), (vectors.shape, F32),
        ((passages * rows, 3 * hw), LOW), ((passages, rows, width), LOW), weight, ((width, 3 * hw + 64), F32),
    ]
    arrays = [x, w, qkv, chance, *grads, vectors]
    return pl.pallas_call(
        attend_back_kernel,
        in_specs=[SMEM] + [HBM] * 5 + [vmem()] + [HBM] * 2 + [HBM] * len(after),
        out_specs=[HBM, HBM, vmem(), HBM, HBM],
        out_shape=[pltpu.HBM(*back), pltpu.HBM(*back), jax.ShapeDtypeStruct(*weight), pltpu.HBM(*weight), TOKEN],
        scratch_shapes=[pltpu.VMEM(*kind) for kind in scratch]
        + [pltpu.SemaphoreType.DMA((passages * (heads + 9) + 2,)), pltpu.SemaphoreType.DMA((4 * passages + 1,))],
        compiler_params=pltpu.CompilerParams(vmem_limit_bytes=32 * MIB),
        cost_estimate=cost(BACK),
        name="attend_back",
    )(place, *map(far, arrays[:5]), arrays[5], *map(far, arrays[6:]), *map(far, after))


def normalise(field):
    centre = field - jnp.mean(field, -1, keepdims=True)
    scale = lax.rsqrt(jnp.mean(centre * centre, -1, keepdims=True) + EPS)
    return centre * scale, scale


def normalise_back(grad, normal, scale):
    return (
        grad
        - jnp.mean(grad, -1, keepdims=True)
        - normal * jnp.mean(grad * normal, -1, keepdims=True)
    ) * scale


def rows_kernel(
    where, x, c0, c1, c2, c3, cot, wa, vec, ib, wi_hbm, wo_hbm,
    layer_out, grad_one_out, active_out, first_out, second_out, left_out, left_send, near_out, sums_out, across_out,
    wi, wo, slope, parts, layer_here, grad_one_here, active_here, first_here, second_here, left_here, near_here,
    sums_here, flipped, load_sem, weight_sem, store_sem, inner_sem,
):
    me = where[0]
    rows, width = x.shape
    chunk = width
    hw = wa.shape[1]
    loads = [pltpu.make_async_copy(f, parts.at[j], load_sem.at[j]) for j, f in enumerate((c0, c1, c2, c3))]
    order = (0, 1, 2, 3)
    weights = []
    for k, c in enumerate(order):
        cols = pl.ds(pl.multiple_of((me ^ c) * chunk, 128), chunk)
        weights.append(pltpu.make_async_copy(wi_hbm.at[:, cols], wi.at[:, cols], weight_sem.at[2 * k]))
        weights.append(pltpu.make_async_copy(wo_hbm.at[cols, :], wo.at[cols, :], weight_sem.at[2 * k + 1]))
    for copy in loads + weights[:2]:
        copy.start()
    stores = [
        pltpu.make_async_copy(here, out, store_sem.at[i])
        for i, (here, out) in enumerate(
            (
                (left_here.at[0], left_out), (left_here.at[1], left_send), (active_here, active_out),
                (first_here, first_out), (layer_here, layer_out), (grad_one_here, grad_one_out),
                (near_here, near_out), (sums_here, sums_out),
            )
        )
    ]
    row = lambda r: vec[r : r + 1, :]
    attn_bias, attn_gain, attn_shift, outer_bias, ffn_gain, ffn_shift = (row(r) for r in range(6))
    sums_here[...] = jnp.zeros_like(sums_here)
    attended = attn_bias + x[...].astype(F32)
    for copy in loads:
        copy.wait()
    for copy in weights[2:4]:
        copy.start()
    for j in range(4):
        attended += dot(parts[j], wa[me ^ j])
    for j in range(4):
        left_here[j & 1, 2 + (j >> 1)] = parts[j].astype(F32).T.astype(LOW)
    normal_one, scale_one = normalise(attended)
    hidden = normal_one * attn_gain + attn_shift
    hidden_low = hidden.astype(LOW)
    flipped[...] = hidden.T
    for j in range(4):
        start = pl.multiple_of((me ^ j) * hw, 64)
        left_here[j & 1, j >> 1] = flipped[pl.ds(start, hw), :].astype(LOW)
    stores[0].start()
    stores[1].start()
    pre_two = hidden + outer_bias
    for k, c in enumerate(order):
        cols = pl.ds(pl.multiple_of((me ^ c) * chunk, 128), chunk)
        for copy in weights[2 * k + 4 : 2 * k + 6]:
            copy.start()
        weights[2 * k].wait()
        u = dot(hidden_low, wi[:, cols]) + ib[:, cols]
        below = 0.5 * (1.0 + lax.erf(u * (0.5**0.5)))
        density = jnp.exp(-0.5 * u * u) * 0.3989422804014327
        active = (u * below).astype(LOW)
        slope[c] = below + u * density
        here = first_here if c & 1 else active_here
        here[:, (c >> 1) * chunk : ((c >> 1) + 1) * chunk] = active
        weights[2 * k + 1].wait()
        pre_two += dot(active, wo[cols, :])
    stores[2].start()
    normal_two, scale_two = normalise(pre_two)
    layer_here[...] = (normal_two * ffn_gain + ffn_shift).astype(LOW)
    stores[4].start()
    dy = cot[...].astype(F32)
    sums_here[4:5, :] = jnp.sum(dy * normal_two, 0, keepdims=True)
    sums_here[5:6, :] = jnp.sum(dy, 0, keepdims=True)
    grad_two = normalise_back(dy * ffn_gain, normal_two, scale_two)
    grad_outer = grad_two.astype(LOW)
    first_here[:, 2 * chunk :] = grad_outer
    stores[3].start()
    sums_here[3:4, :] = jnp.sum(grad_outer.astype(F32), 0, keepdims=True)
    grad_hidden = grad_two
    moved = []
    for c in range(5):
        some = pl.ds(c * chunk, chunk)
        moved.append(pltpu.make_async_copy(second_here.at[:, some], second_out.at[:, some], inner_sem.at[c]))
    for c in range(4):
        cols = slice(c * chunk, (c + 1) * chunk)
        grad_inner = (dot_nt(grad_outer, wo[cols, :]) * slope[me ^ c]).astype(LOW)
        second_here[:, cols] = grad_inner
        moved[c].start()
        column = jnp.sum(grad_inner.astype(F32), 0, keepdims=True)
        for i in range(4):
            sums_here[6 + i : 7 + i, c * hw : (c + 1) * hw] = column[:, i * hw : (i + 1) * hw]
        grad_hidden += dot_nt(grad_inner, wi[:, cols])
    sums_here[1:2, :] = jnp.sum(grad_hidden * normal_one, 0, keepdims=True)
    sums_here[2:3, :] = jnp.sum(grad_hidden, 0, keepdims=True)
    grad_one = normalise_back(grad_hidden * attn_gain, normal_one, scale_one)
    grad_one_here[...] = grad_one
    stores[5].start()
    grad_attn = grad_one.astype(LOW)
    second_here[:, 4 * chunk :] = grad_attn
    moved[4].start()
    for j in range(2):
        near_here[j] = dot_nt(grad_attn, wa[me ^ j]).astype(LOW)
    stores[6].start()
    sums_here[0:1, :] = jnp.sum(grad_attn.astype(F32), 0, keepdims=True)
    stores[7].start()
    for j in range(2):
        across_out[j] = dot_nt(grad_attn, wa[me ^ (j + 2)]).astype(LOW)
    for copy in moved + stores:
        copy.wait()


def rows_pass(where, x, context, cot, wa, vec, ib, wi, wo):
    rows, width = x.shape
    ff = ib.shape[1]
    hw = wa.shape[1]
    kinds = [
        ((rows, width), LOW), ((rows, width), F32), ((rows, 2 * width), LOW), ((rows, 3 * width), LOW),
        ((rows, ff + width), LOW), ((4, hw, rows), LOW), ((4, hw, rows), LOW), ((2, rows, hw), LOW), ((16, width), F32),
    ]
    here = kinds[:5] + [((2, 4, hw, rows), LOW)] + kinds[7:]
    return pl.pallas_call(
        rows_kernel,
        in_specs=[SMEM, vmem()] + [HBM] * 3 + [vmem()] * 5 + [HBM, HBM],
        out_specs=[HBM] * 9 + [vmem()],
        out_shape=[pltpu.HBM(*kind) for kind in kinds] + [jax.ShapeDtypeStruct((2, rows, hw), LOW)],
        scratch_shapes=[
            pltpu.VMEM(wi.shape, LOW),
            pltpu.VMEM(wo.shape, LOW),
            pltpu.VMEM((4, rows, width), F32),
            pltpu.VMEM((4, rows, hw), LOW),
        ]
        + [pltpu.VMEM(*kind) for kind in here]
        + [pltpu.VMEM((width, rows), F32)]
        + [pltpu.SemaphoreType.DMA((n,)) for n in (4, 8, 8, 5)],
        compiler_params=pltpu.CompilerParams(vmem_limit_bytes=36 * MIB),
        cost_estimate=cost(11),
        name="rows_pass",
    )(where, x, *map(far, context[:3]), context[3], cot, wa, vec, ib, far(wi), far(wo))


def outer_grad_kernel(place, active, active_got, grad, grad_got, send_out, keep_out, token):
    half = PIECES // 2
    n = grad.shape[1] // PIECES
    right = jnp.concatenate([grad[...], grad_got[...]], 0)
    product = dot_tn(jnp.concatenate([active[...], active_got[...]], 0), right)

    def store(low_out, high_out):
        for e in range(PIECES):
            out = high_out if e >= half else low_out
            out[0, e % half] = product[e * n : (e + 1) * n].astype(LOW)

    high = (place[0] & half) > 0
    pl.when(high)(lambda: store(send_out, keep_out))
    pl.when(jnp.logical_not(high))(lambda: store(keep_out, send_out))


def outer_grad(place, active, first, first_got):
    rows, width = first.shape
    width //= 3
    block = (1, PIECES // 2, width // PIECES, width)
    side = vmem((rows, width), lambda y: (0, y))
    last = vmem((rows, width), lambda y: (0, 2))
    return pl.pallas_call(
        outer_grad_kernel,
        grid=(2,),
        in_specs=[SMEM, side, side, last, last],
        out_specs=[vmem(block, lambda y: (y, 0, 0, 0))] * 2 + [HBM],
        out_shape=[jax.ShapeDtypeStruct((2,) + block[1:], LOW)] * 2 + [TOKEN],
        compiler_params=pltpu.CompilerParams(vmem_limit_bytes=16 * MIB),
        cost_estimate=cost(30),
        name="outer_grad",
    )(place, far(active), first_got, far(first), first_got)


SPLIT = 128
ORDERS = {
    "a": ([1, "y", 2], 4, [2, 1]),
    "b": (["y", 2, 1], 4, [2, 1]),
    "c": ([2, 1, "y"], 4, [1, 2]),
    "d": ([1, 4], 2, [1, 4]),
}
SEQUENCE = "abcdbacbdacbdedbcadca"


def inner_grad_kernel(bit_b, bit_c, mine_hbm, second_hbm, mine_got, second_got, *refs):
    outs, (mine, second, left, rest, *heres, load_sem, store_sem) = refs[-13:-9], refs[-8:]
    hw, rows = mine.shape[1:]
    width = 4 * hw
    half = PIECES // 2
    n = hw // PIECES
    cols = width // 2
    loads = [pltpu.make_async_copy(mine_hbm, mine, load_sem.at[5])]
    for c in (4, 0, 1, 2, 3):
        some = pl.ds(c * width, width)
        loads.append(pltpu.make_async_copy(second_hbm.at[:, some], second.at[:, some], load_sem.at[c]))
    for copy in loads:
        copy.start()
    for copy in loads[:2]:
        copy.wait()
    grads = jnp.concatenate([second[:, 4 * width :], second_got[:, 4 * width :]], 0)
    for y in range(2):
        left[y * hw : (y + 1) * hw, :rows] = mine[y]
        left[y * hw : (y + 1) * hw, rows:] = mine_got[y]
        rest[y] = dot(jnp.concatenate([mine[2 + y], mine_got[2 + y]], 1), grads)
    waits = []

    def send(part, piece, y, at, keep):
        here = heres[part]
        out = outs[2 * part + 1] if keep else outs[2 * part]
        spot = (part * PIECES + piece) * 2 + y
        copy = pltpu.make_async_copy(here.at[y, piece], out.at[at[0], at[1]], store_sem.at[spot])
        copy.start()
        return copy

    for c in range(4):
        loads[2 + c].wait()
        here = slice(c * width, (c + 1) * width)
        product = dot(left[...], jnp.concatenate([second[:, here], second_got[:, here]], 0))
        for k in range(2):
            piece = 2 * c + k
            for y in range(2):
                some = product[y * hw : (y + 1) * hw, k * cols : (k + 1) * cols]
                heres[0][y, piece] = some[:SPLIT].astype(LOW)
                more = rest[y, piece * n : (piece + 1) * n, :]
                more = jnp.concatenate([some[SPLIT:], more[:, :cols], more[:, cols:]], 0)
                heres[1][y, piece] = more.astype(LOW)
        for part, (which, bit) in enumerate((("b", bit_b), ("c", bit_c))):
            both = [(2 * c + k, y) for k in range(2) for y in range(2)]
            if ORDERS[which][0][0] == "y":
                for piece, y in both:
                    waits.append(send(part, piece, y, (0, piece), y == 0))
            else:
                kept = (bit[0] & half) == (c >> 1) * half
                for here, keep in ((kept, True), (jnp.logical_not(kept), False)):

                    @pl.when(here)
                    def _(part=part, both=both, keep=keep):
                        for piece, y in both:
                            send(part, piece, y, (y, piece % half), keep)

                for piece, y in both:
                    spot = (part * PIECES + piece) * 2 + y
                    out = outs[2 * part].at[y, piece % half]
                    waits.append(pltpu.make_async_copy(heres[part].at[y, piece], out, store_sem.at[spot]))
    for copy in waits:
        copy.wait()


def inner_grad(places, mine, mine_got, second, second_got, after):
    hw = mine.shape[1]
    width = 4 * hw
    half = PIECES // 2
    counts = [(1, PIECES) if ORDERS[which][0][0] == "y" else (2, half) for which in "bc"]
    talls = [SPLIT, hw - SPLIT + 2 * hw // PIECES]
    shapes = [count + (tall, width // 2) for count, tall in zip(counts, talls)]
    return pl.pallas_call(
        inner_grad_kernel,
        in_specs=[SMEM, SMEM, HBM, HBM, vmem(), vmem()] + [HBM] * len(after),
        out_specs=[HBM] * 5,
        out_shape=[pltpu.HBM(shape, LOW) for shape in shapes for _ in range(2)] + [TOKEN],
        scratch_shapes=[
            pltpu.VMEM(mine.shape, LOW),
            pltpu.VMEM(second.shape, LOW),
            pltpu.VMEM((2 * hw, 2 * mine.shape[2]), LOW),
            pltpu.VMEM((2, hw, width), F32),
        ]
        + [pltpu.VMEM((2, PIECES, tall, width // 2), LOW) for tall in talls]
        + [pltpu.SemaphoreType.DMA((6,)), pltpu.SemaphoreType.DMA((4 * PIECES,))],
        compiler_params=pltpu.CompilerParams(vmem_limit_bytes=20 * MIB),
        cost_estimate=cost(4),
        name="inner_grad",
    )(*places, far(mine), far(second), mine_got, second_got, *map(far, after))


ANYWHERE = pl.BlockSpec(memory_space=pl.ANY)


def sum_kernel(spec, place, *refs):
    leads, count, flip, inputs, splits = spec
    ins = refs[: len(inputs)]
    outs = refs[-1 - splits : -1]
    first = (place[0] // count) * count
    if flip:
        first = first ^ count
    for y, lead in enumerate(leads):
        for r in range(count):
            total = None
            for ref in ins:
                pieces = ref.shape[1]
                base = first & (pieces - 1) if count < pieces else 0
                term = ref[lead if ref.shape[0] > 1 else 0, base + r].astype(F32)
                total = term if total is None else total + term
            if splits == 1:
                outs[0][y, r] = total.astype(LOW)
            else:
                n = total.shape[0] // splits
                for j in range(splits):
                    outs[j][r] = total[j * n : (j + 1) * n].astype(LOW)


def sum_pieces(place, inputs, leads, count, flip, after=(), splits=1, name="sum_pieces"):
    tall, wide = inputs[0].shape[2:]
    spec = (tuple(leads), count, flip, tuple(range(len(inputs))), splits)
    if splits == 1:
        out_shape = [jax.ShapeDtypeStruct((len(leads), count, tall, wide), LOW)]
    else:
        out_shape = [jax.ShapeDtypeStruct((count, tall // splits, wide), LOW)] * splits
    return pl.pallas_call(
        lambda *refs: sum_kernel(spec, *refs),
        in_specs=[SMEM] + [vmem()] * len(inputs) + [HBM] * len(after),
        out_specs=[vmem()] * splits + [HBM],
        out_shape=out_shape + [TOKEN],
        compiler_params=pltpu.CompilerParams(vmem_limit_bytes=4 * MIB),
        cost_estimate=cost(STEP),
        name=name,
    )(place, *inputs, *map(far, after))


def outer_place_kernel(spots, place, own, got, *refs):
    out = refs[-1]
    n = own.shape[1]
    for i, spot in enumerate(spots):
        piece = own[i] if i < 4 else got[i - 4]
        out[pl.ds(pl.multiple_of((place[0] ^ spot) * n, 8), n), :] = piece.astype(F32)


def outer_place(spots, place, own, got, after=()):
    n, width = own.shape[1:]
    return pl.pallas_call(
        lambda *refs: outer_place_kernel(spots, *refs),
        in_specs=[SMEM, vmem(), vmem()] + [HBM] * len(after),
        out_specs=vmem(),
        out_shape=jax.ShapeDtypeStruct((PIECES * n, width), F32),
        compiler_params=pltpu.CompilerParams(vmem_limit_bytes=4 * MIB),
        cost_estimate=cost(2),
        name="outer_place",
    )(place, own, got, *map(far, after))


def inner_place_kernel(spots_one, spots_two, one, two, own, got, own_two, got_two, *refs):
    inner, attn = refs[-2:]
    hw, cols = inner.shape[0], own.shape[2]
    n = attn.shape[0] // PIECES
    for i in range(PIECES):
        piece = (own[i] if i < 4 else got[i - 4]).astype(F32)
        here = one[0] ^ spots_one[i]
        inner[:SPLIT, pl.ds(pl.multiple_of(here * cols, 128), cols)] = piece
        piece = (own_two[i] if i < 4 else got_two[i - 4]).astype(F32)
        here = two[0] ^ spots_two[i]
        some = hw - SPLIT
        inner[SPLIT:, pl.ds(pl.multiple_of(here * cols, 128), cols)] = piece[:some]
        more = jnp.concatenate([piece[some : some + n], piece[some + n :]], 1)
        attn[pl.ds(pl.multiple_of(here * n, 8), n), :] = more


def inner_place(spots_one, spots_two, one, two, parts_one, parts_two, hw, after=()):
    cols = parts_one[0].shape[2]
    n = hw // PIECES
    return pl.pallas_call(
        lambda *refs: inner_place_kernel(spots_one, spots_two, *refs),
        in_specs=[SMEM, SMEM] + [vmem()] * 4 + [HBM] * len(after),
        out_specs=[vmem(), vmem()],
        out_shape=[
            jax.ShapeDtypeStruct((hw, PIECES * cols), F32),
            jax.ShapeDtypeStruct((PIECES * n, 2 * cols), F32),
        ],
        compiler_params=pltpu.CompilerParams(vmem_limit_bytes=4 * MIB),
        cost_estimate=cost(2),
        name="inner_place",
    )(one, two, *parts_one, *parts_two, *map(far, after))


def project_place_kernel(spots, place, own, got, *refs):
    out, vectors, tall = refs[-3:]
    n = own.shape[1] // 4
    hw = out.shape[1] // 12
    wide = 3 * hw
    for i, spot in enumerate(spots):
        ref, k = (own, i) if i < 4 else (got, i - 4)
        rows = pl.ds(pl.multiple_of((place[0] ^ spot) * n, 8), n)
        total = None
        for owner in range(4):
            start = pl.multiple_of((owner ^ place[1]) * n, 8)
            block = ref[k, pl.ds(start, n), :].astype(F32)
            for t in range(3):
                at = t * 4 * hw + owner * hw
                out[rows, at : at + hw] = block[:, t * hw : (t + 1) * hw]
            extra = block[:, wide:]
            total = extra if total is None else total + extra
        tall[rows, : total.shape[1]] = total
    vectors[...] = tall[...].T[: vectors.shape[0]]


def project_place(spots, place, own, got, hw, after=()):
    _, tall, wide = own.shape
    n = tall // 4
    return pl.pallas_call(
        lambda *refs: project_place_kernel(spots, *refs),
        in_specs=[SMEM, vmem(), vmem()] + [HBM] * len(after),
        out_specs=[vmem(), vmem()],
        out_shape=[
            jax.ShapeDtypeStruct((PIECES * n, 12 * hw), F32),
            jax.ShapeDtypeStruct((16, PIECES * n), F32),
        ],
        scratch_shapes=[pltpu.VMEM((PIECES * n, 128), F32)],
        compiler_params=pltpu.CompilerParams(vmem_limit_bytes=4 * MIB),
        cost_estimate=cost(2),
        name="project_place",
    )(place, own, got, *map(far, after))


def join_kernel(*refs):
    out, token, sem = refs[-3:]
    own, got = refs[:2]
    n = own.shape[0]
    copies = [pltpu.make_async_copy(f, out.at[pl.ds(i * n, n)], sem.at[i]) for i, f in enumerate((own, got))]
    for copy in copies:
        copy.start()
    for copy in copies:
        copy.wait()


def join(own, got, after):
    shape = (2 * own.shape[0],) + own.shape[1:]
    return pl.pallas_call(
        join_kernel,
        in_specs=[ANYWHERE] * 2 + [HBM] * len(after),
        out_specs=[ANYWHERE, HBM],
        out_shape=[jax.ShapeDtypeStruct(shape, own.dtype), TOKEN],
        scratch_shapes=[pltpu.SemaphoreType.DMA((2,))],
        compiler_params=pltpu.CompilerParams(vmem_limit_bytes=2 * MIB),
        cost_estimate=cost(JOIN),
        name="join",
    )(own, got, *map(far, after))


def pass_on_kernel(source, *refs):
    out, sem = refs[-2:]
    copy = pltpu.make_async_copy(source, out, sem.at[0])
    copy.start()
    copy.wait()


def pass_on(source, after):
    return pl.pallas_call(
        pass_on_kernel,
        in_specs=[vmem()] + [HBM] * len(after),
        out_specs=vmem(),
        out_shape=jax.ShapeDtypeStruct(source.shape, source.dtype),
        scratch_shapes=[pltpu.SemaphoreType.DMA((1,))],
        compiler_params=pltpu.CompilerParams(vmem_limit_bytes=2 * MIB),
        cost_estimate=cost(0.5),
        name="pass_on",
    )(source, *map(far, after))


def pair_kernel(near, far, *refs):
    out, token, sem = refs[-3:]
    copies = [pltpu.make_async_copy(f.at[1], out.at[i], sem.at[i]) for i, f in enumerate((near, far))]
    for copy in copies:
        copy.start()
    for copy in copies:
        copy.wait()


def pair(near, far_got, after):
    return pl.pallas_call(
        pair_kernel,
        in_specs=[ANYWHERE] * 2 + [HBM] * len(after),
        out_specs=[ANYWHERE, HBM],
        out_shape=[jax.ShapeDtypeStruct(near.shape, near.dtype), TOKEN],
        scratch_shapes=[pltpu.SemaphoreType.DMA((2,))],
        compiler_params=pltpu.CompilerParams(vmem_limit_bytes=2 * MIB),
        cost_estimate=cost(0.5),
        name="pair",
    )(near, far_got, *map(far, after))


def swap(field, axis, bit):
    count = lax.axis_size(axis)
    return lax.ppermute(field, axis, [(i, i ^ bit) for i in range(count)])


def add(left, right):
    return (left.astype(F32) + right.astype(F32)).astype(LOW)


class Reduction:
    def __init__(self, order, last, back, lane, me, rest):
        self.order = list(order)
        self.last = last
        self.back = list(back)
        self.rest = rest
        bits = [o for o in order if o != "y"]
        weight = {bit: PIECES >> (k + 1) for k, bit in enumerate(bits)}
        spot = sum(jnp.where(lane & bit, w, 0) for bit, w in weight.items())
        weight[last] = 0
        self.spots = [
            i % 2 + sum(weight[bit] for t, bit in enumerate(back) if i >> (t + 1) & 1) for i in range(PIECES)
        ]
        self.own = None
        self.place = jnp.stack([spot.astype(jnp.int32), me.astype(jnp.int32)])

    def begin(self, keep, send):
        axis = self.order.pop(0)
        got = swap(send, "seq", 2) if axis == "y" else swap(send, "dp", axis)
        self.arrays = [keep, got]
        self.left = keep.shape[1]
        self.folded = keep.shape[0] == 1

    def step(self, after=(), splits=1, name="sum"):
        if not self.order and self.last is None:
            return sum_pieces(self.place, self.arrays, [0], self.left, False, after, splits, name)
        leads = [0] if self.folded else [0, 1]
        if not self.order:
            sent, token = sum_pieces(self.place, self.arrays, [0], self.left, False, after, name=name)
            self.arrays = [sent, swap(sent, "dp", self.last)]
            self.last = None
            return token
        axis = self.order.pop(0)
        if axis == "y":
            sent, token = sum_pieces(self.place, self.arrays, [1], self.left, False, after, name=name)
            self.folded = True
            got = swap(sent, "seq", 2)
        else:
            self.left //= 2
            sent, token = sum_pieces(self.place, self.arrays, leads, self.left, True, after, name=name)
            got = swap(sent, "dp", axis)
        self.arrays = self.arrays + [got]
        return token

    def start(self, piece):
        for bit in self.rest:
            piece = add(piece, swap(piece, "dp", bit))
        self.own = piece
        self.got = swap(piece, "dp", self.back[0])
        self.done = 1

    def grow(self, after):
        self.own, token = join(self.own, self.got, after)
        self.got = swap(self.own, "dp", self.back[self.done])
        self.done += 1
        return token


def local(
    tokens, lengths, query_key_value, query_bias, value_bias, attn_weight, attn_bias, attn_gain,
    attn_shift, inner_weight, inner_bias, outer_weight, outer_bias, ffn_gain, ffn_shift, cotangent,
):
    groups = lax.axis_size("seq")
    lanes = lax.axis_size("dp")
    me = lax.axis_index("seq")
    lane = lax.axis_index("dp")
    passages, quarter, width = tokens.shape
    hw = H // groups * HD
    rows = passages * quarter
    ff = inner_bias.shape[0]
    rest = [1 << i for i in range(3, lanes.bit_length() - 1)]
    where = me.astype(jnp.int32).reshape(1)

    across = swap(tokens, "seq", 2)
    beside = swap(tokens, "seq", 1)
    biases = (query_bias.reshape(1, width), value_bias.reshape(1, width))
    w, bias, token = choose_heads(where, query_key_value, *biases)
    across = pass_on(across, [token])
    corner = swap(across, "seq", 1)
    shards = (tokens, beside, across, corner)
    vec = jnp.stack([attn_bias, attn_gain, attn_shift, outer_bias, ffn_gain, ffn_shift, ffn_shift, ffn_shift])
    vec = vec.astype(F32)
    ib = inner_bias.astype(F32).reshape(1, ff)

    qkv, chance, own, x_all, *context_h = attend(where, lengths, shards, w, bias)
    context = [own] + [swap(part, "seq", j) for j, part in zip((1, 2, 3), context_h)]
    context = [part.reshape(rows, hw) for part in context]

    wa = attn_weight.reshape(groups, hw, width)
    layer_out, grad_one, active, first, second, mine, mine_send, near, vectors, across_heads = rows_pass(
        where, tokens.reshape(rows, width), context, cotangent.reshape(rows, width), wa, vec, ib, inner_weight,
        outer_weight,
    )
    first_got = swap(first, "seq", 1)
    second_got = swap(second, "seq", 1)
    mine_got = swap(mine_send, "seq", 1)
    a, b, c, d = (Reduction(*ORDERS[which], lane, me, rest) for which in "abcd")
    far_got = swap(across_heads, "seq", 2)
    outer_send, outer_keep, token = outer_grad(a.place, active, first, first_got)
    near_send, paired = pair(near, far_got, [token])
    near_got = swap(near_send, "seq", 1)
    a.begin(outer_keep, outer_send)
    first_send, first_keep, second_send, second_keep, token = inner_grad(
        [b.place, c.place], mine, mine_got, second, second_got, [paired]
    )
    b.begin(first_keep, first_send)
    c.begin(second_keep, second_send)
    grads_h = [f.reshape(2, passages, quarter, hw) for f in (near, near_got, far_got)]
    back_keep, back_send, project_send, project_keep, token = attend_back(
        d.place, x_all, w, qkv, chance, grads_h, vectors, [token]
    )
    d.begin(project_keep, project_send)
    back_got = swap(back_send, "seq", 1)

    def begin_back(after):
        total, token = sum_pieces(
            d.place,
            [f.reshape(2, 1, rows, width) for f in (back_keep, back_got)],
            [1], 1, False, after, name="back_y",
        )
        return swap(total, "seq", 2), token

    if "e" not in SEQUENCE:
        back_over, _ = begin_back([])
    parts = None
    for letter in SEQUENCE:
        if letter == "e":
            back_over, token = begin_back([token])
            continue
        chunk = {"a": a, "b": b, "c": c, "d": d}[letter]
        if chunk.order or chunk.last is not None:
            token = chunk.step([token], name="sum_" + letter)
        elif chunk.own is not None:
            token = chunk.grow([token])
        elif chunk is d and parts is None:
            *parts, token = d.step([token], splits=4, name="total_d")
            parts = [parts[0]] + [swap(parts[j], "seq", j) for j in (1, 2, 3)]
        elif chunk is d:
            d.start(jnp.concatenate(parts, 1))
        else:
            total, token = chunk.step([token], name="total_" + letter)
            chunk.start(total[0])
    grad_query_key_value, summed = project_place(d.spots, d.place, d.own, d.got, hw)
    grad_outer_weight = outer_place(a.spots, a.place, a.own, a.got)
    grad_inner_weight, grad_attn_weight = inner_place(
        b.spots, c.spots, b.place, c.place, (b.own, b.got), (c.own, c.got), hw
    )
    input_grad = (
        grad_one + back_keep[0].reshape(rows, width).astype(F32)
        + back_got[0].reshape(rows, width).astype(F32)
        + back_over[0, 0].astype(F32)
    ).astype(LOW)
    return (
        layer_out.reshape(passages, quarter, width),
        input_grad.reshape(passages, quarter, width),
        grad_query_key_value,
        summed[10],
        summed[11],
        grad_attn_weight,
        summed[0],
        summed[1],
        summed[2],
        grad_inner_weight,
        summed[6:10].reshape(-1),
        grad_outer_weight,
        summed[3],
        summed[4],
        summed[5],
    )


def solution(mesh):
    rows = P("dp", "seq", None)
    return jax.shard_map(
        local,
        mesh=mesh,
        in_specs=(rows, P("dp")) + (P(),) * 13 + (rows,),
        out_specs=(
            rows,
            rows,
            P("seq", None),
            P("seq"),
            P("seq"),
            P("seq", None),
            P("seq"),
            P("seq"),
            P("seq"),
            P("seq", None),
            P("seq"),
            P("seq", None),
            P("seq"),
            P("seq"),
            P("seq"),
        ),
        check_vma=False,
    )
```

```python
import jax
import jax.numpy as jnp
from jax import lax
from jax.experimental import pallas as pl
from jax.experimental.pallas import tpu as pltpu
from jax.sharding import PartitionSpec as P

H = 12
HD = 64
EPS = 1e-12
F32 = jnp.float32
LOW = jnp.bfloat16
MIB = 1 << 20
PIECES = 8
STEP = 0.85
JOIN = 1.3
BACK = 1.0
FORE = 0.1


def cost(us):
    return pl.CostEstimate(flops=int(us * 1.15e9), bytes_accessed=int(us * 3.69e6), transcendentals=0)


def dot(a, b):
    return lax.dot_general(a, b, (((1,), (0,)), ((), ())), preferred_element_type=F32)


def dot_nt(a, b):
    return lax.dot_general(a, b, (((1,), (1,)), ((), ())), preferred_element_type=F32)


def dot_tn(a, b):
    return lax.dot_general(a, b, (((0,), (0,)), ((), ())), preferred_element_type=F32)


def vmem(shape=None, index=None):
    if shape is None:
        return pl.BlockSpec(memory_space=pltpu.VMEM)
    return pl.BlockSpec(shape, index)


SMEM = pl.BlockSpec(memory_space=pltpu.SMEM)
HBM = pl.BlockSpec(memory_space=pltpu.HBM)


TOKEN = pltpu.HBM((8, 128), jnp.float32)


def far(array):
    return pltpu.with_memory_space_constraint(array, pltpu.HBM)


def key_mask(me, length, rows, quarter):
    slot = lax.broadcasted_iota(jnp.int32, (rows, 1), 0)
    block = slot // quarter
    return ((block ^ me) * quarter + (slot - block * quarter)) < length


BLOCK = 128


def choose_kernel(where, w_hbm, qb, vb, w_out, bias_out, token, wide, w_here, sem):
    me = where[0]
    hw = bias_out.shape[1]
    width = wide.shape[1]
    window = wide.shape[2]
    first = pl.multiple_of(me * hw - (me & 1) * HD, 128)
    choose = lambda f: jnp.where((me & 1) == 1, f[:, HD : HD + hw], f[:, :hw])
    copies = []
    for t in range(3):
        at = pl.ds(pl.multiple_of(t * width + first, 128), window)
        copies.append(pltpu.make_async_copy(w_hbm.at[:, at], wide.at[t], sem.at[t]))
        copies[t].start()
    for i, bias in enumerate((qb, vb)):
        bias_out[i : i + 1, :] = choose(bias[:, pl.ds(first, window)].astype(F32))
    for t in range(3):
        copies[t].wait()
        w_here[:, t * hw : (t + 1) * hw] = choose(wide[t])
    copy = pltpu.make_async_copy(w_here, w_out, sem.at[3])
    copy.start()
    copy.wait()


def choose_heads(where, w, qb, vb):
    width = w.shape[0]
    hw = width // 4
    return pl.pallas_call(
        choose_kernel,
        in_specs=[SMEM, HBM, vmem(), vmem()],
        out_specs=[HBM, vmem(), HBM],
        out_shape=[pltpu.HBM((width, 3 * hw), LOW), jax.ShapeDtypeStruct((2, hw), F32), TOKEN],
        scratch_shapes=[
            pltpu.VMEM((3, width, hw + HD), LOW),
            pltpu.VMEM((width, 3 * hw), LOW),
            pltpu.SemaphoreType.DMA((4,)),
        ],
        compiler_params=pltpu.CompilerParams(vmem_limit_bytes=6 * MIB),
        cost_estimate=cost(1.5),
        name="choose_heads",
    )(where, far(w), qb, vb)


def attend_kernel(where, lengths, x0, x1, x2, x3, w_hbm, bias, *refs):
    qkv_out, chance_out, own_out, x_out, c1, c2, c3 = refs[:7]
    x, w, qkv_here, chance_here, own_here, load_sem, store_sem = refs[7:]
    me = where[0]
    passages, quarter, width = x0.shape
    rows = 4 * quarter
    hw = w.shape[1] // 3
    heads = hw // HD
    loads = [pltpu.make_async_copy(w_hbm, w, load_sem.at[4 * passages])]
    for p in range(passages):
        for j, shard in enumerate((x0, x1, x2, x3)):
            here = x.at[p, pl.ds(j * quarter, quarter)]
            loads.append(pltpu.make_async_copy(shard.at[p], here, load_sem.at[p * 4 + j]))
    for copy in loads:
        copy.start()
    loads[0].wait()
    stores = []

    def store(here, out):
        stores.append(pltpu.make_async_copy(here, out, store_sem.at[len(stores)]))
        stores[-1].start()

    for p in range(passages):
        for copy in loads[1 + 4 * p : 5 + 4 * p]:
            copy.wait()
        store(x.at[p], x_out.at[p])
        proj = dot(x[p], w[...])
        q = ((proj[:, :hw] + bias[0:1, :]).astype(LOW).astype(F32) * HD ** (-0.5)).astype(LOW)
        k = proj[:, hw : 2 * hw].astype(LOW)
        v = (proj[:, 2 * hw :] + bias[1:2, :]).astype(LOW)
        qkv_here[p] = jnp.concatenate([q, k, v], 1)
        store(qkv_here.at[p], qkv_out.at[p])
        usable = key_mask(me, lengths[p], rows, quarter)
        parts = []
        for h in range(heads):
            cols = slice(h * HD, (h + 1) * HD)
            some = []
            for b in range(rows // BLOCK):
                mine = slice(b * BLOCK, (b + 1) * BLOCK)
                logits = jnp.where(usable, dot_nt(k[:, cols], q[mine, cols]), -1e9)
                highest = jnp.max(logits, 0, keepdims=True)
                weight = jnp.exp(logits - highest)
                total = jnp.sum(weight, 0, keepdims=True)
                chance = (weight * (1.0 / total)).astype(LOW)
                chance_here[p, h, :, mine] = chance
                some.append(dot_tn(chance, v[:, cols]))
            store(chance_here.at[p, h], chance_out.at[p, h])
            parts.append(jnp.concatenate(some, 0))
        context = jnp.concatenate(parts, 1).astype(LOW)
        own_here[p] = context[:quarter]
        store(own_here.at[p], own_out.at[p])
        for j, out in enumerate((c1, c2, c3)):
            out[p] = context[(j + 1) * quarter : (j + 2) * quarter]
    for copy in stores:
        copy.wait()


def attend(where, lengths, shards, w, bias):
    passages, quarter, width = shards[0].shape
    rows = 4 * quarter
    hw = width // 4
    heads = hw // HD
    kinds = [((passages, rows, 3 * hw), LOW), ((passages, heads, rows, rows), LOW), ((passages, quarter, hw), LOW)]
    whole = ((passages, rows, width), LOW)
    return pl.pallas_call(
        attend_kernel,
        in_specs=[SMEM, SMEM, vmem(), HBM, vmem(), vmem(), HBM, vmem()],
        out_specs=[HBM] * 4 + [vmem()] * 3,
        out_shape=[pltpu.HBM(*kind) for kind in kinds + [whole]] + [jax.ShapeDtypeStruct(*kinds[2])] * 3,
        scratch_shapes=[pltpu.VMEM(*whole), pltpu.VMEM((width, 3 * hw), LOW)]
        + [pltpu.VMEM(*kind) for kind in kinds]
        + [pltpu.SemaphoreType.DMA((4 * passages + 1,)), pltpu.SemaphoreType.DMA((passages * (heads + 3),))],
        compiler_params=pltpu.CompilerParams(vmem_limit_bytes=24 * MIB),
        cost_estimate=cost(FORE),
        name="attend",
    )(where, lengths, shards[0], far(shards[1]), shards[2], shards[3], far(w), bias)


def attend_back_kernel(place, *refs):
    x_hbm, w_hbm, qkv_hbm, chance_hbm, near, near_got, far_got, vectors = refs[:8]
    keep_out, send_out, weight_send, weight_keep, _ = refs[-17:-12]
    x, w, qkv, chance, g, extra_here, joined, back, keep_here, acc, load_sem, store_sem = refs[-12:]
    me = place[1]
    quarter, hw = near.shape[2:]
    rows = 4 * quarter
    heads = hw // HD
    wide = 3 * hw
    scale = HD ** (-0.5)
    made = []

    def load(source, here):
        made.append(pltpu.make_async_copy(source, here, load_sem.at[len(made)]))
        return made[-1]

    needs = []
    for p in range(2):
        mine = [load(qkv_hbm.at[p], qkv.at[p])]
        for j, source in enumerate((near.at[0, p], near_got.at[0, p], far_got.at[0, p], near_got.at[1, p])):
            mine.append(load(source, g.at[p, pl.ds(j * quarter, quarter)]))
        needs.append((mine, [load(chance_hbm.at[p, h], chance.at[p, h]) for h in range(heads)]))
    last = [load(w_hbm, w)]
    late = [load(vectors, extra_here)]
    for p in range(2):
        late.append(load(x_hbm.at[p], x.at[pl.ds(p * rows, rows)]))
    for copy in needs[0][0] + needs[0][1] + last + needs[1][0] + needs[1][1]:
        copy.start()
    stores = []
    sums = [0.0, 0.0]
    for p in range(2):
        for copy in needs[p][0]:
            copy.wait()
        if p == 0:
            for copy in late:
                copy.start()
        grad_q, grad_k, grad_v = [], [], []
        for h in range(heads):
            cols = slice(h * HD, (h + 1) * HD)
            qh, kh, vh = (qkv[p, :, t * hw + h * HD : t * hw + (h + 1) * HD] for t in range(3))
            gh = g[p, :, cols]
            grad_chance = dot_nt(vh, gh)
            needs[p][1][h].wait()
            low = chance[p, h]
            full = low.astype(F32)
            inner = jnp.sum(grad_chance * full, 0, keepdims=True)
            grad_logits = (full * (grad_chance - inner)).astype(LOW)
            grad_q.append(dot_tn(grad_logits, kh) * scale)
            grad_k.append(dot(grad_logits, qh))
            grad_v.append(dot(low, gh))
        some = jnp.concatenate([jnp.concatenate(f, 1).astype(LOW) for f in (grad_q, grad_k, grad_v)], 1)
        joined[p * rows : (p + 1) * rows, :] = some
        sums = [
            total + jnp.sum(some[:, at : at + hw].astype(F32), 0, keepdims=True)
            for total, at in zip(sums, (0, 2 * hw))
        ]
        if p == 0:
            last[0].wait()
        back[p] = dot_nt(some, w[...]).astype(LOW)
        for j in range(4):
            out = send_out if j % 2 else keep_out
            piece = back.at[p, pl.ds(j * quarter, quarter)]
            stores.append(pltpu.make_async_copy(piece, out.at[j // 2, p], store_sem.at[len(stores)]))
            stores[-1].start()
    for copy in late:
        copy.wait()
    acc[:, :wide] = dot_tn(x[...], joined[...])
    spread = []
    for total in sums:
        blank = jnp.zeros_like(total)
        spread.append(jnp.concatenate([jnp.where(me == i, total, blank) for i in range(4)], 1))
    extra = jnp.concatenate([extra_here[:10, :]] + spread + [jnp.zeros((52, extra_here.shape[1]), F32)], 0)
    acc[:, wide:] = extra.T
    half = PIECES // 2
    n = weight_send.shape[2] // 4
    spot = place[0] & half
    for out, first in ((keep_here, spot), (weight_send, spot ^ half)):
        for j in range(4):
            for e in range(half):
                start = pl.multiple_of((me ^ j) * (n * PIECES) + (first + e) * n, 8)
                out[0, e, j * n : (j + 1) * n, :] = acc[pl.ds(start, n), :].astype(LOW)
        if out is keep_here:
            stores.append(pltpu.make_async_copy(keep_here, weight_keep, store_sem.at[len(stores)]))
            stores[-1].start()
    for copy in stores:
        copy.wait()


def attend_back(place, x, w, qkv, chance, grads, vectors, after=()):
    passages, rows, width = x.shape
    quarter = rows // 4
    hw = width // 4
    heads = hw // HD
    n = width // (4 * PIECES)
    weight = ((1, PIECES // 2, 4 * n, 3 * hw + 64), LOW)
    back = ((2, passages, quarter, width), LOW)
    scratch = [
        ((passages * rows, width), LOW), ((width, 3 * hw), LOW), ((passages, rows, 3 * hw), LOW),
        ((passages, heads, rows, rows), LOW), ((passages, rows, hw), LOW), (vectors.shape, F32),
        ((passages * rows, 3 * hw), LOW), ((passages, rows, width), LOW), weight, ((width, 3 * hw + 64), F32),
    ]
    arrays = [x, w, qkv, chance, *grads, vectors]
    return pl.pallas_call(
        attend_back_kernel,
        in_specs=[SMEM] + [HBM] * 5 + [vmem()] + [HBM] * 2 + [HBM] * len(after),
        out_specs=[HBM, HBM, vmem(), HBM, HBM],
        out_shape=[pltpu.HBM(*back), pltpu.HBM(*back), jax.ShapeDtypeStruct(*weight), pltpu.HBM(*weight), TOKEN],
        scratch_shapes=[pltpu.VMEM(*kind) for kind in scratch]
        + [pltpu.SemaphoreType.DMA((passages * (heads + 9) + 2,)), pltpu.SemaphoreType.DMA((4 * passages + 1,))],
        compiler_params=pltpu.CompilerParams(vmem_limit_bytes=32 * MIB),
        cost_estimate=cost(BACK),
        name="attend_back",
    )(place, *map(far, arrays[:5]), arrays[5], *map(far, arrays[6:]), *map(far, after))


def normalise(field):
    centre = field - jnp.mean(field, -1, keepdims=True)
    scale = lax.rsqrt(jnp.mean(centre * centre, -1, keepdims=True) + EPS)
    return centre * scale, scale


def normalise_back(grad, normal, scale):
    return (
        grad
        - jnp.mean(grad, -1, keepdims=True)
        - normal * jnp.mean(grad * normal, -1, keepdims=True)
    ) * scale


def rows_kernel(
    where, x, c0, c1, c2, c3, cot, wa, vec, ib, wi_hbm, wo_hbm,
    layer_out, grad_one_out, active_out, first_out, second_out, left_out, left_send, near_out, sums_out, across_out,
    wi, wo, slope, parts, layer_here, grad_one_here, active_here, first_here, second_here, left_here, near_here,
    sums_here, flipped, load_sem, weight_sem, store_sem, inner_sem,
):
    me = where[0]
    rows, width = x.shape
    chunk = width
    hw = wa.shape[1]
    loads = [pltpu.make_async_copy(f, parts.at[j], load_sem.at[j]) for j, f in enumerate((c0, c1, c2, c3))]
    order = (0, 1, 2, 3)
    weights = []
    for k, c in enumerate(order):
        cols = pl.ds(pl.multiple_of((me ^ c) * chunk, 128), chunk)
        weights.append(pltpu.make_async_copy(wi_hbm.at[:, cols], wi.at[:, cols], weight_sem.at[2 * k]))
        weights.append(pltpu.make_async_copy(wo_hbm.at[cols, :], wo.at[cols, :], weight_sem.at[2 * k + 1]))
    for copy in loads + weights[:2]:
        copy.start()
    stores = [
        pltpu.make_async_copy(here, out, store_sem.at[i])
        for i, (here, out) in enumerate(
            (
                (left_here.at[0], left_out), (left_here.at[1], left_send), (active_here, active_out),
                (first_here, first_out), (layer_here, layer_out), (grad_one_here, grad_one_out),
                (near_here, near_out), (sums_here, sums_out),
            )
        )
    ]
    row = lambda r: vec[r : r + 1, :]
    attn_bias, attn_gain, attn_shift, outer_bias, ffn_gain, ffn_shift = (row(r) for r in range(6))
    sums_here[...] = jnp.zeros_like(sums_here)
    attended = attn_bias + x[...].astype(F32)
    for copy in loads:
        copy.wait()
    for copy in weights[2:4]:
        copy.start()
    for j in range(4):
        attended += dot(parts[j], wa[me ^ j])
    for j in range(4):
        left_here[j & 1, 2 + (j >> 1)] = parts[j].astype(F32).T.astype(LOW)
    normal_one, scale_one = normalise(attended)
    hidden = normal_one * attn_gain + attn_shift
    hidden_low = hidden.astype(LOW)
    flipped[...] = hidden.T
    for j in range(4):
        start = pl.multiple_of((me ^ j) * hw, 64)
        left_here[j & 1, j >> 1] = flipped[pl.ds(start, hw), :].astype(LOW)
    stores[0].start()
    stores[1].start()
    pre_two = hidden + outer_bias
    for k, c in enumerate(order):
        cols = pl.ds(pl.multiple_of((me ^ c) * chunk, 128), chunk)
        for copy in weights[2 * k + 4 : 2 * k + 6]:
            copy.start()
        weights[2 * k].wait()
        u = dot(hidden_low, wi[:, cols]) + ib[:, cols]
        below = 0.5 * (1.0 + lax.erf(u * (0.5**0.5)))
        density = jnp.exp(-0.5 * u * u) * 0.3989422804014327
        active = (u * below).astype(LOW)
        slope[c] = below + u * density
        here = first_here if c & 1 else active_here
        here[:, (c >> 1) * chunk : ((c >> 1) + 1) * chunk] = active
        weights[2 * k + 1].wait()
        pre_two += dot(active, wo[cols, :])
    stores[2].start()
    normal_two, scale_two = normalise(pre_two)
    layer_here[...] = (normal_two * ffn_gain + ffn_shift).astype(LOW)
    stores[4].start()
    dy = cot[...].astype(F32)
    sums_here[4:5, :] = jnp.sum(dy * normal_two, 0, keepdims=True)
    sums_here[5:6, :] = jnp.sum(dy, 0, keepdims=True)
    grad_two = normalise_back(dy * ffn_gain, normal_two, scale_two)
    grad_outer = grad_two.astype(LOW)
    first_here[:, 2 * chunk :] = grad_outer
    stores[3].start()
    sums_here[3:4, :] = jnp.sum(grad_outer.astype(F32), 0, keepdims=True)
    grad_hidden = grad_two
    moved = []
    for c in range(5):
        some = pl.ds(c * chunk, chunk)
        moved.append(pltpu.make_async_copy(second_here.at[:, some], second_out.at[:, some], inner_sem.at[c]))
    for c in range(4):
        cols = slice(c * chunk, (c + 1) * chunk)
        grad_inner = (dot_nt(grad_outer, wo[cols, :]) * slope[me ^ c]).astype(LOW)
        second_here[:, cols] = grad_inner
        moved[c].start()
        column = jnp.sum(grad_inner.astype(F32), 0, keepdims=True)
        for i in range(4):
            sums_here[6 + i : 7 + i, c * hw : (c + 1) * hw] = column[:, i * hw : (i + 1) * hw]
        grad_hidden += dot_nt(grad_inner, wi[:, cols])
    sums_here[1:2, :] = jnp.sum(grad_hidden * normal_one, 0, keepdims=True)
    sums_here[2:3, :] = jnp.sum(grad_hidden, 0, keepdims=True)
    grad_one = normalise_back(grad_hidden * attn_gain, normal_one, scale_one)
    grad_one_here[...] = grad_one
    stores[5].start()
    grad_attn = grad_one.astype(LOW)
    second_here[:, 4 * chunk :] = grad_attn
    moved[4].start()
    for j in range(2):
        near_here[j] = dot_nt(grad_attn, wa[me ^ j]).astype(LOW)
    stores[6].start()
    sums_here[0:1, :] = jnp.sum(grad_attn.astype(F32), 0, keepdims=True)
    stores[7].start()
    for j in range(2):
        across_out[j] = dot_nt(grad_attn, wa[me ^ (j + 2)]).astype(LOW)
    for copy in moved + stores:
        copy.wait()


def rows_pass(where, x, context, cot, wa, vec, ib, wi, wo):
    rows, width = x.shape
    ff = ib.shape[1]
    hw = wa.shape[1]
    kinds = [
        ((rows, width), LOW), ((rows, width), F32), ((rows, 2 * width), LOW), ((rows, 3 * width), LOW),
        ((rows, ff + width), LOW), ((4, hw, rows), LOW), ((4, hw, rows), LOW), ((2, rows, hw), LOW), ((16, width), F32),
    ]
    here = kinds[:5] + [((2, 4, hw, rows), LOW)] + kinds[7:]
    return pl.pallas_call(
        rows_kernel,
        in_specs=[SMEM, vmem()] + [HBM] * 3 + [vmem()] * 5 + [HBM, HBM],
        out_specs=[HBM] * 9 + [vmem()],
        out_shape=[pltpu.HBM(*kind) for kind in kinds] + [jax.ShapeDtypeStruct((2, rows, hw), LOW)],
        scratch_shapes=[
            pltpu.VMEM(wi.shape, LOW),
            pltpu.VMEM(wo.shape, LOW),
            pltpu.VMEM((4, rows, width), F32),
            pltpu.VMEM((4, rows, hw), LOW),
        ]
        + [pltpu.VMEM(*kind) for kind in here]
        + [pltpu.VMEM((width, rows), F32)]
        + [pltpu.SemaphoreType.DMA((n,)) for n in (4, 8, 8, 5)],
        compiler_params=pltpu.CompilerParams(vmem_limit_bytes=36 * MIB),
        cost_estimate=cost(11),
        name="rows_pass",
    )(where, x, *map(far, context[:3]), context[3], cot, wa, vec, ib, far(wi), far(wo))


def outer_grad_kernel(place, active, active_got, grad, grad_got, send_out, keep_out, token):
    half = PIECES // 2
    n = grad.shape[1] // PIECES
    right = jnp.concatenate([grad[...], grad_got[...]], 0)
    product = dot_tn(jnp.concatenate([active[...], active_got[...]], 0), right)

    def store(low_out, high_out):
        for e in range(PIECES):
            out = high_out if e >= half else low_out
            out[0, e % half] = product[e * n : (e + 1) * n].astype(LOW)

    high = (place[0] & half) > 0
    pl.when(high)(lambda: store(send_out, keep_out))
    pl.when(jnp.logical_not(high))(lambda: store(keep_out, send_out))


def outer_grad(place, active, first, first_got):
    rows, width = first.shape
    width //= 3
    block = (1, PIECES // 2, width // PIECES, width)
    side = vmem((rows, width), lambda y: (0, y))
    last = vmem((rows, width), lambda y: (0, 2))
    return pl.pallas_call(
        outer_grad_kernel,
        grid=(2,),
        in_specs=[SMEM, side, side, last, last],
        out_specs=[vmem(block, lambda y: (y, 0, 0, 0))] * 2 + [HBM],
        out_shape=[jax.ShapeDtypeStruct((2,) + block[1:], LOW)] * 2 + [TOKEN],
        compiler_params=pltpu.CompilerParams(vmem_limit_bytes=16 * MIB),
        cost_estimate=cost(30),
        name="outer_grad",
    )(place, far(active), first_got, far(first), first_got)


SPLIT = 128
ORDERS = {
    "a": ([1, "y", 2], 4, [2, 1]),
    "b": (["y", 2, 1], 4, [2, 1]),
    "c": ([2, 1, "y"], 4, [1, 2]),
    "d": ([1, 4], 2, [1, 4]),
}
SEQUENCE = "abcdbacbdacbdedbcadca"


def inner_grad_kernel(bit_b, bit_c, mine_hbm, second_hbm, mine_got, second_got, *refs):
    outs, (mine, second, left, rest, *heres, load_sem, store_sem) = refs[-13:-9], refs[-8:]
    hw, rows = mine.shape[1:]
    width = 4 * hw
    half = PIECES // 2
    n = hw // PIECES
    cols = width // 2
    loads = [pltpu.make_async_copy(mine_hbm, mine, load_sem.at[5])]
    for c in (4, 0, 1, 2, 3):
        some = pl.ds(c * width, width)
        loads.append(pltpu.make_async_copy(second_hbm.at[:, some], second.at[:, some], load_sem.at[c]))
    for copy in loads:
        copy.start()
    for copy in loads[:2]:
        copy.wait()
    grads = jnp.concatenate([second[:, 4 * width :], second_got[:, 4 * width :]], 0)
    for y in range(2):
        left[y * hw : (y + 1) * hw, :rows] = mine[y]
        left[y * hw : (y + 1) * hw, rows:] = mine_got[y]
        rest[y] = dot(jnp.concatenate([mine[2 + y], mine_got[2 + y]], 1), grads)
    waits = []

    def send(part, piece, y, at, keep):
        here = heres[part]
        out = outs[2 * part + 1] if keep else outs[2 * part]
        spot = (part * PIECES + piece) * 2 + y
        copy = pltpu.make_async_copy(here.at[y, piece], out.at[at[0], at[1]], store_sem.at[spot])
        copy.start()
        return copy

    for c in range(4):
        loads[2 + c].wait()
        here = slice(c * width, (c + 1) * width)
        product = dot(left[...], jnp.concatenate([second[:, here], second_got[:, here]], 0))
        for k in range(2):
            piece = 2 * c + k
            for y in range(2):
                some = product[y * hw : (y + 1) * hw, k * cols : (k + 1) * cols]
                heres[0][y, piece] = some[:SPLIT].astype(LOW)
                more = rest[y, piece * n : (piece + 1) * n, :]
                more = jnp.concatenate([some[SPLIT:], more[:, :cols], more[:, cols:]], 0)
                heres[1][y, piece] = more.astype(LOW)
        for part, (which, bit) in enumerate((("b", bit_b), ("c", bit_c))):
            both = [(2 * c + k, y) for k in range(2) for y in range(2)]
            if ORDERS[which][0][0] == "y":
                for piece, y in both:
                    waits.append(send(part, piece, y, (0, piece), y == 0))
            else:
                kept = (bit[0] & half) == (c >> 1) * half
                for here, keep in ((kept, True), (jnp.logical_not(kept), False)):

                    @pl.when(here)
                    def _(part=part, both=both, keep=keep):
                        for piece, y in both:
                            send(part, piece, y, (y, piece % half), keep)

                for piece, y in both:
                    spot = (part * PIECES + piece) * 2 + y
                    out = outs[2 * part].at[y, piece % half]
                    waits.append(pltpu.make_async_copy(heres[part].at[y, piece], out, store_sem.at[spot]))
    for copy in waits:
        copy.wait()


def inner_grad(places, mine, mine_got, second, second_got, after):
    hw = mine.shape[1]
    width = 4 * hw
    half = PIECES // 2
    counts = [(1, PIECES) if ORDERS[which][0][0] == "y" else (2, half) for which in "bc"]
    talls = [SPLIT, hw - SPLIT + 2 * hw // PIECES]
    shapes = [count + (tall, width // 2) for count, tall in zip(counts, talls)]
    return pl.pallas_call(
        inner_grad_kernel,
        in_specs=[SMEM, SMEM, HBM, HBM, vmem(), vmem()] + [HBM] * len(after),
        out_specs=[HBM] * 5,
        out_shape=[pltpu.HBM(shape, LOW) for shape in shapes for _ in range(2)] + [TOKEN],
        scratch_shapes=[
            pltpu.VMEM(mine.shape, LOW),
            pltpu.VMEM(second.shape, LOW),
            pltpu.VMEM((2 * hw, 2 * mine.shape[2]), LOW),
            pltpu.VMEM((2, hw, width), F32),
        ]
        + [pltpu.VMEM((2, PIECES, tall, width // 2), LOW) for tall in talls]
        + [pltpu.SemaphoreType.DMA((6,)), pltpu.SemaphoreType.DMA((4 * PIECES,))],
        compiler_params=pltpu.CompilerParams(vmem_limit_bytes=20 * MIB),
        cost_estimate=cost(4),
        name="inner_grad",
    )(*places, far(mine), far(second), mine_got, second_got, *map(far, after))


ANYWHERE = pl.BlockSpec(memory_space=pl.ANY)


def sum_kernel(spec, place, *refs):
    leads, count, flip, inputs, splits = spec
    ins = refs[: len(inputs)]
    outs = refs[-1 - splits : -1]
    first = (place[0] // count) * count
    if flip:
        first = first ^ count
    for y, lead in enumerate(leads):
        for r in range(count):
            total = None
            for ref in ins:
                pieces = ref.shape[1]
                base = first & (pieces - 1) if count < pieces else 0
                term = ref[lead if ref.shape[0] > 1 else 0, base + r].astype(F32)
                total = term if total is None else total + term
            if splits == 1:
                outs[0][y, r] = total.astype(LOW)
            else:
                n = total.shape[0] // splits
                for j in range(splits):
                    outs[j][r] = total[j * n : (j + 1) * n].astype(LOW)


def sum_pieces(place, inputs, leads, count, flip, after=(), splits=1, name="sum_pieces"):
    tall, wide = inputs[0].shape[2:]
    spec = (tuple(leads), count, flip, tuple(range(len(inputs))), splits)
    if splits == 1:
        out_shape = [jax.ShapeDtypeStruct((len(leads), count, tall, wide), LOW)]
    else:
        out_shape = [jax.ShapeDtypeStruct((count, tall // splits, wide), LOW)] * splits
    return pl.pallas_call(
        lambda *refs: sum_kernel(spec, *refs),
        in_specs=[SMEM] + [vmem()] * len(inputs) + [HBM] * len(after),
        out_specs=[vmem()] * splits + [HBM],
        out_shape=out_shape + [TOKEN],
        compiler_params=pltpu.CompilerParams(vmem_limit_bytes=4 * MIB),
        cost_estimate=cost(STEP),
        name=name,
    )(place, *inputs, *map(far, after))


def outer_place_kernel(spots, place, own, got, out, here, sem):
    n = own.shape[1]
    copies = []
    for i, spot in enumerate(spots):
        here[i] = (own[i] if i < 4 else got[i - 4]).astype(F32)
        rows = pl.ds(pl.multiple_of((place[0] ^ spot) * n, 8), n)
        copies.append(pltpu.make_async_copy(here.at[i], out.at[rows], sem.at[i]))
        copies[i].start()
    for copy in copies:
        copy.wait()


def outer_place(spots, place, own, got):
    n, width = own.shape[1:]
    return pl.pallas_call(
        lambda *refs: outer_place_kernel(spots, *refs),
        in_specs=[SMEM, vmem(), vmem()],
        out_specs=HBM,
        out_shape=pltpu.HBM((PIECES * n, width), F32),
        scratch_shapes=[pltpu.VMEM((PIECES, n, width), F32), pltpu.SemaphoreType.DMA((PIECES,))],
        compiler_params=pltpu.CompilerParams(vmem_limit_bytes=6 * MIB),
        cost_estimate=cost(2),
        name="outer_place",
    )(place, own, got)


def inner_place_kernel(spots_one, spots_two, one, two, own, got, own_two, got_two, *refs):
    inner, attn = refs[-2:]
    hw, cols = inner.shape[0], own.shape[2]
    n = attn.shape[0] // PIECES
    for i in range(PIECES):
        piece = (own[i] if i < 4 else got[i - 4]).astype(F32)
        here = one[0] ^ spots_one[i]
        inner[:SPLIT, pl.ds(pl.multiple_of(here * cols, 128), cols)] = piece
        piece = (own_two[i] if i < 4 else got_two[i - 4]).astype(F32)
        here = two[0] ^ spots_two[i]
        some = hw - SPLIT
        inner[SPLIT:, pl.ds(pl.multiple_of(here * cols, 128), cols)] = piece[:some]
        more = jnp.concatenate([piece[some : some + n], piece[some + n :]], 1)
        attn[pl.ds(pl.multiple_of(here * n, 8), n), :] = more


def inner_place(spots_one, spots_two, one, two, parts_one, parts_two, hw, after=()):
    cols = parts_one[0].shape[2]
    n = hw // PIECES
    return pl.pallas_call(
        lambda *refs: inner_place_kernel(spots_one, spots_two, *refs),
        in_specs=[SMEM, SMEM] + [vmem()] * 4 + [HBM] * len(after),
        out_specs=[vmem(), vmem()],
        out_shape=[
            jax.ShapeDtypeStruct((hw, PIECES * cols), F32),
            jax.ShapeDtypeStruct((PIECES * n, 2 * cols), F32),
        ],
        compiler_params=pltpu.CompilerParams(vmem_limit_bytes=4 * MIB),
        cost_estimate=cost(2),
        name="inner_place",
    )(one, two, *parts_one, *parts_two, *map(far, after))


def project_place_kernel(spots, place, own, got, out, vectors, here, tall, sem):
    n = own.shape[1] // 4
    hw = out.shape[1] // 12
    wide = 3 * hw
    copies = []
    for i, spot in enumerate(spots):
        ref, k = (own, i) if i < 4 else (got, i - 4)
        rows = pl.ds(pl.multiple_of((place[0] ^ spot) * n, 8), n)
        total = None
        for owner in range(4):
            start = pl.multiple_of((owner ^ place[1]) * n, 8)
            block = ref[k, pl.ds(start, n), :].astype(F32)
            for t in range(3):
                at = t * 4 * hw + owner * hw
                here[i, :, at : at + hw] = block[:, t * hw : (t + 1) * hw]
            extra = block[:, wide:]
            total = extra if total is None else total + extra
        copies.append(pltpu.make_async_copy(here.at[i], out.at[rows], sem.at[i]))
        copies[i].start()
        tall[rows, : total.shape[1]] = total
    vectors[...] = tall[...].T[: vectors.shape[0]]
    for copy in copies:
        copy.wait()


def project_place(spots, place, own, got, hw):
    _, tall, wide = own.shape
    n = tall // 4
    return pl.pallas_call(
        lambda *refs: project_place_kernel(spots, *refs),
        in_specs=[SMEM, vmem(), vmem()],
        out_specs=[HBM, vmem()],
        out_shape=[pltpu.HBM((PIECES * n, 12 * hw), F32), jax.ShapeDtypeStruct((16, PIECES * n), F32)],
        scratch_shapes=[
            pltpu.VMEM((PIECES, n, 12 * hw), F32),
            pltpu.VMEM((PIECES * n, 128), F32),
            pltpu.SemaphoreType.DMA((PIECES,)),
        ],
        compiler_params=pltpu.CompilerParams(vmem_limit_bytes=6 * MIB),
        cost_estimate=cost(2),
        name="project_place",
    )(place, own, got)


def join_kernel(*refs):
    out, token, sem = refs[-3:]
    own, got = refs[:2]
    n = own.shape[0]
    copies = [pltpu.make_async_copy(f, out.at[pl.ds(i * n, n)], sem.at[i]) for i, f in enumerate((own, got))]
    for copy in copies:
        copy.start()
    for copy in copies:
        copy.wait()


def join(own, got, after):
    shape = (2 * own.shape[0],) + own.shape[1:]
    return pl.pallas_call(
        join_kernel,
        in_specs=[ANYWHERE] * 2 + [HBM] * len(after),
        out_specs=[ANYWHERE, HBM],
        out_shape=[jax.ShapeDtypeStruct(shape, own.dtype), TOKEN],
        scratch_shapes=[pltpu.SemaphoreType.DMA((2,))],
        compiler_params=pltpu.CompilerParams(vmem_limit_bytes=2 * MIB),
        cost_estimate=cost(JOIN),
        name="join",
    )(own, got, *map(far, after))


def pass_on_kernel(source, *refs):
    out, sem = refs[-2:]
    copy = pltpu.make_async_copy(source, out, sem.at[0])
    copy.start()
    copy.wait()


def pass_on(source, after):
    return pl.pallas_call(
        pass_on_kernel,
        in_specs=[vmem()] + [HBM] * len(after),
        out_specs=vmem(),
        out_shape=jax.ShapeDtypeStruct(source.shape, source.dtype),
        scratch_shapes=[pltpu.SemaphoreType.DMA((1,))],
        compiler_params=pltpu.CompilerParams(vmem_limit_bytes=2 * MIB),
        cost_estimate=cost(0.5),
        name="pass_on",
    )(source, *map(far, after))


def pair_kernel(near, far, *refs):
    out, token, sem = refs[-3:]
    copies = [pltpu.make_async_copy(f.at[1], out.at[i], sem.at[i]) for i, f in enumerate((near, far))]
    for copy in copies:
        copy.start()
    for copy in copies:
        copy.wait()


def pair(near, far_got, after):
    return pl.pallas_call(
        pair_kernel,
        in_specs=[ANYWHERE] * 2 + [HBM] * len(after),
        out_specs=[ANYWHERE, HBM],
        out_shape=[jax.ShapeDtypeStruct(near.shape, near.dtype), TOKEN],
        scratch_shapes=[pltpu.SemaphoreType.DMA((2,))],
        compiler_params=pltpu.CompilerParams(vmem_limit_bytes=2 * MIB),
        cost_estimate=cost(0.5),
        name="pair",
    )(near, far_got, *map(far, after))


def swap(field, axis, bit):
    count = lax.axis_size(axis)
    return lax.ppermute(field, axis, [(i, i ^ bit) for i in range(count)])


def add(left, right):
    return (left.astype(F32) + right.astype(F32)).astype(LOW)


class Reduction:
    def __init__(self, order, last, back, lane, me, rest):
        self.order = list(order)
        self.last = last
        self.back = list(back)
        self.rest = rest
        bits = [o for o in order if o != "y"]
        weight = {bit: PIECES >> (k + 1) for k, bit in enumerate(bits)}
        spot = sum(jnp.where(lane & bit, w, 0) for bit, w in weight.items())
        weight[last] = 0
        self.spots = [
            i % 2 + sum(weight[bit] for t, bit in enumerate(back) if i >> (t + 1) & 1) for i in range(PIECES)
        ]
        self.own = None
        self.place = jnp.stack([spot.astype(jnp.int32), me.astype(jnp.int32)])

    def begin(self, keep, send):
        axis = self.order.pop(0)
        got = swap(send, "seq", 2) if axis == "y" else swap(send, "dp", axis)
        self.arrays = [keep, got]
        self.left = keep.shape[1]
        self.folded = keep.shape[0] == 1

    def step(self, after=(), splits=1, name="sum"):
        if not self.order and self.last is None:
            return sum_pieces(self.place, self.arrays, [0], self.left, False, after, splits, name)
        leads = [0] if self.folded else [0, 1]
        if not self.order:
            sent, token = sum_pieces(self.place, self.arrays, [0], self.left, False, after, name=name)
            self.arrays = [sent, swap(sent, "dp", self.last)]
            self.last = None
            return token
        axis = self.order.pop(0)
        if axis == "y":
            sent, token = sum_pieces(self.place, self.arrays, [1], self.left, False, after, name=name)
            self.folded = True
            got = swap(sent, "seq", 2)
        else:
            self.left //= 2
            sent, token = sum_pieces(self.place, self.arrays, leads, self.left, True, after, name=name)
            got = swap(sent, "dp", axis)
        self.arrays = self.arrays + [got]
        return token

    def start(self, piece):
        for bit in self.rest:
            piece = add(piece, swap(piece, "dp", bit))
        self.own = piece
        self.got = swap(piece, "dp", self.back[0])
        self.done = 1

    def grow(self, after):
        self.own, token = join(self.own, self.got, after)
        self.got = swap(self.own, "dp", self.back[self.done])
        self.done += 1
        return token


def local(
    tokens, lengths, query_key_value, query_bias, value_bias, attn_weight, attn_bias, attn_gain,
    attn_shift, inner_weight, inner_bias, outer_weight, outer_bias, ffn_gain, ffn_shift, cotangent,
):
    groups = lax.axis_size("seq")
    lanes = lax.axis_size("dp")
    me = lax.axis_index("seq")
    lane = lax.axis_index("dp")
    passages, quarter, width = tokens.shape
    hw = H // groups * HD
    rows = passages * quarter
    ff = inner_bias.shape[0]
    rest = [1 << i for i in range(3, lanes.bit_length() - 1)]
    where = me.astype(jnp.int32).reshape(1)

    across = swap(tokens, "seq", 2)
    beside = swap(tokens, "seq", 1)
    biases = (query_bias.reshape(1, width), value_bias.reshape(1, width))
    w, bias, token = choose_heads(where, query_key_value, *biases)
    across = pass_on(across, [token])
    corner = swap(across, "seq", 1)
    shards = (tokens, beside, across, corner)
    vec = jnp.stack([attn_bias, attn_gain, attn_shift, outer_bias, ffn_gain, ffn_shift, ffn_shift, ffn_shift])
    vec = vec.astype(F32)
    ib = inner_bias.astype(F32).reshape(1, ff)

    qkv, chance, own, x_all, *context_h = attend(where, lengths, shards, w, bias)
    context = [own] + [swap(part, "seq", j) for j, part in zip((1, 2, 3), context_h)]
    context = [part.reshape(rows, hw) for part in context]

    wa = attn_weight.reshape(groups, hw, width)
    layer_out, grad_one, active, first, second, mine, mine_send, near, vectors, across_heads = rows_pass(
        where, tokens.reshape(rows, width), context, cotangent.reshape(rows, width), wa, vec, ib, inner_weight,
        outer_weight,
    )
    first_got = swap(first, "seq", 1)
    second_got = swap(second, "seq", 1)
    mine_got = swap(mine_send, "seq", 1)
    a, b, c, d = (Reduction(*ORDERS[which], lane, me, rest) for which in "abcd")
    far_got = swap(across_heads, "seq", 2)
    outer_send, outer_keep, token = outer_grad(a.place, active, first, first_got)
    near_send, paired = pair(near, far_got, [token])
    near_got = swap(near_send, "seq", 1)
    a.begin(outer_keep, outer_send)
    first_send, first_keep, second_send, second_keep, token = inner_grad(
        [b.place, c.place], mine, mine_got, second, second_got, [paired]
    )
    b.begin(first_keep, first_send)
    c.begin(second_keep, second_send)
    grads_h = [f.reshape(2, passages, quarter, hw) for f in (near, near_got, far_got)]
    back_keep, back_send, project_send, project_keep, token = attend_back(
        d.place, x_all, w, qkv, chance, grads_h, vectors, [token]
    )
    d.begin(project_keep, project_send)
    back_got = swap(back_send, "seq", 1)

    def begin_back(after):
        total, token = sum_pieces(
            d.place,
            [f.reshape(2, 1, rows, width) for f in (back_keep, back_got)],
            [1], 1, False, after, name="back_y",
        )
        return swap(total, "seq", 2), token

    if "e" not in SEQUENCE:
        back_over, _ = begin_back([])
    parts = None
    for letter in SEQUENCE:
        if letter == "e":
            back_over, token = begin_back([token])
            continue
        chunk = {"a": a, "b": b, "c": c, "d": d}[letter]
        if chunk.order or chunk.last is not None:
            token = chunk.step([token], name="sum_" + letter)
        elif chunk.own is not None:
            token = chunk.grow([token])
        elif chunk is d and parts is None:
            *parts, token = d.step([token], splits=4, name="total_d")
            parts = [parts[0]] + [swap(parts[j], "seq", j) for j in (1, 2, 3)]
        elif chunk is d:
            d.start(jnp.concatenate(parts, 1))
        else:
            total, token = chunk.step([token], name="total_" + letter)
            chunk.start(total[0])
    grad_query_key_value, summed = project_place(d.spots, d.place, d.own, d.got, hw)
    grad_outer_weight = outer_place(a.spots, a.place, a.own, a.got)
    grad_inner_weight, grad_attn_weight = inner_place(
        b.spots, c.spots, b.place, c.place, (b.own, b.got), (c.own, c.got), hw
    )
    input_grad = (
        grad_one + back_keep[0].reshape(rows, width).astype(F32)
        + back_got[0].reshape(rows, width).astype(F32)
        + back_over[0, 0].astype(F32)
    ).astype(LOW)
    return (
        layer_out.reshape(passages, quarter, width),
        input_grad.reshape(passages, quarter, width),
        grad_query_key_value,
        summed[10],
        summed[11],
        grad_attn_weight,
        summed[0],
        summed[1],
        summed[2],
        grad_inner_weight,
        summed[6:10].reshape(-1),
        grad_outer_weight,
        summed[3],
        summed[4],
        summed[5],
    )


def solution(mesh):
    rows = P("dp", "seq", None)
    return jax.shard_map(
        local,
        mesh=mesh,
        in_specs=(rows, P("dp")) + (P(),) * 13 + (rows,),
        out_specs=(
            rows,
            rows,
            P("seq", None),
            P("seq"),
            P("seq"),
            P("seq", None),
            P("seq"),
            P("seq"),
            P("seq"),
            P("seq", None),
            P("seq"),
            P("seq", None),
            P("seq"),
            P("seq"),
            P("seq"),
        ),
        check_vma=False,
    )
```
